128 devices in a mesh: dp: 16 (over z, y), expert: 8 (over x, core).
Axes of the slice: x: 4, y: 4, z: 4, core: 2. Of those that a mesh axis runs over, the one named last changes fastest.
Arguments:
- tokens: bfloat16 [16384, 1536], P(('dp', 'expert')), may hold values from -6 to 6
- segments: int32 [16384], P(('dp', 'expert')), may hold values from 0 to 2, as said below
- routes: int32 [16384, 8], P(('dp', 'expert')), may hold values from 0 to 15, all different within a row; in each aligned block of 128 rows (0 to 127, 128 to 255, ...) at most 96 rows name the same one
- gain_attn: bfloat16 [1536], P('dp'), may hold values from 0.099609375 to 1.8984375
- w_query: bfloat16 [1536, 1536], P('dp'), may hold values from -0.625 to 0.625
- w_key: bfloat16 [1536, 512], P('dp'), may hold values from -0.625 to 0.625
- w_value: bfloat16 [1536, 512], P('dp'), may hold values from -0.15625 to 0.15625
- w_out: bfloat16 [1536, 1536], P('dp'), may hold values from -6 to 6
- gain_moe: bfloat16 [1536], P('dp'), may hold values from 0.099609375 to 1.8984375
- w_router: bfloat16 [1536, 16], P('dp'), may hold values from -0.078125 to 0.078125
- expert_gate: bfloat16 [16, 1536, 512], P('expert'), may hold values from -0.15625 to 0.15625
- expert_up: bfloat16 [16, 1536, 512], P('expert'), may hold values from -0.15625 to 0.15625
- expert_down: bfloat16 [16, 512, 1536], P('expert'), may hold values from -6 to 6
- out_grad: bfloat16 [16384, 1536], P(('dp', 'expert')), may hold values from -6 to 6
Outputs:
- output: bfloat16 [16384, 1536], P(('dp', 'expert'))
- grad_tokens: float32 [16384, 1536], P(('dp', 'expert'))
- grad_gain_attn: float32 [1536], P('dp')
- grad_query: float32 [1536, 1536], P('dp')
- grad_key: float32 [1536, 512], P('dp')
- grad_value: float32 [1536, 512], P('dp')
- grad_out: float32 [1536, 1536], P('dp')
- grad_gain_moe: float32 [1536], P('dp')
- grad_router: float32 [1536, 16], P('dp')
- grad_gate: float32 [16, 1536, 512], P('expert')
- grad_up: float32 [16, 1536, 512], P('expert')
- grad_down: float32 [16, 512, 1536], P('expert')
The draws below stay inside these ranges and needn't reach their ends.
Inputs may be any that keep to these rules, and one draw needn't show every extreme that they name: `segments`: within each sequence of 1024 tokens the id starts at 0 and never falls; every id from 0 to 2 occurs in every sequence. `routes`: each row names 8 different experts; among the rows of one device (aligned blocks of 128 rows) no expert is named more than 96 times, and in some block one is named exactly 96 times.
All inputs are finite; a program needn't handle non-finite values.
Results may differ from the reference program's by a relative error of at most 0.025.
Values may be sent and summed in bfloat16 or wider, within the bound.
No kernel may reach another device: no remote copies, remote signals or barrier semaphores. Data moves between devices by JAX's collectives and lax.ppermute only.
A program may use at most 256 MiB of HBM per device.

```python
import math
import jax
import jax.numpy as jnp
import numpy as np
from jax import lax

D = 1536
HEADS = 24
KV_HEADS = 8
HEAD_DIM = 64
FF = 512
TOP = 8
EXPERTS = 16
SEQ = 1024
ROWS = 128
CAP = 96
TOKENS = 16384
N_DP = 16


def draw_segments(key, part):
    key = jax.random.fold_in(key, 11)
    first_key, last_key, kind_key = jax.random.split(key, 3)
    block_count = SEQ // ROWS
    last_block = block_count - 1
    middle = block_count // 2
    before_middle = max(middle - 1, 1)
    kind_shift = jax.random.randint(kind_key, (), 0, 3)
    kinds = (jnp.arange(N_DP, dtype=jnp.int32) + kind_shift) % 3
    split_block = jnp.where(kinds == 0, last_block, jnp.where(kinds == 1, before_middle, middle)).astype(jnp.int32)[:, None]
    first_ends = jax.random.randint(first_key, (N_DP, 1), 1, ROWS)
    last_starts = split_block * ROWS + jax.random.randint(last_key, (N_DP, 1), 1, ROWS)
    places = jnp.arange(SEQ, dtype=jnp.int32)[None, :]
    doc_ids = (places >= first_ends).astype(jnp.int32) + (places >= last_starts).astype(jnp.int32)
    return doc_ids.reshape(TOKENS)


def level_of(rng, dims, shards, low, top_value):
    def one(axis_at, parts):
        steps = jax.random.uniform(jax.random.fold_in(jax.random.fold_in(rng, 6), axis_at), (parts,), jnp.float32, low / len(shards), top_value / len(shards))
        return jnp.repeat(jnp.exp(steps), dims[axis_at] // parts).reshape((-1,) + (1,) * (len(dims) - axis_at - 1))

    factor_of = one(*shards[0])
    for cut in shards[1:]:
        factor_of = factor_of * one(*cut)
    return factor_of


def shared_out(key, own, number, rows, number_of, top, reach, skew):
    order = jax.random.permutation(key, number_of)
    crowded, common = load_shares(number_of, rows * top, reach, skew, True), load_shares(number_of, rows * top, reach, skew, False)
    places = jnp.arange(number_of)

    def named(sizes, rotation):
        used = int((sizes > 0).sum())
        fixed = max(1, used // 4)
        passed = fixed + (places - fixed + rotation * (used - fixed)) % max(1, number_of - fixed)
        return jnp.zeros((number_of,), jnp.int32).at[order[jnp.where(places < fixed, places, passed)]].set(jnp.asarray(sizes, jnp.int32))

    sizes = jnp.where(number % 4 == 0, named(crowded, number // 4), named(common, number - number // 4 - 1))
    mixed = jax.random.permutation(jax.random.fold_in(own, 3), number_of)
    donor, taker = mixed[0:number_of // 2 * 2:2], mixed[1:number_of // 2 * 2:2]
    slack = jnp.minimum(sizes[donor] - 1, reach - sizes[taker]) // 2
    slack = jnp.where((donor == order[0]) | (taker == order[0]) | (sizes[taker] == 0), 0, jnp.maximum(slack, 0))
    passed = jax.random.randint(jax.random.fold_in(own, 4), (number_of // 2,), 0, 1 << 20) % (slack + 1)
    sizes = sizes.at[donor].add(-passed).at[taker].add(passed)
    members = jnp.searchsorted(jnp.cumsum(sizes), jnp.arange(rows * top), side="right").astype(jnp.int32)
    listing = members.reshape(top, rows).T
    listing = listing[jax.random.permutation(jax.random.fold_in(own, 1), rows)]
    rotation = jax.random.randint(jax.random.fold_in(own, 2), (rows, 1), 0, top)
    return jnp.take_along_axis(listing, (jnp.arange(top)[None, :] + rotation) % top, axis=1)


def load_shares(number_of, total, limit, slope, full):
    weights = [(1 << 20) // math.isqrt(rank ** slope) + 1 for rank in range(1, number_of + 1)]
    largest = limit if full else min(limit, max(-(-total // number_of), total * weights[0] // sum(weights)))
    least = 1 if total - largest >= number_of - 1 else 0
    given, surplus = [largest] + [least] * (number_of - 1), total - largest - least * (number_of - 1)
    while surplus > 0:
        movable = [i for i in range(1, number_of) if given[i] < largest] or [i for i in range(1, number_of) if given[i] < limit]
        whole, budget = sum([weights[i] for i in movable]), surplus
        for i in movable:
            more = min(limit - given[i], max(1, budget * weights[i] // whole), surplus)
            given[i] = given[i] + more
            surplus = surplus - more
    return np.array(given)


def centred(rng, dims, width, most, cuts=(), held_as=jnp.bfloat16):
    entries = width * jax.random.normal(rng, dims, jnp.float32)
    if cuts:
        entries = entries * level_of(rng, dims, cuts, -0.22, 0.18)
    return jnp.clip(entries, -most, most).astype(held_as)


def setup_inputs(seed: int = 0) -> dict:
    keys = jax.random.split(jax.random.key(seed), 15)
    tokens = centred(keys[0], (TOKENS, D), 1.0, 6.0, ((0, 128),))
    segments = draw_segments(jax.random.fold_in(keys[14], 71), 0)
    routes_keys = jax.random.split(jax.random.fold_in(keys[2], 1), TOKENS // ROWS)
    routes_turns = jax.random.permutation(jax.random.fold_in(keys[2], 3), TOKENS // ROWS)
    routes = jax.vmap(lambda own, number: shared_out(jax.random.fold_in(keys[2], 2), own, number, ROWS, EXPERTS, TOP, CAP, 1))(routes_keys, routes_turns).reshape((TOKENS, TOP))
    gain_attn = jnp.clip(1.0 + 0.18 * jax.random.normal(keys[3], (D,), jnp.float32), 0.099609375, 1.8984375).astype(jnp.bfloat16)
    w_query = centred(keys[4], (D, HEADS * HEAD_DIM), (D // 16) ** -0.5, 0.625, ((0, 16),))
    w_key = centred(keys[5], (D, KV_HEADS * HEAD_DIM), (D // 16) ** -0.5, 0.625, ((0, 16),))
    w_value = centred(keys[6], (D, KV_HEADS * HEAD_DIM), D ** -0.5, 0.15625, ((0, 16),))
    w_out = centred(keys[7], (HEADS * HEAD_DIM, D), (max(1, D // 1024)) ** -0.5, 6.0, ((0, 16),))
    gain_moe = jnp.clip(1.0 + 0.18 * jax.random.normal(keys[8], (D,), jnp.float32), 0.099609375, 1.8984375).astype(jnp.bfloat16)
    w_router = centred(keys[9], (D, EXPERTS), (4 * D) ** -0.5, 0.078125, ((0, 16),))
    expert_gate = centred(keys[10], (EXPERTS, D, FF), D ** -0.5, 0.15625, ((0, 8),))
    expert_up = centred(keys[11], (EXPERTS, D, FF), D ** -0.5, 0.15625, ((0, 8),))
    expert_down = centred(keys[12], (EXPERTS, FF, D), (max(1, FF // 512)) ** -0.5, 6.0, ((0, 8),))
    out_grad = centred(keys[13], (TOKENS, D), 1.0, 6.0, ((0, 128),))
    return dict(tokens=tokens, segments=segments, routes=routes, gain_attn=gain_attn, w_query=w_query, w_key=w_key, w_value=w_value, w_out=w_out, gain_moe=gain_moe, w_router=w_router, expert_gate=expert_gate, expert_up=expert_up, expert_down=expert_down, out_grad=out_grad)


@jax.custom_vjp
def low(v):
    return lax.optimization_barrier(v.astype(jnp.bfloat16)).astype(jnp.float32)

@jax.custom_vjp
def low_back(v):
    return v

def low_keep(v):
    return (low(v), None)

def low_pass(kept, grad):
    return (grad,)

def back_keep(v):
    return (v, None)

def back_low(kept, grad):
    return (low(grad),)
low.defvjp(low_keep, low_pass)
low_back.defvjp(back_keep, back_low)
eps = 1e-06
residual_scale = 0.22
score_scale = 0.015625
rope_base = 10000.0
doc_slots = 3

def rms_norm(values, gain):
    return values * lax.rsqrt(lax.optimization_barrier(jnp.mean(values * values, axis=-1, keepdims=True)) + eps) * gain

def rotate(values, positions):
    half_dim = values.shape[-1] // 2
    inv_freq = rope_base ** (-jnp.arange(half_dim, dtype=jnp.float32) * 2.0 / values.shape[-1])
    angles = positions.astype(jnp.float32)[:, None] * inv_freq[None, :]
    cosine = jnp.cos(angles)[:, None, :]
    sine_part = jnp.sin(angles)[:, None, :]
    first_half = values[..., :half_dim]
    second_half = values[..., half_dim:]
    return jnp.concatenate([first_half * cosine - second_half * sine_part, second_half * cosine + first_half * sine_part], axis=-1)

def reference(tokens, segments, routes, gain_attn, w_query, w_key, w_value, w_out, gain_moe, w_router, expert_gate, expert_up, expert_down, out_grad):
    highest = lax.Precision.HIGHEST
    per_group = HEADS // KV_HEADS
    seg_seq = segments.reshape(N_DP, SEQ)
    doc_hot = (seg_seq[:, :, None] == jnp.arange(doc_slots, dtype=jnp.int32)[None, None, :]).astype(jnp.int32)
    counts = lax.optimization_barrier(jnp.sum(doc_hot, axis=1))
    starts = jnp.cumsum(counts, axis=1) - counts
    positions = (jnp.arange(SEQ, dtype=jnp.int32)[None, :] - lax.optimization_barrier(jnp.sum(doc_hot * starts[:, None, :], axis=2))).reshape(TOKENS)
    blocks = TOKENS // ROWS
    pair_count = TOKENS * TOP
    flat_routes = routes.reshape(pair_count)
    pair_hot = (flat_routes[:, None] == jnp.arange(EXPERTS, dtype=jnp.int32)[None, :]).astype(jnp.int32)
    block_hot = pair_hot.reshape(blocks, ROWS * TOP, EXPERTS)
    rank_table = (jnp.cumsum(block_hot, axis=1) - block_hot).reshape(pair_count, EXPERTS)
    slot_of = lax.optimization_barrier(jnp.sum(rank_table * pair_hot, axis=1))
    pair_ids = jnp.arange(pair_count, dtype=jnp.int32)
    slot_table = jnp.full((EXPERTS, blocks * CAP), pair_count, jnp.int32)
    slot_table = slot_table.at[flat_routes, pair_ids // (ROWS * TOP) * CAP + slot_of].set(pair_ids)

    def attend(pieces):
        query_rot, key_rot, value_low, seg_one = pieces
        query_four = query_rot.reshape(SEQ, KV_HEADS, per_group, HEAD_DIM)
        raw = low_back(jnp.einsum('qgrd,kgd->grqk', query_four, key_rot, precision=highest))
        places = jnp.arange(SEQ, dtype=jnp.int32)
        allowed = (seg_one[:, None] == seg_one[None, :]) & (places[:, None] >= places[None, :])
        scores = jnp.where(allowed, raw * score_scale, -1e+30)
        maximum = lax.optimization_barrier(jnp.max(scores, axis=-1, keepdims=True))
        exponent = jnp.exp(scores - maximum)
        attn_probs = exponent / lax.optimization_barrier(jnp.sum(exponent, axis=-1, keepdims=True))
        mixed = jnp.einsum('grqk,kgd->qgrd', low(attn_probs), value_low, precision=highest)
        return mixed.reshape(SEQ, HEADS * HEAD_DIM)

    def forward(inputs, gain_one, query_w, key_w, value_w, out_w, gain_two, router_w, gate_w, up_w, down_w):
        normed = low(rms_norm(inputs, gain_one))
        queries = low_back(jnp.dot(normed, query_w, precision=highest))
        key_proj = low_back(jnp.dot(normed, key_w, precision=highest))
        value_proj = low_back(jnp.dot(normed, value_w, precision=highest))
        query_rot = low(rotate(queries.reshape(TOKENS, HEADS, HEAD_DIM), positions))
        key_rot = low(rotate(key_proj.reshape(TOKENS, KV_HEADS, HEAD_DIM), positions))
        value_low = low(value_proj.reshape(TOKENS, KV_HEADS, HEAD_DIM))
        mixed = lax.map(jax.checkpoint(attend), (query_rot.reshape(N_DP, SEQ, HEADS, HEAD_DIM), key_rot.reshape(N_DP, SEQ, KV_HEADS, HEAD_DIM), value_low.reshape(N_DP, SEQ, KV_HEADS, HEAD_DIM), seg_seq))
        mixed = low(low_back(mixed.reshape(TOKENS, HEADS * HEAD_DIM)))
        hidden = inputs + residual_scale * low_back(jnp.dot(mixed, out_w, precision=highest))
        second = low(rms_norm(hidden, gain_two))
        logits = jnp.dot(second, router_w, precision=highest)
        gate_probs = jax.nn.softmax(jnp.take_along_axis(logits, routes, axis=1), axis=1)
        second_pad = jnp.concatenate([second, jnp.zeros((1, D), second.dtype)], axis=0)
        gates_pad = jnp.concatenate([gate_probs.reshape(pair_count), jnp.zeros((1,), gate_probs.dtype)])

        def expert_step(summed, pieces):
            gate_one, up_one, down_one, pair_list = pieces
            token_rows = pair_list // TOP
            expert_in = jnp.take(second_pad, token_rows, axis=0)
            gate_pre = low_back(jnp.dot(expert_in, gate_one, precision=highest))
            up_pre = low_back(jnp.dot(expert_in, up_one, precision=highest))
            hidden_act = low(jax.nn.silu(gate_pre) * up_pre)
            result = low(low_back(jnp.dot(hidden_act, down_one, precision=highest)))
            weight = jnp.take(gates_pad, pair_list)
            return (summed.at[token_rows].add(weight[:, None] * result), None)
        summed, unused = lax.scan(jax.checkpoint(expert_step), jnp.zeros((TOKENS + 1, D), inputs.dtype), (gate_w, up_w, down_w, slot_table))
        return hidden + residual_scale * summed[:TOKENS]
    result, pullback = jax.vjp(forward, tokens.astype(jnp.float32), gain_attn.astype(jnp.float32), w_query.astype(jnp.float32), w_key.astype(jnp.float32), w_value.astype(jnp.float32), w_out.astype(jnp.float32), gain_moe.astype(jnp.float32), w_router.astype(jnp.float32), expert_gate.astype(jnp.float32), expert_up.astype(jnp.float32), expert_down.astype(jnp.float32))
    g_tokens, g_gain_one, g_query, g_key, g_value, g_out, g_gain_two, g_router, g_gate, g_up, g_down = pullback(out_grad.astype(jnp.float32))
    return (result.astype(jnp.bfloat16), g_tokens, g_gain_one, g_query, g_key, g_value, g_out, g_gain_two, g_router, g_gate, g_up, g_down)
```

```python
import jax
import jax.numpy as jnp
from jax import lax
from jax.sharding import Mesh, PartitionSpec as P

HEADS = 24
KV_HEADS = 8
HEAD_DIM = 64
GROUP = HEADS // KV_HEADS
TOP = 8
EXPERTS = 16

eps = 1e-06
residual_scale = 0.22
score_scale = 0.015625
rope_base = 10000.0
doc_slots = 3

bf16 = jnp.bfloat16
f32 = jnp.float32


def shift(value, axis, amount):
    size = lax.axis_size(axis)
    return lax.ppermute(value, axis, [((i + amount) % size, i) for i in range(size)])


def swap(value):
    return lax.ppermute(value, "core", [(0, 1), (1, 0)])


def dot(a, b, dims, out=f32):
    return lax.dot_general(a, b, (dims, ((), ())), preferred_element_type=out)


def turned(stacked, start):
    return lax.dynamic_slice_in_dim(
        jnp.concatenate([stacked, stacked], axis=0), start, stacked.shape[0], axis=0
    )


def gather_expert(block):
    far = [block] + [shift(block, "x", m) for m in (1, 2, 3)]
    mine = jnp.stack(far)
    return jnp.stack([mine, swap(mine)], axis=1)


def scatter_expert(parts):
    near = parts[:, 0].astype(f32) + swap(parts[:, 1]).astype(f32)
    low = near.astype(bf16)
    total = near[0]
    for m in (1, 2, 3):
        total = total + shift(low[m], "x", -m).astype(f32)
    return total


def gather_dp(block):
    row = jnp.stack([block] + [shift(block, "y", m) for m in (1, 2, 3)])
    y, z = lax.axis_index("y"), lax.axis_index("z")
    row = turned(row, (4 - y) % 4)
    whole = jnp.stack([row] + [shift(row, "z", m) for m in (1, 2, 3)])
    whole = turned(whole, (4 - z) % 4)
    return whole.reshape((16,) + block.shape)


def inverse_rms(values):
    return lax.rsqrt(jnp.mean(values * values, axis=-1, keepdims=True) + eps)


def rotate(values, cosine, sine):
    half_dim = values.shape[-1] // 2
    first_half = values[..., :half_dim]
    second_half = values[..., half_dim:]
    return jnp.concatenate(
        [
            first_half * cosine - second_half * sine,
            second_half * cosine + first_half * sine,
        ],
        axis=-1,
    )


def per_device(
    tokens,
    segments,
    routes,
    gain_attn,
    w_query,
    w_key,
    w_value,
    w_out,
    gain_moe,
    w_router,
    expert_gate,
    expert_up,
    expert_down,
    out_grad,
):
    rows, width = tokens.shape
    parts = 8
    seq = rows * parts
    x, core = lax.axis_index("x"), lax.axis_index("core")
    me = x * 2 + core
    q_cols = GROUP * HEAD_DIM

    share = jnp.concatenate(
        [
            lax.dynamic_slice_in_dim(w_query, me * q_cols, q_cols, axis=1),
            lax.dynamic_slice_in_dim(w_key, me * HEAD_DIM, HEAD_DIM, axis=1),
            lax.dynamic_slice_in_dim(w_value, me * HEAD_DIM, HEAD_DIM, axis=1),
            gain_attn[:, None],
            gain_moe[:, None],
            w_router,
            jnp.zeros((gain_attn.shape[0], 46), bf16),
        ],
        axis=1,
    )
    out_w = lax.all_gather(w_out, ("z", "y"), axis=0, tiled=True)
    sent = jnp.concatenate(
        [tokens, jnp.broadcast_to(segments.astype(bf16)[:, None], (rows, 128))], axis=1
    )
    everyone = gather_expert(sent).reshape(seq, width + 128)
    whole = gather_dp(share).reshape(width, 384)
    qkv_w = whole[:, : q_cols + 2 * HEAD_DIM]
    gain_one = whole[:, 320].astype(f32)
    gain_two = whole[:, 321].astype(f32)
    router_w = whole[:, 322:338]

    grad_sent, everyone = lax.optimization_barrier((out_grad, everyone))
    grad_all = gather_expert(grad_sent).reshape(seq, width)

    inputs_all = everyone[:, :width].astype(f32)
    seg_all = everyone[:, width].astype(jnp.int32)
    chips = (x + jnp.arange(4, dtype=jnp.int32)) % 4
    cores = jnp.bitwise_xor(core, jnp.arange(2, dtype=jnp.int32))
    place = (
        (chips[:, None, None] * 2 + cores[None, :, None]) * rows
        + jnp.arange(rows, dtype=jnp.int32)[None, None, :]
    ).reshape(seq)
    first = jnp.sum((seg_all < 1).astype(jnp.int32))
    second_start = jnp.sum((seg_all < 2).astype(jnp.int32))
    positions = place - jnp.where(
        seg_all == 0, 0, jnp.where(seg_all == 1, first, second_start)
    )
    half_dim = HEAD_DIM // 2
    inv_freq = rope_base ** (-jnp.arange(half_dim, dtype=f32) * 2.0 / HEAD_DIM)
    angles = positions.astype(f32)[:, None] * inv_freq[None, :]
    cosine, sine = jnp.cos(angles), jnp.sin(angles)

    scale_all = inverse_rms(inputs_all)
    normed = (inputs_all * scale_all * gain_one[None, :]).astype(bf16)
    qkv = dot(normed, qkv_w, ((1,), (0,)))
    queries = rotate(
        qkv[:, :q_cols].reshape(seq, GROUP, HEAD_DIM), cosine[:, None], sine[:, None]
    ).astype(bf16)
    keys = rotate(qkv[:, q_cols : q_cols + HEAD_DIM], cosine, sine).astype(bf16)
    values = qkv[:, q_cols + HEAD_DIM :].astype(bf16)
    allowed = (seg_all[:, None] == seg_all[None, :]) & (place[:, None] >= place[None, :])
    raw = jnp.einsum("qrd,kd->rqk", queries, keys, preferred_element_type=f32)
    scores = jnp.where(allowed[None], raw * score_scale, -1e30)
    maximum = jnp.max(scores, axis=-1, keepdims=True)
    exponent = jnp.exp(scores - maximum)
    denom = jnp.sum(exponent, axis=-1, keepdims=True)
    log_total = maximum + jnp.log(denom)
    probs = (exponent / denom).astype(bf16)
    mixed_head = jnp.einsum("rqk,kd->qrd", probs, values, preferred_element_type=f32).astype(bf16)

    by_owner = turned(mixed_head.reshape(4, 2, rows, q_cols), (4 - x) % 4)
    by_owner = jnp.where(core == 0, by_owner, by_owner[:, ::-1]).reshape(parts, rows, q_cols)
    mixed = lax.all_to_all(by_owner, ("x", "core"), 0, 0, tiled=True)
    mixed = mixed.transpose(1, 0, 2).reshape(rows, HEADS * HEAD_DIM)

    inputs = tokens.astype(f32)
    hidden = inputs + residual_scale * dot(mixed, out_w, ((1,), (0,)))
    scale_two = inverse_rms(hidden)
    second = (hidden * scale_two * gain_two[None, :]).astype(bf16)
    logits = dot(second, router_w, ((1,), (0,)))
    named = jnp.any(
        routes[:, :, None] == jnp.arange(EXPERTS, dtype=jnp.int32)[None, None, :], axis=1
    )
    gates = jax.nn.softmax(jnp.where(named, logits, -1e30), axis=1)
    gates = jnp.where(named, gates, 0.0)
    gates_high = gates.astype(bf16)
    gates_low = (gates - gates_high.astype(f32)).astype(bf16)
    sent_two = jnp.concatenate(
        [second, gates_high, gates_low, jnp.zeros((rows, 96), bf16)], axis=1
    )
    second_all = gather_expert(sent_two).reshape(seq, width + 128)

    gate_table = second_all[:, width : width + 16].astype(f32) + second_all[
        :, width + 16 : width + 32
    ].astype(f32)
    second_rows = second_all[:, :width]
    mine = (
        jnp.arange(EXPERTS, dtype=jnp.int32)[None, :]
        == 2 * me + jnp.arange(2, dtype=jnp.int32)[:, None]
    ).astype(f32)
    weight = jnp.sum(gate_table[None] * mine[:, None, :], axis=2)
    back = jnp.einsum("td,efd->etf", grad_all, expert_down, preferred_element_type=f32)
    gate_pre = jnp.einsum("td,edf->etf", second_rows, expert_gate, preferred_element_type=f32)
    up_pre = jnp.einsum("td,edf->etf", second_rows, expert_up, preferred_element_type=f32)
    sigmoid_gate = jax.nn.sigmoid(gate_pre)
    silu_gate = gate_pre * sigmoid_gate
    act = silu_gate * up_pre
    weighted = (act * weight[:, :, None]).astype(bf16)
    grad_gates = residual_scale * jnp.sum(act * back, axis=2)
    grad_act = back * (residual_scale * weight)[:, :, None]
    grad_gate_pre = (
        grad_act * up_pre * sigmoid_gate * (1.0 + gate_pre * (1.0 - sigmoid_gate))
    ).astype(bf16)
    grad_up_pre = (grad_act * silu_gate).astype(bf16)
    grad_w_down = residual_scale * jnp.einsum(
        "etf,td->efd", weighted, grad_all, preferred_element_type=f32
    )
    grad_w_gate = jnp.einsum("td,etf->edf", second_rows, grad_gate_pre, preferred_element_type=f32)
    grad_w_up = jnp.einsum("td,etf->edf", second_rows, grad_up_pre, preferred_element_type=f32)
    sums = lax.psum(
        (grad_w_gate.astype(bf16), grad_w_up.astype(bf16), grad_w_down.astype(bf16)), ("z", "y")
    )
    grad_rows = (
        jnp.einsum("etf,edf->td", grad_gate_pre, expert_gate, preferred_element_type=f32)
        + jnp.einsum("etf,edf->td", grad_up_pre, expert_up, preferred_element_type=f32)
    ).astype(bf16)
    routed = jnp.sum(grad_gates[:, :, None] * mine[:, None, :], axis=0)
    routed_high = routed.astype(bf16)
    routed_low = (routed - routed_high.astype(f32)).astype(bf16)
    grad_parts = jnp.concatenate(
        [grad_rows, routed_high, routed_low, jnp.zeros((seq, 96), bf16)], axis=1
    )
    grad_mine = scatter_expert(grad_parts.reshape(4, 2, rows, width + 128))
    combined = jnp.einsum("etf,efd->td", weighted, expert_down, preferred_element_type=f32)
    combined = combined.astype(bf16)
    combined, grad_mine = lax.optimization_barrier((combined, grad_mine))
    output = (
        hidden + residual_scale * scatter_expert(combined.reshape(4, 2, rows, width))
    ).astype(bf16)

    grad_second = grad_mine[:, :width]
    grad_gate_table = (
        grad_mine[:, width : width + 16] + grad_mine[:, width + 16 : width + 32]
    )
    grad_logits = gates * (
        grad_gate_table - jnp.sum(gates * grad_gate_table, axis=1, keepdims=True)
    )
    grad_logits_low = grad_logits.astype(bf16)
    grad_router = dot(second, grad_logits_low, ((0,), (0,)))
    grad_second = grad_second + dot(grad_logits_low, router_w, ((1,), (1,)))
    scaled_two = grad_second * gain_two[None, :]
    grad_gain_two = jnp.sum(grad_second * hidden * scale_two, axis=0)
    grad_final = out_grad.astype(f32)
    grad_hidden = (
        grad_final
        + scale_two * scaled_two
        - hidden * scale_two**3 * jnp.mean(hidden * scaled_two, axis=-1, keepdims=True)
    )
    grad_branch = (residual_scale * grad_hidden).astype(bf16)
    grad_mixed = dot(grad_branch, out_w, ((1,), (1,))).astype(bf16)

    def to_heads(value):
        blocks = value.reshape(rows, parts, q_cols).transpose(1, 0, 2)
        return lax.all_to_all(blocks, ("x", "core"), 0, 0, tiled=True)

    def from_here(blocks):
        blocks = turned(blocks.reshape(4, 2, rows, q_cols), x)
        return jnp.where(core == 0, blocks, blocks[:, ::-1]).reshape(seq, q_cols)

    grad_four = from_here(to_heads(grad_mixed)).reshape(seq, GROUP, HEAD_DIM)

    again = jnp.exp(scores - log_total)
    grad_probs = jnp.einsum("qrd,kd->rqk", grad_four, values, preferred_element_type=f32)
    delta = jnp.sum(again * grad_probs, axis=-1, keepdims=True)
    grad_raw = (again * (grad_probs - delta) * score_scale).astype(bf16)
    grad_q = jnp.einsum("rqk,kd->qrd", grad_raw, keys, preferred_element_type=f32)
    grad_k = jnp.einsum("rqk,qrd->kd", grad_raw, queries, preferred_element_type=f32)
    grad_v = jnp.einsum("rqk,qrd->kd", again.astype(bf16), grad_four, preferred_element_type=f32)
    grad_qkv = jnp.concatenate(
        [
            rotate(grad_q, cosine[:, None], -sine[:, None]).astype(bf16).reshape(seq, q_cols),
            rotate(grad_k, cosine, -sine).astype(bf16),
            grad_v.astype(bf16),
        ],
        axis=1,
    )
    grad_normed = dot(grad_qkv, qkv_w, ((1,), (1,)))
    grad_gain_one = jnp.sum(grad_normed * inputs_all * scale_all, axis=0)
    grad_w_qkv = dot(normed, grad_qkv, ((0,), (0,)))
    normed_mine = scatter_expert(grad_normed.astype(bf16).reshape(4, 2, rows, width))
    scale_one = inverse_rms(inputs)
    scaled_one = normed_mine * gain_one[None, :]
    grad_inputs = (
        grad_hidden
        + scale_one * scaled_one
        - inputs * scale_one**3 * jnp.mean(inputs * scaled_one, axis=-1, keepdims=True)
    )

    mixed_sent, second_all = lax.optimization_barrier((mixed, second_all))
    mixed_all = lax.all_gather(mixed_sent, ("x", "core"), axis=0, tiled=True)
    branch_cols = to_heads(grad_branch).reshape(seq, q_cols)
    grad_w_out = dot(mixed_all, branch_cols, ((0,), (0,)))

    table = jnp.concatenate(
        [
            grad_w_qkv.astype(bf16),
            grad_w_out.astype(bf16),
            grad_gain_one.astype(bf16)[:, None],
            grad_gain_two.astype(bf16)[:, None],
            grad_router.astype(bf16),
            jnp.zeros((width, 110), bf16),
        ],
        axis=1,
    ).reshape(16, width // 16, 640)
    pieces = lax.all_to_all(table, ("z", "y"), 0, 0, tiled=True)
    summed = jnp.sum(pieces.astype(f32), axis=0).astype(bf16)
    lines = gather_expert(summed)
    lines = turned(lines, (4 - x) % 4)
    lines = jnp.where(core == 0, lines, lines[:, ::-1]).reshape(parts, width // 16, 640)
    lines = lines.astype(f32)
    side = lambda a, b: lines[:, :, a:b].transpose(1, 0, 2).reshape(width // 16, parts * (b - a))
    rest = jnp.sum(lines[:, :, 512:530], axis=0)
    return (
        output,
        grad_inputs,
        rest[:, 0],
        side(0, 192),
        side(192, 256),
        side(256, 320),
        side(320, 512),
        rest[:, 1],
        rest[:, 2:18],
        sums[0].astype(f32),
        sums[1].astype(f32),
        sums[2].astype(f32),
    )


def solution(mesh):
    fine = Mesh(mesh.devices.reshape(4, 4, 4, 2), ("z", "y", "x", "core"))
    dp, expert, both = ("z", "y"), ("x", "core"), ("z", "y", "x", "core")
    return jax.shard_map(
        per_device,
        mesh=fine,
        in_specs=(
            P(both, None),
            P(both),
            P(both, None),
            P(dp),
            P(dp, None),
            P(dp, None),
            P(dp, None),
            P(dp, None),
            P(dp),
            P(dp, None),
            P(expert, None, None),
            P(expert, None, None),
            P(expert, None, None),
            P(both, None),
        ),
        out_specs=(
            P(both, None),
            P(both, None),
            P(dp),
            P(dp, None),
            P(dp, None),
            P(dp, None),
            P(dp, None),
            P(dp),
            P(dp, None),
            P(expert, None, None),
            P(expert, None, None),
            P(expert, None, None),
        ),
        check_vma=False,
    )
```

```python
import jax
import jax.numpy as jnp
from jax import lax
from jax.experimental import pallas as pl
from jax.experimental.pallas import tpu as pltpu
from jax.sharding import Mesh, PartitionSpec as P

HEADS = 24
KV_HEADS = 8
HEAD_DIM = 64
GROUP = HEADS // KV_HEADS
TOP = 8
EXPERTS = 16

eps = 1e-06
residual_scale = 0.22
score_scale = 0.015625
rope_base = 10000.0
doc_slots = 3
MIB = 1024 * 1024

bf16 = jnp.bfloat16
f32 = jnp.float32


def mm(a, b):
    return lax.dot_general(a, b, (((1,), (0,)), ((), ())), preferred_element_type=f32)


def mm_nt(a, b):
    return lax.dot_general(a, b, (((1,), (1,)), ((), ())), preferred_element_type=f32)


def low_half(value):
    lane = lax.broadcasted_iota(jnp.int32, value.shape, 1)
    return jnp.where(lane < 64, value, jnp.zeros_like(value))


def high_half(value):
    lane = lax.broadcasted_iota(jnp.int32, value.shape, 1)
    return jnp.where(lane >= 64, value, jnp.zeros_like(value))


def quarter(value):
    lane = lax.broadcasted_iota(jnp.int32, value.shape, 1)
    up, down = pltpu.roll(value, 96, 1), pltpu.roll(value, 32, 1)
    return jnp.where(lane % 64 < 32, -up, down)


def query_bounds(ids, chunk, starts):
    lane = lax.broadcasted_iota(jnp.int32, (1, 256), 1)
    place = jnp.where(lane < 128, ids[2 * chunk] * 128 + lane, ids[2 * chunk + 1] * 128 + lane - 128)
    place = place.astype(f32)
    one = jnp.concatenate([starts[0:1], starts[0:1]], axis=1)
    two = jnp.concatenate([starts[1:2], starts[1:2]], axis=1)
    begin = jnp.where(place >= two, two, jnp.where(place >= one, one, jnp.zeros_like(one)))
    return place, begin


def key_mask(ids, place, begin):
    rows = lax.broadcasted_iota(jnp.int32, (128, 256), 0).astype(f32)
    pieces = []
    for b in range(8):
        at = rows + (ids[b] * 128).astype(f32)
        pieces.append((at <= place) & (at >= begin))
    return jnp.concatenate(pieces, axis=0)


def attend_body(ids, *refs):
    blocks, w = refs[:8], refs[8:12]
    (gain, cos_t, sin_t, freq,
     normed, q01, q2k, val, lse, cos_o, sin_o, starts, mixed, ka, kb, vt) = refs[12:]
    one = jnp.zeros((1, 128), f32)
    two = jnp.zeros((1, 128), f32)
    for b in range(8):
        seg = blocks[b][:, 1536:1664].astype(f32)
        one = one + jnp.sum(jnp.where(seg < 0.5, 1.0, 0.0), axis=0, keepdims=True)
        two = two + jnp.sum(jnp.where(seg < 1.5, 1.0, 0.0), axis=0, keepdims=True)
    starts[...] = jnp.concatenate([one, two, jnp.zeros((6, 128), f32)], axis=0)
    begin_rows = jnp.concatenate([one, two, jnp.zeros((6, 128), f32)], axis=0)
    angles = begin_rows * freq[...]
    cos_b, sin_b = jnp.cos(angles), jnp.sin(angles)
    for b in range(8):
        x = blocks[b][:, 0:1536].astype(f32)
        r = lax.rsqrt(jnp.mean(x * x, axis=1, keepdims=True) + eps)
        normed[b * 128 : (b + 1) * 128, :] = (x * r * gain[...]).astype(bf16)
    def project(c, carry):
        at = pl.ds(pl.multiple_of(c * 256, 256), 256)
        u = jnp.zeros((256, 384), f32)
        for m in range(4):
            cols = pl.ds(pl.multiple_of(lax.rem(ids[8] + m, 4) * 384, 128), 384)
            u = u + mm(normed[at, cols], w[m][...])
        rows = lax.broadcasted_iota(jnp.int32, (128, 128), 0)
        place = jnp.concatenate(
            [rows + ids[2 * c] * 128, rows + ids[2 * c + 1] * 128], axis=0
        ).astype(f32)
        in_two, in_one = place >= two, place >= one
        cb = jnp.where(in_two, cos_b[1:2], jnp.where(in_one, cos_b[0:1], 1.0))
        sb = jnp.where(in_two, sin_b[1:2], jnp.where(in_one, sin_b[0:1], 0.0))
        ct, st = cos_t[at, :], sin_t[at, :]
        cc = ct * cb + st * sb
        ss = st * cb - ct * sb
        cos_o[at, :] = cc
        sin_o[at, :] = ss
        a, bq, v = u[:, 0:128], u[:, 128:256], u[:, 256:384]
        a = a * cc + quarter(a) * ss
        bq = bq * cc + quarter(bq) * ss
        v = low_half(v)
        q01[at, :] = a.astype(bf16)
        q2k[at, :] = bq.astype(bf16)
        val[at, :] = v.astype(bf16)
        k = high_half(bq) * score_scale
        kb[at, :] = k.astype(bf16)
        ka[at, :] = pltpu.roll(k, 64, 1).astype(bf16)
        vt[:, at] = v.T.astype(bf16)
        return carry

    lax.fori_loop(0, 4, project, 0)

    def attend(c, carry):
        at = pl.ds(pl.multiple_of(c * 256, 256), 256)
        place, begin = query_bounds(ids, c, starts)
        allowed = key_mask(ids, place, begin)
        outs = []
        for h in range(3):
            q = q2k[at, :] if h == 2 else q01[at, :]
            kk = kb if h == 1 else ka
            s = mm_nt(kk[...], q)
            s = jnp.where(allowed, s, -1e30)
            top = jnp.max(s, axis=0, keepdims=True)
            p = jnp.exp(s - top)
            total = jnp.sum(p, axis=0, keepdims=True)
            lse[h : h + 1, at] = top + jnp.log(total)
            pb = (p * (1.0 / total)).astype(bf16)
            outs.append(mm(vt[0:64, :], pb))
        out = jnp.concatenate(outs + [jnp.zeros((64, 256), f32)], axis=0).T.astype(bf16)
        mixed[ids[2 * c]] = out[0:128]
        mixed[ids[2 * c + 1]] = out[128:256]
        return carry

    lax.fori_loop(0, 4, attend, 0)


def attend_forward(ids, blocks, w, gain, cos_t, sin_t, freq):
    vm = pl.BlockSpec(memory_space=pltpu.VMEM)
    shape = jax.ShapeDtypeStruct
    return pl.pallas_call(
        attend_body,
        out_shape=(
            shape((1024, 1536), bf16),
            shape((1024, 128), bf16),
            shape((1024, 128), bf16),
            shape((1024, 128), bf16),
            shape((8, 1024), f32),
            shape((1024, 128), f32),
            shape((1024, 128), f32),
            shape((8, 128), f32),
            shape((8, 128, 256), bf16),
        ),
        in_specs=[pl.BlockSpec(memory_space=pltpu.SMEM)] + [vm] * 16,
        out_specs=(vm,) * 9,
        scratch_shapes=[
            pltpu.VMEM((1024, 128), bf16),
            pltpu.VMEM((1024, 128), bf16),
            pltpu.VMEM((128, 1024), bf16),
        ],
        compiler_params=pltpu.CompilerParams(vmem_limit_bytes=56 * MIB),
        cost_estimate=pl.CostEstimate(flops=14_000_000_000, bytes_accessed=12_000_000, transcendentals=3_200_000),
        name="attend_forward",
    )(ids, *blocks, *w, gain, cos_t, sin_t, freq)


def attend_back_body(ids, *refs):
    w = refs[:4]
    (gm, q01, q2k, val, lse, cc, ss, starts, normed, gain,
     dqkv, own, other, grad_gain, ka, kb, vb, kt, do01, do2, dk, dv, d01, dq2, gn) = refs[4:]
    k = high_half(q2k[...].astype(f32)) * score_scale
    kb[...] = k.astype(bf16)
    k_low = pltpu.roll(k, 64, 1)
    ka[...] = k_low.astype(bf16)
    kt[...] = k_low.T.astype(bf16)
    vb[...] = pltpu.roll(val[...].astype(f32), 64, 1).astype(bf16)
    for b in range(8):
        do01[b * 128 : (b + 1) * 128, :] = gm[ids[b], :, 0:128]
        do2[b * 128 : (b + 1) * 128, :] = gm[ids[b], :, 128:256]
    dk[...] = jnp.zeros_like(dk)
    dv[...] = jnp.zeros_like(dv)

    def step(c, carry):
        at = pl.ds(pl.multiple_of(c * 256, 256), 256)
        place, begin = query_bounds(ids, c, starts)
        allowed = key_mask(ids, place, begin)
        qa, qb = q01[at, :], q2k[at, :]
        da, db = do01[at, :], do2[at, :]
        outs = []
        for h in range(3):
            q = qb if h == 2 else qa
            kk = kb if h == 1 else ka
            s = mm_nt(kk[...], q)
            p = jnp.where(allowed, jnp.exp(s - lse[h : h + 1, at]), 0.0)
            d = db if h == 2 else da
            vv = vb if h == 1 else val
            dp = mm_nt(vv[...], d)
            delta = jnp.sum(p * dp, axis=0, keepdims=True)
            ds = (p * (dp - delta)).astype(bf16)
            outs.append(mm(kt[0:64, :], ds))
            half = high_half if h == 1 else low_half
            dk[...] += mm(ds, half(q))
            dv[...] += mm(p.astype(bf16), half(d))
        out = jnp.concatenate(outs + [jnp.zeros((64, 256), f32)], axis=0).T
        d01[at, :] = out[:, 0:128]
        dq2[at, :] = out[:, 128:256]
        return carry

    lax.fori_loop(0, 4, step, 0)

    def finish(c, total):
        at = pl.ds(pl.multiple_of(c * 256, 256), 256)
        dkk = dk[at, :]
        dkk = (dkk + pltpu.roll(dkk, 64, 1)) * score_scale
        dvv = dv[at, :]
        dvv = low_half(dvv + pltpu.roll(dvv, 64, 1))
        a = d01[at, :]
        lane = lax.broadcasted_iota(jnp.int32, (256, 128), 1)
        b = jnp.where(lane < 64, dq2[at, :], dkk)
        cos, sin = cc[at, :], ss[at, :]
        a = a * cos - quarter(a) * sin
        b = b * cos - quarter(b) * sin
        row = jnp.concatenate([a, b, dvv], axis=1).astype(bf16)
        dqkv[at, :] = row
        for m in range(4):
            cols = pl.ds(pl.multiple_of(lax.rem(ids[8] + m, 4) * 384, 128), 384)
            gn[:, cols] = mm_nt(row, w[m][...])
        whole = gn[...]
        total = total + jnp.sum(whole * normed[at, :].astype(f32), axis=0, keepdims=True)
        low = whole.astype(bf16)
        own[c] = low[0:128]
        other[c] = low[128:256]
        return total

    total = lax.fori_loop(0, 4, finish, jnp.zeros((1, 1536), f32))
    grad_gain[...] = total / gain[...]


def attend_backward(ids, gm, q01, q2k, val, lse, cc, ss, starts, normed, w, gain):
    vm = pl.BlockSpec(memory_space=pltpu.VMEM)
    shape = jax.ShapeDtypeStruct
    half = pltpu.VMEM((1024, 128), bf16)
    full = pltpu.VMEM((1024, 128), f32)
    return pl.pallas_call(
        attend_back_body,
        out_shape=(
            shape((1024, 384), bf16),
            shape((4, 128, 1536), bf16),
            shape((4, 128, 1536), bf16),
            shape((1, 1536), f32),
        ),
        in_specs=[pl.BlockSpec(memory_space=pltpu.SMEM)] + [vm] * 14,
        out_specs=(vm,) * 4,
        scratch_shapes=[
            half, half, half, pltpu.VMEM((128, 1024), bf16), half, half, full, full, full, full,
            pltpu.VMEM((256, 1536), f32),
        ],
        compiler_params=pltpu.CompilerParams(vmem_limit_bytes=56 * MIB),
        cost_estimate=pl.CostEstimate(flops=16_000_000_000, bytes_accessed=14_000_000, transcendentals=3_200_000),
        name="attend_backward",
    )(ids, *w, gm, q01, q2k, val, lse, cc, ss, starts, normed, gain)


def experts_body(me, *refs):
    blocks = refs[:8]
    (grads, back, gate_w, up_w, d_gate, d_up, d_down, aw, gg, gu, routed, s, st, col) = refs[8:]
    e, c = pl.program_id(0), pl.program_id(1)

    @pl.when((e == 0) & (c == 0))
    def _():
        for b in range(8):
            rows = blocks[b][:, 0:1536]
            s[b * 128 : (b + 1) * 128, :] = rows
            st[:, b * 128 : (b + 1) * 128] = rows.T
        routed[...] = jnp.zeros_like(routed)

    @pl.when(c == 0)
    def _():
        lane = lax.broadcasted_iota(jnp.int32, (128, 128), 1)
        name = 2 * me[0] + e
        hit = (lane == name) | (lane == name + 16)
        for b in range(8):
            table = blocks[b][:, 1536:1664].astype(f32)
            w = jnp.sum(jnp.where(hit, table, 0.0), axis=1, keepdims=True)
            col[b * 128 : (b + 1) * 128, :] = jnp.broadcast_to(w, (128, 128))

    def forward(r, carry):
        at = pl.ds(pl.multiple_of(r * 256, 256), 256)
        x = s[at, :]
        gated = mm(x, gate_w[0])
        upper = mm(x, up_w[0])
        h = back[at, :].astype(f32)
        w = jnp.concatenate([col[at, :]] * 2, axis=1)
        sig = 1.0 / (1.0 + jnp.exp(-gated))
        silu = gated * sig
        act = silu * upper
        aw[at, :] = (act * w).astype(bf16)
        dots = residual_scale * jnp.sum(act * h, axis=1, keepdims=True)
        lane = lax.broadcasted_iota(jnp.int32, (256, 128), 1)
        routed[at, :] += jnp.where(lane == 2 * me[0] + e, dots, 0.0)
        ga = h * (w * residual_scale)
        gg[at, :] = (ga * upper * sig * (1.0 + gated * (1.0 - sig))).astype(bf16)
        gu[at, :] = (ga * silu).astype(bf16)
        return carry

    lax.fori_loop(0, 4, forward, 0)

    d_down[0] = (mm(aw[...].T, grads[...]) * residual_scale).astype(bf16)

    def weights(r, carry):
        at = pl.ds(pl.multiple_of(r * 512, 512), 512)
        x = st[at, :]
        d_gate[0, at, :] = mm(x, gg[...]).astype(bf16)
        d_up[0, at, :] = mm(x, gu[...]).astype(bf16)
        return carry

    lax.fori_loop(0, 3, weights, 0)


def experts(me, blocks, grads, back, gate_w, up_w):
    vm = pl.BlockSpec(memory_space=pltpu.VMEM)
    shape = jax.ShapeDtypeStruct
    wide = pl.BlockSpec((1, 1536, 256), lambda e, c: (e, 0, c))
    tall = pl.BlockSpec((1, 256, 1536), lambda e, c: (e, c, 0))
    line = pl.BlockSpec((1024, 256), lambda e, c: (0, 2 * e + c))
    return pl.pallas_call(
        experts_body,
        grid=(2, 2),
        out_shape=(
            shape((2, 1536, 512), bf16),
            shape((2, 1536, 512), bf16),
            shape((2, 512, 1536), bf16),
            shape((1024, 1024), bf16),
            shape((1024, 1024), bf16),
            shape((1024, 1024), bf16),
            shape((1024, 128), f32),
        ),
        in_specs=[pl.BlockSpec(memory_space=pltpu.SMEM)] + [vm] * 9 + [line, wide, wide],
        out_specs=(wide, wide, tall, line, line, line, vm),
        scratch_shapes=[
            pltpu.VMEM((1024, 1536), bf16),
            pltpu.VMEM((1536, 1024), bf16),
            pltpu.VMEM((1024, 128), f32),
        ],
        compiler_params=pltpu.CompilerParams(vmem_limit_bytes=56 * MIB),
        cost_estimate=pl.CostEstimate(flops=16_000_000_000, bytes_accessed=34_000_000, transcendentals=1_000_000),
        name="experts",
    )(me, *blocks, grads, back, gate_w, up_w)


def back_body(gg, gu, routed, gate_w, up_w, own, other):
    total = mm_nt(gg[:, 0:512], gate_w[0]) + mm_nt(gg[:, 512:1024], gate_w[1])
    total = total + mm_nt(gu[:, 0:512], up_w[0]) + mm_nt(gu[:, 512:1024], up_w[1])
    table = routed[...]
    high = table.astype(bf16)
    low = pltpu.roll(table - high.astype(f32), 16, 1).astype(bf16)
    lane = lax.broadcasted_iota(jnp.int32, table.shape, 1)
    tail = jnp.where(lane < 16, high, low)
    total = total.astype(bf16)
    own[0, :, 0:1536] = total[0:128]
    other[0, :, 0:1536] = total[128:256]
    own[0, :, 1536:1664] = tail[0:128]
    other[0, :, 1536:1664] = tail[128:256]


def experts_back(gg, gu, routed, gate_w, up_w):
    vm = pl.BlockSpec(memory_space=pltpu.VMEM)
    line = pl.BlockSpec((256, 1024), lambda m: (m, 0))
    out = pl.BlockSpec((1, 128, 1664), lambda m: (m, 0, 0))
    shape = jax.ShapeDtypeStruct((4, 128, 1664), bf16)
    return pl.pallas_call(
        back_body,
        grid=(4,),
        out_shape=(shape, shape),
        in_specs=[line, line, pl.BlockSpec((256, 128), lambda m: (m, 0)), vm, vm],
        out_specs=(out, out),
        compiler_params=pltpu.CompilerParams(vmem_limit_bytes=56 * MIB),
        cost_estimate=pl.CostEstimate(flops=1_000_000, bytes_accessed=100_000, transcendentals=0),
        name="experts_back",
    )(gg, gu, routed, gate_w, up_w)


def combine_body(aw, down_w, own, other):
    total = mm(aw[:, 0:512], down_w[0]) + mm(aw[:, 512:1024], down_w[1])
    total = total.astype(bf16)
    own[0] = total[0:128]
    other[0] = total[128:256]


def combine(aw, down_w):
    vm = pl.BlockSpec(memory_space=pltpu.VMEM)
    out = pl.BlockSpec((1, 128, 1536), lambda m: (m, 0, 0))
    shape = jax.ShapeDtypeStruct((4, 128, 1536), bf16)
    return pl.pallas_call(
        combine_body,
        grid=(4,),
        out_shape=(shape, shape),
        in_specs=[pl.BlockSpec((256, 1024), lambda m: (m, 0)), vm],
        out_specs=(out, out),
        compiler_params=pltpu.CompilerParams(vmem_limit_bytes=56 * MIB),
        cost_estimate=pl.CostEstimate(flops=1_000_000, bytes_accessed=100_000, transcendentals=0),
        name="combine",
    )(aw, down_w)


def back_rows_body(*refs):
    blocks, (down_w, grads, back) = refs[:8], refs[8:]

    @pl.when(pl.program_id(0) == 0)
    def _():
        for b in range(8):
            grads[b * 128 : (b + 1) * 128, :] = blocks[b][...]

    back[...] = mm_nt(grads[...], down_w[0]).astype(bf16)


def back_rows(blocks, down_w):
    vm = pl.BlockSpec(memory_space=pltpu.VMEM)
    shape = jax.ShapeDtypeStruct
    return pl.pallas_call(
        back_rows_body,
        grid=(2,),
        out_shape=(shape((1024, 1536), bf16), shape((1024, 1024), bf16)),
        in_specs=[vm] * 8 + [pl.BlockSpec((1, 512, 1536), lambda e: (e, 0, 0))],
        out_specs=(vm, pl.BlockSpec((1024, 512), lambda e: (0, e))),
        compiler_params=pltpu.CompilerParams(vmem_limit_bytes=56 * MIB),
        cost_estimate=pl.CostEstimate(flops=3_200_000_000, bytes_accessed=11_000_000, transcendentals=0),
        name="back_rows",
    )(*blocks, down_w)


def weight_body(a, b, extra, out):
    out[...] = (mm(a[...].T, b[...]) + extra[...].astype(f32)).astype(bf16)


def weight_grad(a, b, extra):
    n = b.shape[1]
    line = pl.BlockSpec((256, n), lambda i: (i, 0))
    return pl.pallas_call(
        weight_body,
        grid=(6,),
        out_shape=jax.ShapeDtypeStruct((1536, n), bf16),
        in_specs=[
            pl.BlockSpec((1024, 256), lambda i: (0, i)),
            pl.BlockSpec((1024, n), lambda i: (0, 0)),
            line,
        ],
        out_specs=line,
        compiler_params=pltpu.CompilerParams(vmem_limit_bytes=56 * MIB),
        cost_estimate=pl.CostEstimate(flops=1_000_000_000, bytes_accessed=6_000_000, transcendentals=0),
        name="weight_grad",
    )(a, b, extra)


def assemble_body(place, *refs):
    blocks, (query, key, value, out, rest) = refs[:8], refs[8:]
    first = place[1] == 0
    total = jnp.zeros((96, 128), f32)
    for m in range(4):
        here, there = blocks[2 * m][...].astype(f32), blocks[2 * m + 1][...].astype(f32)
        total = total + here[:, 256:384] + there[:, 256:384]
        a, b = jnp.where(first, here, there), jnp.where(first, there, here)
        chip = lax.rem(place[0] + m, 4)
        wide = pl.ds(pl.multiple_of(chip * 384, 128), 384)
        slim = pl.ds(pl.multiple_of(chip * 128, 128), 128)
        query[:, wide] = jnp.concatenate([a[:, 0:192], b[:, 0:192]], axis=1)
        key[:, slim] = jnp.concatenate([a[:, 192:256], b[:, 192:256]], axis=1)
        value[:, slim] = jnp.concatenate([a[:, 256:320], b[:, 256:320]], axis=1)
        out[:, wide] = jnp.concatenate([a[:, 384:576], b[:, 384:576]], axis=1)
    rest[...] = total


def assemble(place, blocks):
    vm = pl.BlockSpec(memory_space=pltpu.VMEM)
    shape = jax.ShapeDtypeStruct
    return pl.pallas_call(
        assemble_body,
        out_shape=(
            shape((96, 1536), f32),
            shape((96, 512), f32),
            shape((96, 512), f32),
            shape((96, 1536), f32),
            shape((96, 128), f32),
        ),
        in_specs=[pl.BlockSpec(memory_space=pltpu.SMEM)] + [vm] * 8,
        out_specs=(vm,) * 5,
        cost_estimate=pl.CostEstimate(flops=1_000_000, bytes_accessed=3_000_000, transcendentals=0),
        name="assemble",
    )(place, *blocks)


def column(row):
    n = row.shape[1]
    down = lax.broadcasted_iota(jnp.int32, (n, n), 0)
    along = lax.broadcasted_iota(jnp.int32, (n, n), 1)
    return jnp.sum(jnp.where(down == along, row.astype(f32), 0.0), axis=1, keepdims=True)


def pack_body(at, w_query, w_key, w_value, gain_a, gain_b, router, tokens, seg, w_out, share, sent, half):
    first = at[1] == 0
    x = at[0]
    wide = w_query[:, pl.ds(pl.multiple_of(x * 384, 128), 384)].astype(f32)
    slim = pl.ds(pl.multiple_of(x * 128, 128), 128)
    key, value = w_key[:, slim].astype(f32), w_value[:, slim].astype(f32)
    share[...] = jnp.concatenate(
        [
            jnp.where(first, wide[:, 0:192], wide[:, 192:384]),
            jnp.where(first, key[:, 0:64], key[:, 64:128]),
            jnp.where(first, value[:, 0:64], value[:, 64:128]),
            column(gain_a[...]),
            column(gain_b[...]),
            router[...].astype(f32),
            jnp.zeros((96, 46), f32),
        ],
        axis=1,
    ).astype(bf16)
    sent[:, 0:1536] = tokens[...]
    sent[:, 1536:1664] = jnp.broadcast_to(column(seg[...]), (128, 128)).astype(bf16)
    half[...] = w_out[:, pl.ds(pl.multiple_of(at[1] * 768, 128), 768)]


def pack(at, w_query, w_key, w_value, gain_a, gain_b, router, tokens, seg, w_out):
    vm = pl.BlockSpec(memory_space=pltpu.VMEM)
    shape = jax.ShapeDtypeStruct
    return pl.pallas_call(
        pack_body,
        out_shape=(shape((96, 384), bf16), shape((128, 1664), bf16), shape((96, 768), bf16)),
        in_specs=[pl.BlockSpec(memory_space=pltpu.SMEM)] + [vm] * 9,
        out_specs=(vm,) * 3,
        cost_estimate=pl.CostEstimate(flops=1_000_000, bytes_accessed=2_000_000, transcendentals=0),
        name="pack",
    )(at, w_query, w_key, w_value, gain_a, gain_b, router, tokens, seg, w_out)


def project_out_body(at, mixed, *refs):
    (near, far, tokens, gain, router, named, sent, hidden, gates, mx, hid) = refs
    core = at[1]
    for p in range(4):
        mx[:, 384 * p : 384 * (p + 1)] = jnp.concatenate(
            [mixed[2 * p, :, 0:192], mixed[2 * p + 1, :, 0:192]], axis=1
        )
    own, other = mm(mx[...], near[...]), mm(mx[...], far[...])
    hid[:, pl.ds(pl.multiple_of(core * 768, 128), 768)] = own
    hid[:, pl.ds(pl.multiple_of((1 - core) * 768, 128), 768)] = other
    value = tokens[...].astype(f32) + residual_scale * hid[...]
    hidden[...] = value
    r = lax.rsqrt(jnp.mean(value * value, axis=1, keepdims=True) + eps)
    second = (value * r * gain[...]).astype(bf16)
    sent[:, 0:1536] = second
    logits = mm(second, router[...])
    on = named[...] > 0.5
    logits = jnp.where(on, logits, -1e30)
    top = jnp.max(logits, axis=1, keepdims=True)
    e = jnp.where(on, jnp.exp(logits - top), 0.0)
    g = e / jnp.sum(e, axis=1, keepdims=True)
    gates[...] = g
    high = g.astype(bf16)
    low = pltpu.roll(g - high.astype(f32), 16, 1)
    lane = lax.broadcasted_iota(jnp.int32, g.shape, 1)
    sent[:, 1536:1664] = jnp.where(lane < 16, g, low).astype(bf16)


def project_out(at, mixed, near, far, tokens, gain, router, named):
    vm = pl.BlockSpec(memory_space=pltpu.VMEM)
    shape = jax.ShapeDtypeStruct
    return pl.pallas_call(
        project_out_body,
        out_shape=(
            shape((128, 1664), bf16),
            shape((128, 1536), f32),
            shape((128, 128), f32),
            shape((128, 1536), bf16),
        ),
        in_specs=[pl.BlockSpec(memory_space=pltpu.SMEM)] + [vm] * 7,
        out_specs=(vm,) * 4,
        scratch_shapes=[pltpu.VMEM((128, 1536), f32)],
        compiler_params=pltpu.CompilerParams(vmem_limit_bytes=56 * MIB),
        cost_estimate=pl.CostEstimate(flops=4_000_000_000, bytes_accessed=8_000_000, transcendentals=0),
        name="project_out",
    )(at, mixed, near, far, tokens, gain, router, named)


def middle_body(at, *refs):
    near, far, sums = refs[0], refs[1], refs[2:6]
    (grads, hidden, gates, gain, router, _,
     grad_hidden, heads, branch, grad_gain, grad_router, gb, gx) = refs[6:]
    core = at[1]
    total = sums[0][...]
    for other in sums[1:]:
        total = total + other[...].astype(f32)
    value = hidden[...]
    r = lax.rsqrt(jnp.mean(value * value, axis=1, keepdims=True) + eps)
    second = (value * r * gain[...]).astype(bf16)
    g = gates[...]
    table = total[:, 1536:1664]
    lane = lax.broadcasted_iota(jnp.int32, g.shape, 1)
    table = jnp.where(lane < 16, table + pltpu.roll(table, 112, 1), 0.0)
    logits = (g * (table - jnp.sum(g * table, axis=1, keepdims=True))).astype(bf16)
    grad_router[...] = mm(second.T, logits)
    grad_second = total[:, 0:1536] + mm_nt(logits, router[...])
    grad_gain[...] = jnp.sum(grad_second * value * r, axis=0, keepdims=True)
    scaled = grad_second * gain[...]
    gh = (
        grads[...].astype(f32)
        + r * scaled
        - value * (r * r * r) * jnp.mean(value * scaled, axis=1, keepdims=True)
    )
    grad_hidden[...] = gh
    low = (residual_scale * gh).astype(bf16)
    gb[...] = low
    mine = gb[:, pl.ds(pl.multiple_of(core * 768, 128), 768)]
    twin = gb[:, pl.ds(pl.multiple_of((1 - core) * 768, 128), 768)]
    gx[...] = mm_nt(mine, near[...]) + mm_nt(twin, far[...])
    zero = jnp.zeros((128, 64), bf16)
    for j in range(8):
        cols = slice(192 * j, 192 * (j + 1))
        heads[j] = jnp.concatenate([gx[:, cols].astype(bf16), zero], axis=1)
        branch[j] = jnp.concatenate([low[:, cols], zero], axis=1)


def middle(at, near, far, sums, grads, hidden, gates, gain, router, held):
    vm = pl.BlockSpec(memory_space=pltpu.VMEM)
    shape = jax.ShapeDtypeStruct
    return pl.pallas_call(
        middle_body,
        out_shape=(
            shape((128, 1536), f32),
            shape((8, 128, 256), bf16),
            shape((8, 128, 256), bf16),
            shape((1, 1536), f32),
            shape((1536, 128), f32),
        ),
        in_specs=[pl.BlockSpec(memory_space=pltpu.SMEM)] + [vm] * 11 + [pl.BlockSpec(memory_space=pl.ANY)],
        out_specs=(vm,) * 5,
        scratch_shapes=[pltpu.VMEM((128, 1536), bf16), pltpu.VMEM((128, 1536), f32)],
        compiler_params=pltpu.CompilerParams(vmem_limit_bytes=56 * MIB),
        cost_estimate=pl.CostEstimate(flops=4_000_000_000, bytes_accessed=8_000_000, transcendentals=0),
        name="middle",
    )(at, near, far, *sums, grads, hidden, gates, gain, router, held)


def shift(value, axis, amount):
    size = lax.axis_size(axis)
    return lax.ppermute(value, axis, [((i + amount) % size, i) for i in range(size)])


def swap(value):
    return lax.ppermute(value, "core", [(0, 1), (1, 0)])


def dot(a, b, dims, out=f32):
    return lax.dot_general(a, b, (dims, ((), ())), preferred_element_type=out)


def turned(stacked, start):
    return lax.dynamic_slice_in_dim(
        jnp.concatenate([stacked, stacked], axis=0), start, stacked.shape[0], axis=0
    )


def tied(*values):
    return lax.optimization_barrier(values)


def gather_x(block):
    return [block] + [shift(block, "x", m) for m in (1, 2, 3)]


def both_cores(blocks):
    return [each for block in blocks for each in (block, swap(block))]


def gather_expert(block):
    return both_cores(gather_x(block))


def scatter_core(own, other):
    near = own.astype(f32) + swap(other).astype(f32)
    return near[0], [near[m].astype(bf16) for m in range(4)]


def scatter_x(first, low):
    return [first] + [shift(low[m], "x", -m) for m in (2, 1, 3)]


def total_of(terms):
    total = terms[0]
    for term in terms[1:]:
        total = total + term.astype(f32)
    return total


def gather_y(block):
    row = jnp.stack([block] + [shift(block, "y", m) for m in (1, 2, 3)])
    return turned(row, (4 - lax.axis_index("y")) % 4).reshape(-1, block.shape[1])


def inverse_rms(values):
    return lax.rsqrt(jnp.mean(values * values, axis=-1, keepdims=True) + eps)


def per_device(
    tokens,
    segments,
    routes,
    gain_attn,
    w_query,
    w_key,
    w_value,
    w_out,
    gain_moe,
    w_router,
    expert_gate,
    expert_up,
    expert_down,
    out_grad,
):
    rows, width = tokens.shape
    parts = 8
    seq = rows * parts
    x, core = lax.axis_index("x"), lax.axis_index("core")
    me = x * 2 + core
    z = lax.axis_index("z")
    at = jnp.stack([x, core, z])

    share, sent, half = pack(
        at,
        w_query,
        w_key,
        w_value,
        gain_attn[None, :],
        gain_moe[None, :],
        w_router,
        tokens,
        segments[None, :],
        w_out,
    )
    row, half = tied(gather_y(share), half)
    out_half = lax.all_gather(half, ("z", "y"), axis=0, tiled=True)
    qkv_w = [row] + [shift(row, "z", m) for m in (1, 2, 3)]
    far = gather_x(sent)
    *far, grads_sent = tied(*far, out_grad)
    blocks = both_cores(far)
    grads_far = gather_x(grads_sent)
    extra = turned(jnp.stack([w[:, 256:384] for w in qkv_w]), (4 - z) % 4).reshape(width, 128)
    gain_one = extra[:, 64].astype(f32)[None, :]
    gain_two = extra[:, 65].astype(f32)[None, :]
    lane = jnp.arange(128, dtype=jnp.int32)
    router_w = jnp.where(lane[None, :] < 16, jnp.roll(extra, -66, axis=1), 0)

    chips = (x + jnp.arange(4, dtype=jnp.int32)) % 4
    cores = jnp.bitwise_xor(core, jnp.arange(2, dtype=jnp.int32))
    order = (chips[:, None] * 2 + cores[None, :]).reshape(parts)
    ids = jnp.concatenate([order, z[None]])
    place = (order[:, None] * rows + jnp.arange(rows, dtype=jnp.int32)[None, :]).reshape(seq)
    freq = rope_base ** (
        -(jnp.arange(128, dtype=jnp.int32) % 32).astype(f32) * 2.0 / HEAD_DIM
    )[None, :]
    angles = place.astype(f32)[:, None] * freq

    normed, q01, q2k, val, lse, cos, sin, starts, mixed_head = attend_forward(
        ids, blocks, qkv_w, gain_one, jnp.cos(angles), jnp.sin(angles), freq
    )
    lse, out_near, *grads_far = tied(lse, out_half, *grads_far)
    out_far = swap(out_near)
    grad_blocks = both_cores(grads_far)
    mixed = lax.all_to_all(mixed_head, ("x", "core"), 0, 0, tiled=True)
    named = jnp.any(routes[:, :, None] == lane[None, None, :], axis=1).astype(f32)
    sent_two, hidden, gates, mixed = project_out(
        at, mixed, out_near, out_far, tokens, gain_two, router_w, named
    )
    far_two = gather_x(sent_two)
    grad_all, back = back_rows(grad_blocks, expert_down)
    far_two[2], back = tied(far_two[2], back)
    second_blocks = both_cores(far_two)
    mixed, *second_blocks = tied(mixed, *second_blocks)
    mixed_all = lax.all_gather(mixed, ("x", "core"), axis=0, tiled=True)

    grad_w_gate, grad_w_up, grad_w_down, weighted, grad_gate_pre, grad_up_pre, routed = experts(
        me[None], second_blocks, grad_all, back, expert_gate, expert_up
    )
    sums = lax.psum((grad_w_gate, grad_w_up, grad_w_down), ("z", "y"))
    own, other = experts_back(grad_gate_pre, grad_up_pre, routed, expert_gate, expert_up)
    first, low = scatter_core(own, other)
    terms = scatter_x(first, low)
    own_out, other_out = combine(weighted, expert_down)
    first_out, low_out = scatter_core(own_out, other_out)

    grad_hidden, heads, branch, grad_gain_two, grad_router = middle(
        at, out_near, out_far, terms, out_grad, hidden, gates, gain_two, router_w, first_out
    )
    grad_heads = lax.all_to_all(heads, ("x", "core"), 0, 0, tiled=True)
    grad_heads, branch, *low_out = tied(grad_heads, branch, *low_out)
    output = (hidden + residual_scale * total_of(scatter_x(first_out, low_out))).astype(bf16)
    grad_qkv, own, other, grad_gain_one = attend_backward(
        ids, grad_heads, q01, q2k, val, lse, cos, sin, starts, normed, qkv_w, gain_one
    )
    first, low = scatter_core(own, other)
    normed_terms = scatter_x(first, low)
    inputs = tokens.astype(f32)
    branch_cols = lax.all_to_all(branch, ("x", "core"), 0, 0, tiled=True)
    rest = jnp.concatenate(
        [grad_gain_one.reshape(width, 1), grad_gain_two.reshape(width, 1), grad_router[:, :16]],
        axis=1,
    ).astype(bf16)
    grad_w_qkv = weight_grad(normed, grad_qkv, jnp.pad(rest, ((0, 0), (320, 46))))
    normed_terms[0], grad_w_qkv, branch_cols = tied(normed_terms[0], grad_w_qkv, branch_cols)
    normed_mine = total_of(normed_terms)
    scale_one = inverse_rms(inputs)
    scaled_one = normed_mine * gain_one
    grad_inputs = (
        grad_hidden
        + scale_one * scaled_one
        - inputs * scale_one**3 * jnp.mean(inputs * scaled_one, axis=-1, keepdims=True)
    )

    grad_w_out = weight_grad(
        mixed_all, branch_cols.reshape(seq, 256), jnp.zeros((width, 256), bf16)
    )
    def sum_dp(table):
        table = table.reshape(16, width // 16, table.shape[1])
        pieces = lax.all_to_all(table, ("z", "y"), 0, 0, tiled=True)
        return jnp.sum(pieces.astype(f32), axis=0).astype(bf16)

    summed = jnp.concatenate([sum_dp(grad_w_qkv), sum_dp(grad_w_out)], axis=1)
    grad_q, grad_k, grad_v, grad_o, rest = assemble(
        jnp.stack([x, core]), gather_expert(summed)
    )
    return (
        output,
        grad_inputs,
        rest[:, 64],
        grad_q,
        grad_k,
        grad_v,
        grad_o,
        rest[:, 65],
        rest[:, 66:82],
        sums[0].astype(f32),
        sums[1].astype(f32),
        sums[2].astype(f32),
    )


def solution(mesh):
    fine = Mesh(mesh.devices.reshape(4, 4, 4, 2), ("z", "y", "x", "core"))
    dp, expert, both = ("z", "y"), ("x", "core"), ("z", "y", "x", "core")
    placed = (
        P(both, None),
        P(both),
        P(both, None),
        P(dp),
        P(dp, None),
        P(dp, None),
        P(dp, None),
        P(dp, None),
        P(dp),
        P(dp, None),
        P(expert, None, None),
        P(expert, None, None),
        P(expert, None, None),
    )
    return jax.shard_map(
        per_device,
        mesh=fine,
        in_specs=placed + (P(both, None),),
        out_specs=(P(both, None),) * 2 + placed[3:],
        check_vma=False,
    )
```

```python
import jax
import jax.numpy as jnp
from jax import lax
from jax.experimental import pallas as pl
from jax.experimental.pallas import tpu as pltpu
from jax.sharding import Mesh, PartitionSpec as P

HEADS = 24
KV_HEADS = 8
HEAD_DIM = 64
GROUP = HEADS // KV_HEADS
TOP = 8
EXPERTS = 16

eps = 1e-06
residual_scale = 0.22
score_scale = 0.015625
rope_base = 10000.0
doc_slots = 3
MIB = 1024 * 1024

bf16 = jnp.bfloat16
f32 = jnp.float32


def mm(a, b):
    return lax.dot_general(a, b, (((1,), (0,)), ((), ())), preferred_element_type=f32)


def mm_nt(a, b):
    return lax.dot_general(a, b, (((1,), (1,)), ((), ())), preferred_element_type=f32)


def low_half(value):
    lane = lax.broadcasted_iota(jnp.int32, value.shape, 1)
    return jnp.where(lane < 64, value, jnp.zeros_like(value))


def high_half(value):
    lane = lax.broadcasted_iota(jnp.int32, value.shape, 1)
    return jnp.where(lane >= 64, value, jnp.zeros_like(value))


def quarter(value):
    lane = lax.broadcasted_iota(jnp.int32, value.shape, 1)
    up, down = pltpu.roll(value, 96, 1), pltpu.roll(value, 32, 1)
    return jnp.where(lane % 64 < 32, -up, down)


def visible(chunk, starts):
    keys = 256 * (chunk + 1)
    place = (256 * chunk + lax.broadcasted_iota(jnp.int32, (1, 256), 1)).astype(f32)
    one = jnp.concatenate([starts[0:1], starts[0:1]], axis=1)
    two = jnp.concatenate([starts[1:2], starts[1:2]], axis=1)
    begin = jnp.where(place >= two, two, jnp.where(place >= one, one, jnp.zeros_like(one)))
    at = lax.broadcasted_iota(jnp.int32, (keys, 256), 0).astype(f32)
    return (at <= place) & (at >= begin)


def attend_body(ids, *refs):
    blocks = refs[:8]
    (w, gain, cos_t, sin_t, freq, _, __,
     normed, q01, q2k, val, lse, cos_o, sin_o, starts, mixed, ka, kb, vt) = refs[8:]
    one = jnp.zeros((1, 128), f32)
    two = jnp.zeros((1, 128), f32)
    for b in range(8):
        seg = blocks[b][:, 1536:1664].astype(f32)
        one = one + jnp.sum(jnp.where(seg < 0.5, 1.0, 0.0), axis=0, keepdims=True)
        two = two + jnp.sum(jnp.where(seg < 1.5, 1.0, 0.0), axis=0, keepdims=True)
    starts[...] = jnp.concatenate([one, two, jnp.zeros((6, 128), f32)], axis=0)
    begin_rows = jnp.concatenate([one, two, jnp.zeros((6, 128), f32)], axis=0)
    angles = begin_rows * freq[...]
    cos_b, sin_b = jnp.cos(angles), jnp.sin(angles)
    for b in range(8):
        x = blocks[b][:, 0:1536].astype(f32)
        r = lax.rsqrt(jnp.mean(x * x, axis=1, keepdims=True) + eps)
        at = pl.ds(pl.multiple_of(ids[b] * 128, 128), 128)
        normed[at, :] = (x * r * gain[...]).astype(bf16)
    def project(c, carry):
        at = pl.ds(pl.multiple_of(c * 256, 256), 256)
        u = mm(normed[at, :], w[...])
        place = (lax.broadcasted_iota(jnp.int32, (256, 128), 0) + c * 256).astype(f32)
        in_two, in_one = place >= two, place >= one
        cb = jnp.where(in_two, cos_b[1:2], jnp.where(in_one, cos_b[0:1], 1.0))
        sb = jnp.where(in_two, sin_b[1:2], jnp.where(in_one, sin_b[0:1], 0.0))
        ct, st = cos_t[at, :], sin_t[at, :]
        cc = ct * cb + st * sb
        ss = st * cb - ct * sb
        cos_o[at, :] = cc
        sin_o[at, :] = ss
        a, bq, v = u[:, 0:128], u[:, 128:256], u[:, 256:384]
        a = a * cc + quarter(a) * ss
        bq = bq * cc + quarter(bq) * ss
        v = low_half(v)
        q01[at, :] = a.astype(bf16)
        q2k[at, :] = bq.astype(bf16)
        val[at, :] = v.astype(bf16)
        k = high_half(bq) * score_scale
        kb[at, :] = k.astype(bf16)
        ka[at, :] = pltpu.roll(k, 64, 1).astype(bf16)
        vt[:, at] = v.T.astype(bf16)
        return carry

    lax.fori_loop(0, 4, project, 0)

    for c in range(4):
        at, seen = slice(256 * c, 256 * (c + 1)), slice(0, 256 * (c + 1))
        allowed = visible(c, starts)
        outs = []
        for h in range(3):
            q = q2k[at, :] if h == 2 else q01[at, :]
            kk = kb if h == 1 else ka
            s = mm_nt(kk[seen, :], q)
            s = jnp.where(allowed, s, -1e30)
            top = jnp.max(s, axis=0, keepdims=True)
            p = jnp.exp(s - top)
            total = jnp.sum(p, axis=0, keepdims=True)
            lse[h : h + 1, at] = top + jnp.log(total)
            pb = (p * (1.0 / total)).astype(bf16)
            outs.append(mm(vt[0:64, seen], pb))
        out = jnp.concatenate(outs + [jnp.zeros((64, 256), f32)], axis=0).T.astype(bf16)
        mixed[2 * c] = out[0:128]
        mixed[2 * c + 1] = out[128:256]


def attend_forward(ids, blocks, w, gain, cos_t, sin_t, freq, held):
    vm = pl.BlockSpec(memory_space=pltpu.VMEM)
    shape = jax.ShapeDtypeStruct
    return pl.pallas_call(
        attend_body,
        out_shape=(
            shape((1024, 1536), bf16),
            shape((1024, 128), bf16),
            shape((1024, 128), bf16),
            shape((1024, 128), bf16),
            shape((8, 1024), f32),
            shape((1024, 128), f32),
            shape((1024, 128), f32),
            shape((8, 128), f32),
            shape((8, 128, 256), bf16),
        ),
        in_specs=[pl.BlockSpec(memory_space=pltpu.SMEM)]
        + [vm] * 13
        + [pl.BlockSpec(memory_space=pl.ANY)] * 2,
        out_specs=(vm,) * 9,
        scratch_shapes=[
            pltpu.VMEM((1024, 128), bf16),
            pltpu.VMEM((1024, 128), bf16),
            pltpu.VMEM((128, 1024), bf16),
        ],
        compiler_params=pltpu.CompilerParams(vmem_limit_bytes=56 * MIB),
        cost_estimate=pl.CostEstimate(flops=14_000_000_000, bytes_accessed=12_000_000, transcendentals=3_200_000),
        name="attend_forward",
    )(ids, *blocks, w, gain, cos_t, sin_t, freq, *held)


def attend_back_body(
    here, w, gm, q01, q2k, val, lse, cc, ss, starts, normed, gain,
    dqkv, own, other, grad_gain, ka, kb, vb, kt, do01, do2, dk, dv, d01, dq2,
):
    k = high_half(q2k[...].astype(f32)) * score_scale
    kb[...] = k.astype(bf16)
    k_low = pltpu.roll(k, 64, 1)
    ka[...] = k_low.astype(bf16)
    kt[...] = k_low.T.astype(bf16)
    vb[...] = pltpu.roll(val[...].astype(f32), 64, 1).astype(bf16)
    for b in range(8):
        do01[b * 128 : (b + 1) * 128, :] = gm[b, :, 0:128]
        do2[b * 128 : (b + 1) * 128, :] = gm[b, :, 128:256]
    dk[...] = jnp.zeros_like(dk)
    dv[...] = jnp.zeros_like(dv)

    for c in range(4):
        at, seen = slice(256 * c, 256 * (c + 1)), slice(0, 256 * (c + 1))
        allowed = visible(c, starts)
        qa, qb = q01[at, :], q2k[at, :]
        da, db = do01[at, :], do2[at, :]
        outs = []
        for h in range(3):
            q = qb if h == 2 else qa
            kk = kb if h == 1 else ka
            s = mm_nt(kk[seen, :], q)
            p = jnp.where(allowed, jnp.exp(s - lse[h : h + 1, at]), 0.0)
            d = db if h == 2 else da
            vv = vb if h == 1 else val
            dp = mm_nt(vv[seen, :], d)
            delta = jnp.sum(p * dp, axis=0, keepdims=True)
            ds = (p * (dp - delta)).astype(bf16)
            outs.append(mm(kt[0:64, seen], ds))
            half = high_half if h == 1 else low_half
            dk[seen, :] += mm(ds, half(q))
            dv[seen, :] += mm(p.astype(bf16), half(d))
        out = jnp.concatenate(outs + [jnp.zeros((64, 256), f32)], axis=0).T
        d01[at, :] = out[:, 0:128]
        dq2[at, :] = out[:, 128:256]

    def finish(c, total):
        at = pl.ds(pl.multiple_of(c * 256, 256), 256)
        dkk = dk[at, :]
        dkk = (dkk + pltpu.roll(dkk, 64, 1)) * score_scale
        dvv = dv[at, :]
        dvv = low_half(dvv + pltpu.roll(dvv, 64, 1))
        a = d01[at, :]
        lane = lax.broadcasted_iota(jnp.int32, (256, 128), 1)
        b = jnp.where(lane < 64, dq2[at, :], dkk)
        cos, sin = cc[at, :], ss[at, :]
        a = a * cos - quarter(a) * sin
        b = b * cos - quarter(b) * sin
        row = jnp.concatenate([a, b, dvv], axis=1).astype(bf16)
        dqkv[at, :] = row
        whole = mm_nt(row, w[...])
        total = total + jnp.sum(whole * normed[at, :].astype(f32), axis=0, keepdims=True)
        low = whole.astype(bf16)
        m = lax.rem(c - here[0] + 4, 4)
        own[m] = jnp.where(here[1] == 0, low[0:128], low[128:256])
        other[m] = jnp.where(here[1] == 0, low[128:256], low[0:128])
        return total

    total = lax.fori_loop(0, 4, finish, jnp.zeros((1, 1536), f32))
    grad_gain[...] = total / gain[...]


def attend_backward(here, gm, q01, q2k, val, lse, cc, ss, starts, normed, w, gain):
    vm = pl.BlockSpec(memory_space=pltpu.VMEM)
    shape = jax.ShapeDtypeStruct
    half = pltpu.VMEM((1024, 128), bf16)
    full = pltpu.VMEM((1024, 128), f32)
    return pl.pallas_call(
        attend_back_body,
        out_shape=(
            shape((1024, 384), bf16),
            shape((4, 128, 1536), bf16),
            shape((4, 128, 1536), bf16),
            shape((1, 1536), f32),
        ),
        in_specs=[pl.BlockSpec(memory_space=pltpu.SMEM)] + [vm] * 11,
        out_specs=(vm,) * 4,
        scratch_shapes=[
            half, half, half, pltpu.VMEM((128, 1024), bf16), half, half, full, full, full, full,
        ],
        compiler_params=pltpu.CompilerParams(vmem_limit_bytes=56 * MIB),
        cost_estimate=pl.CostEstimate(flops=1_000_000, bytes_accessed=100_000, transcendentals=0),
        name="attend_backward",
    )(here, w, gm, q01, q2k, val, lse, cc, ss, starts, normed, gain)


def experts_body(
    here, second, grads, back, gate_w, up_w, d_gate, d_up, d_down, aw, gg, gu, routed, st, col
):
    e, c = pl.program_id(0), pl.program_id(1)
    first = (e == 0) & (c == 0)

    @pl.when(first)
    def _():
        for b in range(8):
            at = slice(128 * b, 128 * (b + 1))
            st[:, at] = second[at, 0:1536].T
        routed[...] = jnp.zeros_like(routed)

    @pl.when(c == 0)
    def _():
        lane = lax.broadcasted_iota(jnp.int32, (128, 128), 1)
        name = 4 * here[0] + 2 * here[1] + e
        hit = (lane == name) | (lane == name + 16)
        for b in range(8):
            at = slice(128 * b, 128 * (b + 1))
            table = second[at, 1536:1664].astype(f32)
            w = jnp.sum(jnp.where(hit, table, 0.0), axis=1, keepdims=True)
            col[at, :] = jnp.broadcast_to(w, (128, 128))

    x = second[:, 0:1536]
    gated = mm(x, gate_w[0])
    upper = mm(x, up_w[0])
    h = back[...].astype(f32)
    w = jnp.concatenate([col[...]] * 2, axis=1)
    sig = 1.0 / (1.0 + jnp.exp(-gated))
    silu = gated * sig
    act = silu * upper
    aw[...] = (act * w).astype(bf16)
    dots = residual_scale * jnp.sum(act * h, axis=1, keepdims=True)
    lane = lax.broadcasted_iota(jnp.int32, (1024, 128), 1)
    routed[...] += jnp.where(lane == 4 * here[0] + 2 * here[1] + e, dots, 0.0)
    ga = h * (w * residual_scale)
    gg[...] = (ga * upper * (sig * (1.0 + gated * (1.0 - sig)))).astype(bf16)
    gu[...] = (ga * silu).astype(bf16)

    d_gate[0] = mm(st[...], gg[...]).astype(bf16)
    d_up[0] = mm(st[...], gu[...]).astype(bf16)
    d_down[0] = (mm(aw[...].T, grads[...]) * residual_scale).astype(bf16)


def experts(here, second, grads, back, gate_w, up_w):
    vm = pl.BlockSpec(memory_space=pltpu.VMEM)
    shape = jax.ShapeDtypeStruct
    wide = pl.BlockSpec((1, 1536, 256), lambda e, c: (e, 0, c))
    tall = pl.BlockSpec((1, 256, 1536), lambda e, c: (e, c, 0))
    line = pl.BlockSpec((1024, 256), lambda e, c: (0, 2 * e + c))
    return pl.pallas_call(
        experts_body,
        grid=(2, 2),
        out_shape=(
            shape((2, 1536, 512), bf16),
            shape((2, 1536, 512), bf16),
            shape((2, 512, 1536), bf16),
            shape((1024, 1024), bf16),
            shape((1024, 1024), bf16),
            shape((1024, 1024), bf16),
            shape((1024, 128), f32),
        ),
        in_specs=[pl.BlockSpec(memory_space=pltpu.SMEM)] + [vm] * 2 + [line, wide, wide],
        out_specs=(wide, wide, tall, line, line, line, vm),
        scratch_shapes=[pltpu.VMEM((1536, 1024), bf16), pltpu.VMEM((1024, 128), f32)],
        compiler_params=pltpu.CompilerParams(vmem_limit_bytes=60 * MIB),
        cost_estimate=pl.CostEstimate(flops=16_000_000_000, bytes_accessed=34_000_000, transcendentals=1_000_000),
        name="experts",
    )(here, second, grads, back, gate_w, up_w)


def split_cores(here, value, own, other):
    first = here[1] == 0
    own[0] = jnp.where(first, value[0:128], value[128:256])
    other[0] = jnp.where(first, value[128:256], value[0:128])


def by_chip(here, body, width, name, rows, whole, flops):
    out = pl.BlockSpec((1, 128, width), lambda m, here: (m, 0, 0))
    shape = jax.ShapeDtypeStruct((4, 128, width), bf16)
    lines = [
        pl.BlockSpec((256, a.shape[1]), lambda m, here: (lax.rem(here[0] + m, 4), 0)) for a in rows
    ]
    return pl.pallas_call(
        body,
        grid_spec=pltpu.PrefetchScalarGridSpec(
            num_scalar_prefetch=1,
            grid=(4,),
            in_specs=lines + [pl.BlockSpec(memory_space=pltpu.VMEM)] * len(whole),
            out_specs=(out, out),
        ),
        out_shape=(shape, shape),
        compiler_params=pltpu.CompilerParams(vmem_limit_bytes=56 * MIB),
        cost_estimate=pl.CostEstimate(flops=flops, bytes_accessed=100_000, transcendentals=0),
        name=name,
    )(here, *rows, *whole)


def back_body(here, gg, gu, routed, gate_w, up_w, own, other):
    total = mm_nt(gg[:, 0:512], gate_w[0]) + mm_nt(gg[:, 512:1024], gate_w[1])
    total = total + mm_nt(gu[:, 0:512], up_w[0]) + mm_nt(gu[:, 512:1024], up_w[1])
    table = routed[...]
    high = table.astype(bf16).astype(f32)
    low = pltpu.roll(table - high, 16, 1)
    lane = lax.broadcasted_iota(jnp.int32, table.shape, 1)
    tail = jnp.where(lane < 16, high, low)
    split_cores(here, jnp.concatenate([total, tail], axis=1).astype(bf16), own, other)


def experts_back(here, gg, gu, routed, gate_w, up_w):
    return by_chip(here, back_body, 1664, "experts_back", (gg, gu, routed), (gate_w, up_w), 10**6)


def combine_body(here, aw, down_w, own, other):
    total = mm(aw[:, 0:512], down_w[0]) + mm(aw[:, 512:1024], down_w[1])
    split_cores(here, total.astype(bf16), own, other)


def combine(here, aw, down_w):
    return by_chip(here, combine_body, 1536, "combine", (aw,), (down_w,), 8 * 10**9)


def back_rows_body(ids, *refs):
    blocks, (down_w, grads, back) = refs[:8], refs[8:]

    @pl.when(pl.program_id(0) == 0)
    def _():
        for b in range(8):
            grads[pl.ds(pl.multiple_of(ids[b] * 128, 128), 128), :] = blocks[b][...]

    back[...] = mm_nt(grads[...], down_w[0]).astype(bf16)


def back_rows(ids, blocks, down_w):
    vm = pl.BlockSpec(memory_space=pltpu.VMEM)
    shape = jax.ShapeDtypeStruct
    return pl.pallas_call(
        back_rows_body,
        grid=(2,),
        out_shape=(shape((1024, 1536), bf16), shape((1024, 1024), bf16)),
        in_specs=[pl.BlockSpec(memory_space=pltpu.SMEM)]
        + [vm] * 8
        + [pl.BlockSpec((1, 512, 1536), lambda e: (e, 0, 0))],
        out_specs=(vm, pl.BlockSpec((1024, 512), lambda e: (0, e))),
        compiler_params=pltpu.CompilerParams(vmem_limit_bytes=56 * MIB),
        cost_estimate=pl.CostEstimate(flops=8_000_000_000, bytes_accessed=11_000_000, transcendentals=0),
        name="back_rows",
    )(ids, *blocks, down_w)


def weight_body(normed, grad_qkv, mixed, branch, gain_a, gain_b, router, out):
    first = mm(normed[...].T, grad_qkv[...])
    out[:, 0:256] = first[:, 0:256].astype(bf16)
    lane = lax.broadcasted_iota(jnp.int32, (256, 128), 1)
    rest = jnp.where((lane >= 66) & (lane < 82), pltpu.roll(router[...], 66, 1), first[:, 256:384])
    rest = jnp.where(lane == 64, column(gain_a[...]), rest)
    rest = jnp.where(lane == 65, column(gain_b[...]), rest)
    out[:, 256:384] = rest.astype(bf16)
    cols = jnp.concatenate([branch[b, :, 256:512] for b in range(8)], axis=0)
    out[:, 384:640] = mm(mixed[...].T, cols).astype(bf16)


def weight_grads(normed, grad_qkv, mixed, branch, gain_a, gain_b, router):
    vm = pl.BlockSpec(memory_space=pltpu.VMEM)
    slab = pl.BlockSpec((1024, 256), lambda i: (0, i))
    flat = pl.BlockSpec((1, 256), lambda i: (0, i))
    return pl.pallas_call(
        weight_body,
        grid=(6,),
        out_shape=jax.ShapeDtypeStruct((1536, 640), bf16),
        in_specs=[slab, vm, slab, vm, flat, flat, pl.BlockSpec((256, 128), lambda i: (i, 0))],
        out_specs=pl.BlockSpec((256, 640), lambda i: (i, 0)),
        compiler_params=pltpu.CompilerParams(vmem_limit_bytes=56 * MIB),
        cost_estimate=pl.CostEstimate(flops=1_000_000, bytes_accessed=100_000, transcendentals=0),
        name="weight_grads",
    )(normed, grad_qkv, mixed, branch, gain_a, gain_b, router)


def assemble_body(blocks, query, key, value, out, rest):
    total = jnp.zeros((96, 128), f32)
    for p in range(4):
        a, b = blocks[2 * p].astype(f32), blocks[2 * p + 1].astype(f32)
        total = total + a[:, 256:384] + b[:, 256:384]
        wide, slim = slice(384 * p, 384 * (p + 1)), slice(128 * p, 128 * (p + 1))
        query[:, wide] = jnp.concatenate([a[:, 0:192], b[:, 0:192]], axis=1)
        key[:, slim] = jnp.concatenate([a[:, 192:256], b[:, 192:256]], axis=1)
        value[:, slim] = jnp.concatenate([a[:, 256:320], b[:, 256:320]], axis=1)
        out[:, wide] = jnp.concatenate([a[:, 384:576], b[:, 384:576]], axis=1)
    rest[...] = total


def assemble(blocks):
    vm = pl.BlockSpec(memory_space=pltpu.VMEM)
    shape = jax.ShapeDtypeStruct
    return pl.pallas_call(
        assemble_body,
        out_shape=(
            shape((96, 1536), f32),
            shape((96, 512), f32),
            shape((96, 512), f32),
            shape((96, 1536), f32),
            shape((96, 128), f32),
        ),
        in_specs=[vm],
        out_specs=(vm,) * 5,
        cost_estimate=pl.CostEstimate(flops=1_000_000, bytes_accessed=100_000, transcendentals=0),
        name="assemble",
    )(blocks)


def column(row):
    n = row.shape[1]
    down = lax.broadcasted_iota(jnp.int32, (n, n), 0)
    along = lax.broadcasted_iota(jnp.int32, (n, n), 1)
    return jnp.sum(jnp.where(down == along, row.astype(f32), 0.0), axis=1, keepdims=True)


def pack_body(at, w_query, w_key, w_value, gain_a, gain_b, router, tokens, seg, w_out, share, sent, half):
    first = at[1] == 0
    x = at[0]
    wide = w_query[:, pl.ds(pl.multiple_of(x * 384, 128), 384)].astype(f32)
    slim = pl.ds(pl.multiple_of(x * 128, 128), 128)
    key, value = w_key[:, slim].astype(f32), w_value[:, slim].astype(f32)
    columns = jnp.concatenate(
        [
            jnp.where(first, wide[:, 0:192], wide[:, 192:384]),
            jnp.where(first, key[:, 0:64], key[:, 64:128]),
            jnp.where(first, value[:, 0:64], value[:, 64:128]),
            column(gain_a[...]),
            column(gain_b[...]),
            router[...].astype(f32),
            jnp.zeros((96, 46), f32),
        ],
        axis=1,
    ).astype(bf16)
    for i in range(16):
        share[i] = columns
    sent[:, 0:1536] = tokens[...]
    sent[:, 1536:1664] = jnp.broadcast_to(column(seg[...]), (128, 128)).astype(bf16)
    half[...] = w_out[:, pl.ds(pl.multiple_of(at[1] * 768, 128), 768)]


def pack(at, w_query, w_key, w_value, gain_a, gain_b, router, tokens, seg, w_out):
    vm = pl.BlockSpec(memory_space=pltpu.VMEM)
    shape = jax.ShapeDtypeStruct
    return pl.pallas_call(
        pack_body,
        out_shape=(shape((16, 96, 384), bf16), shape((128, 1664), bf16), shape((96, 768), bf16)),
        in_specs=[pl.BlockSpec(memory_space=pltpu.SMEM)] + [vm] * 9,
        out_specs=(vm,) * 3,
        cost_estimate=pl.CostEstimate(flops=1_000_000, bytes_accessed=2_000_000, transcendentals=0),
        name="pack",
    )(at, w_query, w_key, w_value, gain_a, gain_b, router, tokens, seg, w_out)


def project_out_body(at, mixed, *refs):
    (near, far, tokens, gain, router, named, sent, hidden, gates, mx, hid) = refs
    core = at[1]
    for p in range(4):
        mx[:, 384 * p : 384 * (p + 1)] = jnp.concatenate(
            [mixed[2 * p, :, 0:192], mixed[2 * p + 1, :, 0:192]], axis=1
        )
    own, other = mm(mx[...], near[...]), mm(mx[...], far[...])
    hid[:, pl.ds(pl.multiple_of(core * 768, 128), 768)] = own
    hid[:, pl.ds(pl.multiple_of((1 - core) * 768, 128), 768)] = other
    value = tokens[...].astype(f32) + residual_scale * hid[...]
    hidden[...] = value
    r = lax.rsqrt(jnp.mean(value * value, axis=1, keepdims=True) + eps)
    second = (value * r * gain[...]).astype(bf16)
    sent[:, 0:1536] = second
    logits = mm(second, router[...])
    on = named[...] > 0.5
    logits = jnp.where(on, logits, -1e30)
    top = jnp.max(logits, axis=1, keepdims=True)
    e = jnp.where(on, jnp.exp(logits - top), 0.0)
    g = e / jnp.sum(e, axis=1, keepdims=True)
    gates[...] = g
    high = g.astype(bf16)
    low = pltpu.roll(g - high.astype(f32), 16, 1)
    lane = lax.broadcasted_iota(jnp.int32, g.shape, 1)
    sent[:, 1536:1664] = jnp.where(lane < 16, g, low).astype(bf16)


def project_out(at, mixed, near, far, tokens, gain, router, named):
    vm = pl.BlockSpec(memory_space=pltpu.VMEM)
    shape = jax.ShapeDtypeStruct
    return pl.pallas_call(
        project_out_body,
        out_shape=(
            shape((128, 1664), bf16),
            shape((128, 1536), f32),
            shape((128, 128), f32),
            shape((128, 1536), bf16),
        ),
        in_specs=[pl.BlockSpec(memory_space=pltpu.SMEM)] + [vm] * 7,
        out_specs=(vm,) * 4,
        scratch_shapes=[pltpu.VMEM((128, 1536), f32)],
        compiler_params=pltpu.CompilerParams(vmem_limit_bytes=56 * MIB),
        cost_estimate=pl.CostEstimate(flops=4_000_000_000, bytes_accessed=8_000_000, transcendentals=0),
        name="project_out",
    )(at, mixed, near, far, tokens, gain, router, named)


def middle_body(at, *refs):
    near, far, sums = refs[0], refs[1], refs[2:6]
    (grads, hidden, gates, gain, router, grad_hidden, heads, grad_gain, grad_router, gb, gx) = refs[6:]
    core = at[1]
    total = sums[0][...]
    for other in sums[1:]:
        total = total + other[...].astype(f32)
    value = hidden[...]
    r = lax.rsqrt(jnp.mean(value * value, axis=1, keepdims=True) + eps)
    second = (value * r * gain[...]).astype(bf16)
    g = gates[...]
    table = total[:, 1536:1664]
    lane = lax.broadcasted_iota(jnp.int32, g.shape, 1)
    table = jnp.where(lane < 16, table + pltpu.roll(table, 112, 1), 0.0)
    logits = (g * (table - jnp.sum(g * table, axis=1, keepdims=True))).astype(bf16)
    grad_router[...] = mm(second.T, logits)
    grad_second = total[:, 0:1536] + mm_nt(logits, router[...])
    grad_gain[...] = jnp.sum(grad_second * value * r, axis=0, keepdims=True)
    scaled = grad_second * gain[...]
    gh = (
        grads[...].astype(f32)
        + r * scaled
        - value * (r * r * r) * jnp.mean(value * scaled, axis=1, keepdims=True)
    )
    grad_hidden[...] = gh
    low = (residual_scale * gh).astype(bf16)
    gb[...] = low
    mine = gb[:, pl.ds(pl.multiple_of(core * 768, 128), 768)]
    twin = gb[:, pl.ds(pl.multiple_of((1 - core) * 768, 128), 768)]
    gx[...] = mm_nt(mine, near[...]) + mm_nt(twin, far[...])
    zero = jnp.zeros((128, 64), f32)
    low = low.astype(f32)
    for j in range(8):
        cols = slice(192 * j, 192 * (j + 1))
        heads[j] = jnp.concatenate(
            [gx[:, cols], zero, low[:, cols], zero], axis=1
        ).astype(bf16)


def middle(at, near, far, sums, grads, hidden, gates, gain, router):
    vm = pl.BlockSpec(memory_space=pltpu.VMEM)
    shape = jax.ShapeDtypeStruct
    return pl.pallas_call(
        middle_body,
        out_shape=(
            shape((128, 1536), f32),
            shape((8, 128, 512), bf16),
            shape((1, 1536), f32),
            shape((1536, 128), f32),
        ),
        in_specs=[pl.BlockSpec(memory_space=pltpu.SMEM)] + [vm] * 11,
        out_specs=(vm,) * 4,
        scratch_shapes=[pltpu.VMEM((128, 1536), bf16), pltpu.VMEM((128, 1536), f32)],
        compiler_params=pltpu.CompilerParams(vmem_limit_bytes=56 * MIB),
        cost_estimate=pl.CostEstimate(flops=1_000_000, bytes_accessed=100_000, transcendentals=0),
        name="middle",
    )(at, near, far, *sums, grads, hidden, gates, gain, router)


def shift(value, axis, amount):
    size = lax.axis_size(axis)
    return lax.ppermute(value, axis, [((i + amount) % size, i) for i in range(size)])


def swap(value):
    return lax.ppermute(value, "core", [(0, 1), (1, 0)])


def tied(*values):
    return lax.optimization_barrier(values)


def gather_x(block):
    return [block] + [shift(block, "x", m) for m in (1, 2, 3)]


def both_cores(blocks):
    return [each for block in blocks for each in (block, swap(block))]


def scatter_core(own, other):
    near = own.astype(f32) + swap(other).astype(f32)
    return near[0], [near[m].astype(bf16) for m in range(4)]


def scatter_x(first, low):
    return [first] + [shift(low[m], "x", -m) for m in (2, 1, 3)]


def total_of(terms):
    total = terms[0]
    for term in terms[1:]:
        total = total + term.astype(f32)
    return total


def inverse_rms(values):
    return lax.rsqrt(jnp.mean(values * values, axis=-1, keepdims=True) + eps)


def per_device(
    tokens,
    segments,
    routes,
    gain_attn,
    w_query,
    w_key,
    w_value,
    w_out,
    gain_moe,
    w_router,
    expert_gate,
    expert_up,
    expert_down,
    out_grad,
):
    rows, width = tokens.shape
    parts = 8
    seq = rows * parts
    x, core = lax.axis_index("x"), lax.axis_index("core")
    me = x * 2 + core
    z = lax.axis_index("z")
    at = jnp.stack([x, core, z])

    share, sent, half = pack(
        at,
        w_query,
        w_key,
        w_value,
        gain_attn[None, :],
        gain_moe[None, :],
        w_router,
        tokens,
        segments[None, :],
        w_out,
    )
    out_near = lax.all_gather(half, ("z", "y"), axis=0, tiled=True)
    qkv_w = lax.all_to_all(share, ("z", "y"), 0, 0, tiled=True).reshape(width, 384)
    far = gather_x(sent)
    far[1], grads_sent = tied(far[1], out_grad)
    blocks = both_cores(far)
    grads_far = gather_x(grads_sent)
    extra = qkv_w[:, 256:384]
    gain_one = extra[:, 64].astype(f32)[None, :]
    gain_two = extra[:, 65].astype(f32)[None, :]
    lane = jnp.arange(128, dtype=jnp.int32)
    router_w = jnp.where(lane[None, :] < 16, jnp.roll(extra, -66, axis=1), 0)

    chips = (x + jnp.arange(4, dtype=jnp.int32)) % 4
    cores = jnp.bitwise_xor(core, jnp.arange(2, dtype=jnp.int32))
    ids = (chips[:, None] * 2 + cores[None, :]).reshape(parts)
    place = jnp.arange(seq, dtype=jnp.int32)
    freq = rope_base ** (
        -(jnp.arange(128, dtype=jnp.int32) % 32).astype(f32) * 2.0 / HEAD_DIM
    )[None, :]
    angles = place.astype(f32)[:, None] * freq

    named = jnp.any(routes[:, :, None] == lane[None, None, :], axis=1).astype(f32)

    normed, q01, q2k, val, lse, cos, sin, starts, mixed_head = attend_forward(
        ids, blocks, qkv_w, gain_one, jnp.cos(angles), jnp.sin(angles), freq, (named, router_w)
    )
    lse, out_near, *grads_far = tied(lse, out_near, *grads_far)
    out_far = swap(out_near)
    grad_blocks = both_cores(grads_far)
    mixed = lax.all_to_all(mixed_head, ("x", "core"), 0, 0, tiled=True)
    sent_two, hidden, gates, mixed = project_out(
        at, mixed, out_near, out_far, tokens, gain_two, router_w, named
    )
    second_all = lax.all_gather(sent_two, ("x", "core"), axis=0, tiled=True)
    grad_all, back = back_rows(ids, grad_blocks, expert_down)
    mixed, back = tied(mixed, back)
    mixed_all = lax.all_gather(mixed, ("x", "core"), axis=0, tiled=True)

    grad_w_gate, grad_w_up, grad_w_down, weighted, grad_gate_pre, grad_up_pre, routed = experts(
        at, second_all, grad_all, back, expert_gate, expert_up
    )
    sums = lax.psum((grad_w_gate, grad_w_up, grad_w_down), ("z", "y"))
    own, other = experts_back(at, grad_gate_pre, grad_up_pre, routed, expert_gate, expert_up)
    terms = scatter_x(*scatter_core(own, other))
    grad_hidden, heads, grad_gain_two, grad_router = middle(
        at, out_near, out_far, terms, out_grad, hidden, gates, gain_two, router_w
    )
    grad_router, weighted = tied(grad_router, weighted)
    own_out, other_out = combine(at, weighted, expert_down)
    grad_heads = lax.all_to_all(heads, ("x", "core"), 0, 0, tiled=True)
    first_out, low_out = scatter_core(own_out, other_out)
    output = (hidden + residual_scale * total_of(scatter_x(first_out, low_out))).astype(bf16)
    grad_qkv, own, other, grad_gain_one = attend_backward(
        at, grad_heads, q01, q2k, val, lse, cos, sin, starts, normed, qkv_w, gain_one
    )
    first, low = scatter_core(own, other)
    normed_terms = scatter_x(first, low)
    inputs = tokens.astype(f32)
    normed_mine = total_of(normed_terms)
    scale_one = inverse_rms(inputs)
    scaled_one = normed_mine * gain_one
    grad_inputs = (
        grad_hidden
        + scale_one * scaled_one
        - inputs * scale_one**3 * jnp.mean(inputs * scaled_one, axis=-1, keepdims=True)
    )

    table = weight_grads(
        normed, grad_qkv, mixed_all, grad_heads, grad_gain_one, grad_gain_two, grad_router
    ).reshape(16, width // 16, 640)
    pieces = lax.all_to_all(table, ("z", "y"), 0, 0, tiled=True)
    summed = jnp.sum(pieces.astype(f32), axis=0).astype(bf16)
    lines = jnp.broadcast_to(summed[None], (parts,) + summed.shape)
    lines = lax.all_to_all(lines, ("x", "core"), 0, 0, tiled=True)
    grad_q, grad_k, grad_v, grad_o, rest = assemble(lines)
    return (
        output,
        grad_inputs,
        rest[:, 64],
        grad_q,
        grad_k,
        grad_v,
        grad_o,
        rest[:, 65],
        rest[:, 66:82],
        sums[0].astype(f32),
        sums[1].astype(f32),
        sums[2].astype(f32),
    )


def solution(mesh):
    fine = Mesh(mesh.devices.reshape(4, 4, 4, 2), ("z", "y", "x", "core"))
    dp, expert, both = ("z", "y"), ("x", "core"), ("z", "y", "x", "core")
    placed = (
        P(both, None),
        P(both),
        P(both, None),
        P(dp),
        P(dp, None),
        P(dp, None),
        P(dp, None),
        P(dp, None),
        P(dp),
        P(dp, None),
        P(expert, None, None),
        P(expert, None, None),
        P(expert, None, None),
    )
    return jax.shard_map(
        per_device,
        mesh=fine,
        in_specs=placed + (P(both, None),),
        out_specs=(P(both, None),) * 2 + placed[3:],
        check_vma=False,
    )
```

```python
import jax
import jax.numpy as jnp
from jax import lax
from jax.experimental import pallas as pl
from jax.experimental.pallas import tpu as pltpu
from jax.sharding import Mesh, PartitionSpec as P

HEADS = 24
KV_HEADS = 8
HEAD_DIM = 64
GROUP = HEADS // KV_HEADS
TOP = 8
EXPERTS = 16

eps = 1e-06
residual_scale = 0.22
score_scale = 0.015625
rope_base = 10000.0
doc_slots = 3
MIB = 1024 * 1024

bf16 = jnp.bfloat16
f32 = jnp.float32


def mm(a, b):
    return lax.dot_general(a, b, (((1,), (0,)), ((), ())), preferred_element_type=f32)


def mm_nt(a, b):
    return lax.dot_general(a, b, (((1,), (1,)), ((), ())), preferred_element_type=f32)


def low_half(value):
    lane = lax.broadcasted_iota(jnp.int32, value.shape, 1)
    return jnp.where(lane < 64, value, jnp.zeros_like(value))


def high_half(value):
    lane = lax.broadcasted_iota(jnp.int32, value.shape, 1)
    return jnp.where(lane >= 64, value, jnp.zeros_like(value))


def quarter(value):
    lane = lax.broadcasted_iota(jnp.int32, value.shape, 1)
    up, down = pltpu.roll(value, 96, 1), pltpu.roll(value, 32, 1)
    return jnp.where(lane % 64 < 32, -up, down)


def visible(chunk, starts):
    keys = 256 * (chunk + 1)
    place = (256 * chunk + lax.broadcasted_iota(jnp.int32, (1, 256), 1)).astype(f32)
    one = jnp.concatenate([starts[0:1], starts[0:1]], axis=1)
    two = jnp.concatenate([starts[1:2], starts[1:2]], axis=1)
    begin = jnp.where(place >= two, two, jnp.where(place >= one, one, jnp.zeros_like(one)))
    at = lax.broadcasted_iota(jnp.int32, (keys, 256), 0).astype(f32)
    return (at <= place) & (at >= begin)


def attend_body(ids, *refs):
    blocks = refs[:8]
    (w, cos_t, sin_t, freq, _, normed, narrow, q01, q2k, val, lse, cos_o, sin_o, starts, mixed, ka, kb, vt) = refs[8:]
    one = jnp.zeros((1, 128), f32)
    two = jnp.zeros((1, 128), f32)
    for b in range(8):
        seg = blocks[b][:, 1536:1664].astype(f32)
        one = one + jnp.sum(jnp.where(seg < 0.5, 1.0, 0.0), axis=0, keepdims=True)
        two = two + jnp.sum(jnp.where(seg < 1.5, 1.0, 0.0), axis=0, keepdims=True)
    starts[...] = jnp.concatenate([one, two, jnp.zeros((6, 128), f32)], axis=0)
    begin_rows = jnp.concatenate([one, two, jnp.zeros((6, 128), f32)], axis=0)
    angles = begin_rows * freq[...]
    cos_b, sin_b = jnp.cos(angles), jnp.sin(angles)
    narrow[...] = w[:, 256:384].astype(f32).T
    gain = narrow[64:65, :]
    for b in range(8):
        x = blocks[b][:, 0:1536].astype(f32)
        r = lax.rsqrt(jnp.mean(x * x, axis=1, keepdims=True) + eps)
        at = pl.ds(pl.multiple_of(ids[b] * 128, 128), 128)
        normed[at, :] = (x * r * gain).astype(bf16)
    def project(c, carry):
        at = pl.ds(pl.multiple_of(c * 256, 256), 256)
        u = mm(normed[at, :], w[...])
        place = (lax.broadcasted_iota(jnp.int32, (256, 128), 0) + c * 256).astype(f32)
        in_two, in_one = place >= two, place >= one
        cb = jnp.where(in_two, cos_b[1:2], jnp.where(in_one, cos_b[0:1], 1.0))
        sb = jnp.where(in_two, sin_b[1:2], jnp.where(in_one, sin_b[0:1], 0.0))
        ct, st = cos_t[at, :], sin_t[at, :]
        cc = ct * cb + st * sb
        ss = st * cb - ct * sb
        cos_o[at, :] = cc
        sin_o[at, :] = ss
        a, bq, v = u[:, 0:128], u[:, 128:256], u[:, 256:384]
        a = a * cc + quarter(a) * ss
        bq = bq * cc + quarter(bq) * ss
        v = low_half(v)
        q01[at, :] = a.astype(bf16)
        q2k[at, :] = bq.astype(bf16)
        val[at, :] = v.astype(bf16)
        k = high_half(bq) * score_scale
        kb[at, :] = k.astype(bf16)
        ka[at, :] = pltpu.roll(k, 64, 1).astype(bf16)
        vt[:, at] = v.T.astype(bf16)
        return carry

    lax.fori_loop(0, 4, project, 0)

    for c in range(4):
        at, seen = slice(256 * c, 256 * (c + 1)), slice(0, 256 * (c + 1))
        allowed = visible(c, starts)
        outs = []
        for h in range(3):
            q = q2k[at, :] if h == 2 else q01[at, :]
            kk = kb if h == 1 else ka
            s = mm_nt(kk[seen, :], q)
            s = jnp.where(allowed, s, -1e30)
            top = jnp.max(s, axis=0, keepdims=True)
            p = jnp.exp(s - top)
            total = jnp.sum(p, axis=0, keepdims=True)
            lse[h : h + 1, at] = top + jnp.log(total)
            pb = (p * (1.0 / total)).astype(bf16)
            outs.append(mm(vt[0:64, seen], pb))
        out = jnp.concatenate(outs + [jnp.zeros((64, 256), f32)], axis=0).T.astype(bf16)
        mixed[2 * c] = out[0:128]
        mixed[2 * c + 1] = out[128:256]


def attend_forward(ids, blocks, w, cos_t, sin_t, freq, held):
    vm = pl.BlockSpec(memory_space=pltpu.VMEM)
    shape = jax.ShapeDtypeStruct
    return pl.pallas_call(
        attend_body,
        out_shape=(
            shape((1024, 1536), bf16),
            shape((128, 1536), f32),
            shape((1024, 128), bf16),
            shape((1024, 128), bf16),
            shape((1024, 128), bf16),
            shape((8, 1024), f32),
            shape((1024, 128), f32),
            shape((1024, 128), f32),
            shape((8, 128), f32),
            shape((8, 128, 256), bf16),
        ),
        in_specs=[pl.BlockSpec(memory_space=pltpu.SMEM)]
        + [vm] * 12
        + [pl.BlockSpec(memory_space=pl.ANY)],
        out_specs=(vm,) * 10,
        scratch_shapes=[
            pltpu.VMEM((1024, 128), bf16),
            pltpu.VMEM((1024, 128), bf16),
            pltpu.VMEM((128, 1024), bf16),
        ],
        compiler_params=pltpu.CompilerParams(vmem_limit_bytes=56 * MIB),
        cost_estimate=pl.CostEstimate(flops=14_000_000_000, bytes_accessed=12_000_000, transcendentals=3_200_000),
        name="attend_forward",
    )(ids, *blocks, w, cos_t, sin_t, freq, held)


def attend_back_body(
    here, w, gm, q01, q2k, val, lse, cc, ss, starts, normed, narrow,
    dqkv, own, other, grad_gain, ka, kb, vb, kt, do01, do2, dk, dv, d01, dq2,
):
    k = high_half(q2k[...].astype(f32)) * score_scale
    kb[...] = k.astype(bf16)
    k_low = pltpu.roll(k, 64, 1)
    ka[...] = k_low.astype(bf16)
    kt[...] = k_low.T.astype(bf16)
    vb[...] = pltpu.roll(val[...].astype(f32), 64, 1).astype(bf16)
    for b in range(8):
        do01[b * 128 : (b + 1) * 128, :] = gm[b, :, 0:128]
        do2[b * 128 : (b + 1) * 128, :] = gm[b, :, 128:256]
    dk[...] = jnp.zeros_like(dk)
    dv[...] = jnp.zeros_like(dv)

    for c in range(4):
        at, seen = slice(256 * c, 256 * (c + 1)), slice(0, 256 * (c + 1))
        allowed = visible(c, starts)
        qa, qb = q01[at, :], q2k[at, :]
        da, db = do01[at, :], do2[at, :]
        outs = []
        for h in range(3):
            q = qb if h == 2 else qa
            kk = kb if h == 1 else ka
            s = mm_nt(kk[seen, :], q)
            p = jnp.where(allowed, jnp.exp(s - lse[h : h + 1, at]), 0.0)
            d = db if h == 2 else da
            vv = vb if h == 1 else val
            dp = mm_nt(vv[seen, :], d)
            delta = jnp.sum(p * dp, axis=0, keepdims=True)
            ds = (p * (dp - delta)).astype(bf16)
            outs.append(mm(kt[0:64, seen], ds))
            half = high_half if h == 1 else low_half
            dk[seen, :] += mm(ds, half(q))
            dv[seen, :] += mm(p.astype(bf16), half(d))
        out = jnp.concatenate(outs + [jnp.zeros((64, 256), f32)], axis=0).T
        d01[at, :] = out[:, 0:128]
        dq2[at, :] = out[:, 128:256]

    def finish(c, total):
        at = pl.ds(pl.multiple_of(c * 256, 256), 256)
        dkk = dk[at, :]
        dkk = (dkk + pltpu.roll(dkk, 64, 1)) * score_scale
        dvv = dv[at, :]
        dvv = low_half(dvv + pltpu.roll(dvv, 64, 1))
        a = d01[at, :]
        lane = lax.broadcasted_iota(jnp.int32, (256, 128), 1)
        b = jnp.where(lane < 64, dq2[at, :], dkk)
        cos, sin = cc[at, :], ss[at, :]
        a = a * cos - quarter(a) * sin
        b = b * cos - quarter(b) * sin
        row = jnp.concatenate([a, b, dvv], axis=1).astype(bf16)
        dqkv[at, :] = row
        whole = mm_nt(row, w[...])
        total = total + jnp.sum(whole * normed[at, :].astype(f32), axis=0, keepdims=True)
        low = whole.astype(bf16)
        own[c] = jnp.where(here[1] == 0, low[0:128], low[128:256])
        other[c] = jnp.where(here[1] == 0, low[128:256], low[0:128])
        return total

    total = lax.fori_loop(0, 4, finish, jnp.zeros((1, 1536), f32))
    grad_gain[...] = total / narrow[64:65, :]


def attend_backward(here, gm, q01, q2k, val, lse, cc, ss, starts, normed, w, narrow):
    vm = pl.BlockSpec(memory_space=pltpu.VMEM)
    shape = jax.ShapeDtypeStruct
    half = pltpu.VMEM((1024, 128), bf16)
    full = pltpu.VMEM((1024, 128), f32)
    return pl.pallas_call(
        attend_back_body,
        out_shape=(
            shape((1024, 384), bf16),
            shape((4, 128, 1536), bf16),
            shape((4, 128, 1536), bf16),
            shape((1, 1536), f32),
        ),
        in_specs=[pl.BlockSpec(memory_space=pltpu.SMEM)] + [vm] * 11,
        out_specs=(vm,) * 4,
        scratch_shapes=[
            half, half, half, pltpu.VMEM((128, 1024), bf16), half, half, full, full, full, full,
        ],
        compiler_params=pltpu.CompilerParams(vmem_limit_bytes=56 * MIB),
        cost_estimate=pl.CostEstimate(flops=1_000_000, bytes_accessed=100_000, transcendentals=0),
        name="attend_backward",
    )(here, w, gm, q01, q2k, val, lse, cc, ss, starts, normed, narrow)


def experts_body(ids, *refs):
    blocks = refs[:8]
    (grads, back, gate_w, up_w, d_gate, d_up, d_down, aw, gg, gu, routed, second, st, col) = refs[8:]
    e, c = pl.program_id(0), pl.program_id(1)
    first = (e == 0) & (c == 0)

    @pl.when(first)
    def _():
        for b in range(8):
            second[pl.ds(pl.multiple_of(ids[b] * 128, 128), 128), :] = blocks[b][...]
        for b in range(8):
            at = slice(128 * b, 128 * (b + 1))
            st[:, at] = second[at, 0:1536].T
        routed[...] = jnp.zeros_like(routed)

    @pl.when(c == 0)
    def _():
        lane = lax.broadcasted_iota(jnp.int32, (128, 128), 1)
        name = 2 * ids[0] + e
        hit = (lane == name) | (lane == name + 16)
        for b in range(8):
            at = slice(128 * b, 128 * (b + 1))
            table = second[at, 1536:1664].astype(f32)
            w = jnp.sum(jnp.where(hit, table, 0.0), axis=1, keepdims=True)
            col[at, :] = jnp.broadcast_to(w, (128, 128))

    x = second[:, 0:1536]
    gated = mm(x, gate_w[0])
    upper = mm(x, up_w[0])
    h = back[...].astype(f32)
    w = jnp.concatenate([col[...]] * 2, axis=1)
    sig = 1.0 / (1.0 + jnp.exp(-gated))
    silu = gated * sig
    act = silu * upper
    aw[...] = (act * w).astype(bf16)
    dots = residual_scale * jnp.sum(act * h, axis=1, keepdims=True)
    lane = lax.broadcasted_iota(jnp.int32, (1024, 128), 1)
    routed[...] += jnp.where(lane == 2 * ids[0] + e, dots, 0.0)
    ga = h * (w * residual_scale)
    gg[...] = (ga * upper * (sig * (1.0 + gated * (1.0 - sig)))).astype(bf16)
    gu[...] = (ga * silu).astype(bf16)

    d_gate[0] = mm(st[...], gg[...]).astype(bf16)
    d_up[0] = mm(st[...], gu[...]).astype(bf16)
    d_down[0] = (mm(aw[...].T, grads[...]) * residual_scale).astype(bf16)


def experts(ids, blocks, grads, back, gate_w, up_w):
    vm = pl.BlockSpec(memory_space=pltpu.VMEM)
    shape = jax.ShapeDtypeStruct
    wide = pl.BlockSpec((1, 1536, 256), lambda e, c: (e, 0, c))
    tall = pl.BlockSpec((1, 256, 1536), lambda e, c: (e, c, 0))
    line = pl.BlockSpec((1024, 256), lambda e, c: (0, 2 * e + c))
    return pl.pallas_call(
        experts_body,
        grid=(2, 2),
        out_shape=(
            shape((2, 1536, 512), bf16),
            shape((2, 1536, 512), bf16),
            shape((2, 512, 1536), bf16),
            shape((1024, 1024), bf16),
            shape((1024, 1024), bf16),
            shape((1024, 1024), bf16),
            shape((1024, 128), f32),
        ),
        in_specs=[pl.BlockSpec(memory_space=pltpu.SMEM)] + [vm] * 9 + [line, wide, wide],
        out_specs=(wide, wide, tall, line, line, line, vm),
        scratch_shapes=[
            pltpu.VMEM((1024, 1664), bf16),
            pltpu.VMEM((1536, 1024), bf16),
            pltpu.VMEM((1024, 128), f32),
        ],
        compiler_params=pltpu.CompilerParams(vmem_limit_bytes=60 * MIB),
        cost_estimate=pl.CostEstimate(flops=16_000_000_000, bytes_accessed=34_000_000, transcendentals=1_000_000),
        name="experts",
    )(ids, *blocks, grads, back, gate_w, up_w)


def split_cores(here, value, own, other):
    first = here[1] == 0
    own[0] = jnp.where(first, value[0:128], value[128:256])
    other[0] = jnp.where(first, value[128:256], value[0:128])


def by_chip(here, body, width, name, rows, whole, held, flops):
    out = pl.BlockSpec((1, 128, width), lambda m, here: (m, 0, 0))
    shape = jax.ShapeDtypeStruct((4, 128, width), bf16)
    lines = [
        pl.BlockSpec((256, a.shape[1]), lambda m, here: (m, 0)) for a in rows
    ]
    return pl.pallas_call(
        body,
        grid_spec=pltpu.PrefetchScalarGridSpec(
            num_scalar_prefetch=1,
            grid=(4,),
            in_specs=lines
            + [pl.BlockSpec(memory_space=pltpu.VMEM)] * len(whole)
            + [pl.BlockSpec(memory_space=pl.ANY)] * len(held),
            out_specs=(out, out),
        ),
        out_shape=(shape, shape),
        compiler_params=pltpu.CompilerParams(vmem_limit_bytes=56 * MIB),
        cost_estimate=pl.CostEstimate(flops=flops, bytes_accessed=100_000, transcendentals=0),
        name=name,
    )(here, *rows, *whole, *held)


def back_body(here, gg, gu, routed, gate_w, up_w, *refs):
    own, other = refs[-2:]
    total = mm_nt(gg[:, 0:512], gate_w[0]) + mm_nt(gg[:, 512:1024], gate_w[1])
    total = total + mm_nt(gu[:, 0:512], up_w[0]) + mm_nt(gu[:, 512:1024], up_w[1])
    table = routed[...]
    high = table.astype(bf16).astype(f32)
    low = pltpu.roll(table - high, 16, 1)
    lane = lax.broadcasted_iota(jnp.int32, table.shape, 1)
    tail = jnp.where(lane < 16, high, low)
    split_cores(here, jnp.concatenate([total, tail], axis=1).astype(bf16), own, other)


def experts_back(here, gg, gu, routed, gate_w, up_w, held):
    rows, whole = (gg, gu, routed), (gate_w, up_w)
    return by_chip(here, back_body, 1664, "experts_back", rows, whole, held, 10**6)


def combine_body(here, aw, down_w, own, other):
    total = mm(aw[:, 0:512], down_w[0]) + mm(aw[:, 512:1024], down_w[1])
    split_cores(here, total.astype(bf16), own, other)


def combine(here, aw, down_w):
    return by_chip(here, combine_body, 1536, "combine", (aw,), (down_w,), (), 8 * 10**9)


def widen_body(a, b, c, x, y, z):
    x[...] = a[...].astype(f32)
    y[...] = b[...].astype(f32)
    z[...] = c[...].astype(f32)


def widen(a, b, c):
    wide = pl.BlockSpec((1, 384, 512), lambda e, i: (e, i, 0))
    tall = pl.BlockSpec((1, 128, 1536), lambda e, i: (e, i, 0))
    return pl.pallas_call(
        widen_body,
        grid=(2, 4),
        out_shape=tuple(jax.ShapeDtypeStruct(v.shape, f32) for v in (a, b, c)),
        in_specs=[wide, wide, tall],
        out_specs=(wide, wide, tall),
        compiler_params=pltpu.CompilerParams(vmem_limit_bytes=56 * MIB),
        cost_estimate=pl.CostEstimate(flops=1_000_000, bytes_accessed=28_000_000, transcendentals=0),
        name="widen",
    )(a, b, c)


def back_rows_body(ids, *refs):
    blocks, (down_w, grads, back) = refs[:8], refs[8:]

    @pl.when(pl.program_id(0) == 0)
    def _():
        for b in range(8):
            grads[pl.ds(pl.multiple_of(ids[b] * 128, 128), 128), :] = blocks[b][...]

    back[...] = mm_nt(grads[...], down_w[0]).astype(bf16)


def back_rows(ids, blocks, down_w):
    vm = pl.BlockSpec(memory_space=pltpu.VMEM)
    shape = jax.ShapeDtypeStruct
    return pl.pallas_call(
        back_rows_body,
        grid=(2,),
        out_shape=(shape((1024, 1536), bf16), shape((1024, 1024), bf16)),
        in_specs=[pl.BlockSpec(memory_space=pltpu.SMEM)]
        + [vm] * 8
        + [pl.BlockSpec((1, 512, 1536), lambda e: (e, 0, 0))],
        out_specs=(vm, pl.BlockSpec((1024, 512), lambda e: (0, e))),
        compiler_params=pltpu.CompilerParams(vmem_limit_bytes=56 * MIB),
        cost_estimate=pl.CostEstimate(flops=8_000_000_000, bytes_accessed=11_000_000, transcendentals=0),
        name="back_rows",
    )(ids, *blocks, down_w)


def weight_body(normed, grad_qkv, mixed, branch, gain_a, gain_b, router, out):
    first = mm(normed[...].T, grad_qkv[...])
    cols = jnp.concatenate([branch[b, :, 256:512] for b in range(8)], axis=0)
    second = mm(mixed[...].T, cols)
    last = jnp.concatenate([first[:, 256:320], second[:, 0:192]], axis=1)
    zero = jnp.zeros((1, 32), f32)
    for y in range(4):
        rows, lanes = slice(96 * y, 96 * (y + 1)), slice(96 * y, 96 * (y + 1))
        gains = jnp.concatenate(
            [gain_a[:, lanes], zero, gain_b[:, lanes], zero], axis=1
        )
        small = jnp.concatenate([router[:, lanes], jnp.zeros((16, 160), f32)], axis=1)
        row = lax.broadcasted_iota(jnp.int32, (16, 256), 0)
        extra = jnp.where(row == 0, jnp.broadcast_to(gains, (16, 256)), 0.0)
        out[y, 0:96, 0:256] = first[rows, 0:256].astype(bf16)
        out[y, 96:112, 0:256] = small.astype(bf16)
        out[y, 0:96, 256:512] = last[rows].astype(bf16)
        out[y, 96:112, 256:512] = extra.astype(bf16)


def weight_grads(normed, grad_qkv, mixed, branch, gain_a, gain_b, router):
    vm = pl.BlockSpec(memory_space=pltpu.VMEM)
    slab = pl.BlockSpec((1024, 384), lambda i: (0, i))
    flat = pl.BlockSpec((1, 384), lambda i: (0, i))
    return pl.pallas_call(
        weight_body,
        grid=(4,),
        out_shape=jax.ShapeDtypeStruct((16, 112, 512), bf16),
        in_specs=[slab, vm, slab, vm, flat, flat, pl.BlockSpec((16, 384), lambda i: (0, i))],
        out_specs=pl.BlockSpec((4, 112, 512), lambda i: (i, 0, 0)),
        compiler_params=pltpu.CompilerParams(vmem_limit_bytes=56 * MIB),
        cost_estimate=pl.CostEstimate(flops=1_000_000, bytes_accessed=100_000, transcendentals=0),
        name="weight_grads",
    )(normed, grad_qkv, mixed, branch, gain_a, gain_b, router)


def sum_body(pieces, out):
    total = pieces[0].astype(f32)
    for i in range(1, pieces.shape[0]):
        total = total + pieces[i].astype(f32)
    out[...] = total.astype(bf16)


def sum_pieces(pieces):
    vm = pl.BlockSpec(memory_space=pltpu.VMEM)
    return pl.pallas_call(
        sum_body,
        out_shape=jax.ShapeDtypeStruct(pieces.shape[1:], bf16),
        in_specs=[vm],
        out_specs=vm,
        cost_estimate=pl.CostEstimate(flops=1_000_000, bytes_accessed=100_000, transcendentals=0),
        name="sum_pieces",
    )(pieces)


def assemble_body(ids, *refs):
    blocks, (query, key, value, out, gain_a, gain_b, router) = refs[:8], refs[8:]
    total = jnp.zeros((16, 512), f32)
    for m in range(4):
        here, there = blocks[2 * m][...].astype(f32), blocks[2 * m + 1][...].astype(f32)
        total = total + here[96:112] + there[96:112]
        first = ids[2 * m] < ids[2 * m + 1]
        a, b = jnp.where(first, here, there)[0:96], jnp.where(first, there, here)[0:96]
        chip = ids[2 * m] // 2
        wide = pl.ds(pl.multiple_of(chip * 384, 128), 384)
        slim = pl.ds(pl.multiple_of(chip * 128, 128), 128)
        query[:, wide] = jnp.concatenate([a[:, 0:192], b[:, 0:192]], axis=1)
        key[:, slim] = jnp.concatenate([a[:, 192:256], b[:, 192:256]], axis=1)
        value[:, slim] = jnp.concatenate([a[:, 256:320], b[:, 256:320]], axis=1)
        out[:, wide] = jnp.concatenate([a[:, 320:512], b[:, 320:512]], axis=1)
    router[...] = total[:, 0:96]
    gain_a[...] = total[0:1, 256:352]
    gain_b[...] = total[0:1, 384:480]


def assemble(ids, blocks):
    vm = pl.BlockSpec(memory_space=pltpu.VMEM)
    shape = jax.ShapeDtypeStruct
    return pl.pallas_call(
        assemble_body,
        out_shape=(
            shape((96, 1536), f32),
            shape((96, 512), f32),
            shape((96, 512), f32),
            shape((96, 1536), f32),
            shape((1, 96), f32),
            shape((1, 96), f32),
            shape((16, 96), f32),
        ),
        in_specs=[pl.BlockSpec(memory_space=pltpu.SMEM)] + [vm] * 8,
        out_specs=(vm,) * 7,
        cost_estimate=pl.CostEstimate(flops=1_000_000, bytes_accessed=100_000, transcendentals=0),
        name="assemble",
    )(ids, *blocks)


def column(row):
    n = row.shape[1]
    down = lax.broadcasted_iota(jnp.int32, (n, n), 0)
    along = lax.broadcasted_iota(jnp.int32, (n, n), 1)
    return jnp.sum(jnp.where(down == along, row.astype(f32), 0.0), axis=1, keepdims=True)


def pack_body(
    at, w_query, w_key, w_value, gain_a, gain_b, router, tokens, seg, share, sent
):
    first = at[1] == 0
    x = at[0]
    wide = w_query[:, pl.ds(pl.multiple_of(x * 384, 128), 384)].astype(f32)
    slim = pl.ds(pl.multiple_of(x * 128, 128), 128)
    key, value = w_key[:, slim].astype(f32), w_value[:, slim].astype(f32)
    columns = jnp.concatenate(
        [
            jnp.where(first, wide[:, 0:192], wide[:, 192:384]),
            jnp.where(first, key[:, 0:64], key[:, 64:128]),
            jnp.where(first, value[:, 0:64], value[:, 64:128]),
            column(gain_a[...]),
            column(gain_b[...]),
            router[...].astype(f32).T,
            jnp.zeros((96, 46), f32),
        ],
        axis=1,
    ).astype(bf16)
    for i in range(16):
        share[i] = columns
    sent[:, 0:1536] = tokens[...]
    sent[:, 1536:1664] = jnp.broadcast_to(column(seg[...]), (128, 128)).astype(bf16)


def pack(at, w_query, w_key, w_value, gain_a, gain_b, router, tokens, seg):
    vm = pl.BlockSpec(memory_space=pltpu.VMEM)
    shape = jax.ShapeDtypeStruct
    return pl.pallas_call(
        pack_body,
        out_shape=(shape((16, 96, 384), bf16), shape((128, 1664), bf16)),
        in_specs=[pl.BlockSpec(memory_space=pltpu.SMEM)] + [vm] * 8,
        out_specs=(vm,) * 2,
        cost_estimate=pl.CostEstimate(flops=1_000_000, bytes_accessed=2_000_000, transcendentals=0),
        name="pack",
    )(at, w_query, w_key, w_value, gain_a, gain_b, router, tokens, seg)


def project_out_body(mixed, w_out, tokens, narrow, named, sent, hidden, gates, mx):
    for p in range(4):
        mx[:, 384 * p : 384 * (p + 1)] = jnp.concatenate(
            [mixed[2 * p, :, 0:192], mixed[2 * p + 1, :, 0:192]], axis=1
        )
    value = tokens[...].astype(f32) + residual_scale * mm(mx[...], w_out[...])
    hidden[...] = value
    r = lax.rsqrt(jnp.mean(value * value, axis=1, keepdims=True) + eps)
    second = (value * r * narrow[65:66, :]).astype(bf16)
    sent[:, 0:1536] = second
    logits = pltpu.roll(mm_nt(second, narrow[...].astype(bf16)), 62, 1)
    on = named[...] > 0.5
    logits = jnp.where(on, logits, -1e30)
    top = jnp.max(logits, axis=1, keepdims=True)
    e = jnp.where(on, jnp.exp(logits - top), 0.0)
    g = e / jnp.sum(e, axis=1, keepdims=True)
    gates[...] = g
    high = g.astype(bf16)
    low = pltpu.roll(g - high.astype(f32), 16, 1)
    lane = lax.broadcasted_iota(jnp.int32, g.shape, 1)
    sent[:, 1536:1664] = jnp.where(lane < 16, g, low).astype(bf16)


def project_out(mixed, w_out, tokens, narrow, named):
    vm = pl.BlockSpec(memory_space=pltpu.VMEM)
    shape = jax.ShapeDtypeStruct
    return pl.pallas_call(
        project_out_body,
        out_shape=(
            shape((128, 1664), bf16),
            shape((128, 1536), f32),
            shape((128, 128), f32),
            shape((128, 1536), bf16),
        ),
        in_specs=[vm] * 5,
        out_specs=(vm,) * 4,
        compiler_params=pltpu.CompilerParams(vmem_limit_bytes=56 * MIB),
        cost_estimate=pl.CostEstimate(flops=4_000_000_000, bytes_accessed=8_000_000, transcendentals=0),
        name="project_out",
    )(mixed, w_out, tokens, narrow, named)


def middle_body(
    w_out, sums, grads, hidden, gates, narrow, _, grad_hidden, heads, grad_gain, grad_router, gx
):
    gain = narrow[65:66, :]
    total = sums[0].astype(f32)
    for i in range(1, 4):
        total = total + sums[i].astype(f32)
    value = hidden[...]
    r = lax.rsqrt(jnp.mean(value * value, axis=1, keepdims=True) + eps)
    second = (value * r * gain).astype(bf16)
    g = gates[...]
    table = total[:, 1536:1664]
    lane = lax.broadcasted_iota(jnp.int32, g.shape, 1)
    table = jnp.where(lane < 16, table + pltpu.roll(table, 112, 1), 0.0)
    logits = (g * (table - jnp.sum(g * table, axis=1, keepdims=True))).astype(bf16)
    grad_router[...] = mm(logits.astype(f32).T.astype(bf16), second)[0:16]
    router = pltpu.roll(logits.astype(f32), 66, 1).astype(bf16)
    grad_second = total[:, 0:1536] + mm(router, narrow[...].astype(bf16))
    grad_gain[...] = jnp.sum(grad_second * value * r, axis=0, keepdims=True)
    scaled = grad_second * gain
    gh = (
        grads[...].astype(f32)
        + r * scaled
        - value * (r * r * r) * jnp.mean(value * scaled, axis=1, keepdims=True)
    )
    grad_hidden[...] = gh
    low = (residual_scale * gh).astype(bf16)
    gx[...] = mm_nt(low, w_out[...])
    zero = jnp.zeros((128, 64), f32)
    low = low.astype(f32)
    for j in range(8):
        cols = slice(192 * j, 192 * (j + 1))
        heads[j] = jnp.concatenate([gx[:, cols], zero, low[:, cols], zero], axis=1).astype(bf16)


def middle(w_out, sums, grads, hidden, gates, narrow, held):
    vm = pl.BlockSpec(memory_space=pltpu.VMEM)
    shape = jax.ShapeDtypeStruct
    return pl.pallas_call(
        middle_body,
        out_shape=(
            shape((128, 1536), f32),
            shape((8, 128, 512), bf16),
            shape((1, 1536), f32),
            shape((16, 1536), f32),
        ),
        in_specs=[vm] * 6 + [pl.BlockSpec(memory_space=pl.ANY)],
        out_specs=(vm,) * 4,
        scratch_shapes=[pltpu.VMEM((128, 1536), f32)],
        compiler_params=pltpu.CompilerParams(vmem_limit_bytes=56 * MIB),
        cost_estimate=pl.CostEstimate(flops=1_000_000, bytes_accessed=100_000, transcendentals=0),
        name="middle",
    )(w_out, sums, grads, hidden, gates, narrow, held)


def shift(value, axis, amount):
    size = lax.axis_size(axis)
    return lax.ppermute(value, axis, [((i + amount) % size, i) for i in range(size)])


def swap(value):
    return lax.ppermute(value, "core", [(0, 1), (1, 0)])


def tied(*values):
    return lax.optimization_barrier(values)


def gather_x(block):
    return [block] + [shift(block, "x", m) for m in (1, 2, 3)]


def both_cores(blocks):
    return [each for block in blocks for each in (block, swap(block))]


def near_sum(own, other):
    return (own.astype(f32) + swap(other).astype(f32)).astype(bf16)


def exchange(near):
    return lax.all_to_all(near, "x", 0, 0, tiled=True)


def exchange_apart(near):
    x = lax.axis_index("x")
    pieces = [lax.dynamic_index_in_dim(near, (x + m) % 4, 0, False) for m in range(4)]
    return [pieces[0]] + [shift(pieces[m], "x", -m) for m in (2, 1, 3)]


def total_of(terms):
    total = terms[0].astype(f32)
    for term in terms[1:]:
        total = total + term.astype(f32)
    return total


def inverse_rms(values):
    return lax.rsqrt(jnp.mean(values * values, axis=-1, keepdims=True) + eps)


def per_device(
    tokens,
    segments,
    routes,
    gain_attn,
    w_query,
    w_key,
    w_value,
    w_out,
    gain_moe,
    w_router,
    expert_gate,
    expert_up,
    expert_down,
    out_grad,
):
    rows, width = tokens.shape
    parts = 8
    seq = rows * parts
    x, core = lax.axis_index("x"), lax.axis_index("core")
    me = x * 2 + core
    z = lax.axis_index("z")
    at = jnp.stack([x, core, z])

    share, sent = pack(
        at,
        w_query,
        w_key,
        w_value,
        gain_attn[None, :],
        gain_moe[None, :],
        w_router.T,
        tokens,
        segments[None, :],
    )
    out_all = lax.all_gather(w_out, ("z", "y"), axis=0, tiled=True)
    qkv_w = lax.all_to_all(share, ("z", "y"), 0, 0, tiled=True).reshape(width, 384)
    far = gather_x(sent)
    far[1], grads_sent = tied(far[1], out_grad)
    blocks = both_cores(far)
    grads_far = gather_x(grads_sent)
    lane = jnp.arange(128, dtype=jnp.int32)

    chips = (x + jnp.arange(4, dtype=jnp.int32)) % 4
    cores = jnp.bitwise_xor(core, jnp.arange(2, dtype=jnp.int32))
    ids = (chips[:, None] * 2 + cores[None, :]).reshape(parts)
    place = jnp.arange(seq, dtype=jnp.int32)
    freq = rope_base ** (
        -(jnp.arange(128, dtype=jnp.int32) % 32).astype(f32) * 2.0 / HEAD_DIM
    )[None, :]
    angles = place.astype(f32)[:, None] * freq

    named = jnp.any(routes[:, :, None] == lane[None, None, :], axis=1).astype(f32)

    normed, narrow, q01, q2k, val, lse, cos, sin, starts, mixed_head = attend_forward(
        ids, blocks, qkv_w, jnp.cos(angles), jnp.sin(angles), freq, named
    )
    mixed_head, *grads_far = tied(mixed_head, *grads_far)
    grad_blocks = both_cores(grads_far)
    mixed = lax.all_to_all(mixed_head, ("x", "core"), 0, 0, tiled=True)
    sent_two, hidden, gates, mixed = project_out(
        mixed, out_all, tokens, narrow, named
    )
    far_two = gather_x(sent_two)
    grad_all, back = back_rows(ids, grad_blocks, expert_down)
    far_two[2], back = tied(far_two[2], back)
    mixed, *far_two = tied(mixed, *far_two)
    second_blocks = both_cores(far_two)
    mixed_all = lax.all_gather(mixed, ("x", "core"), axis=0, tiled=True)

    grad_w_gate, grad_w_up, grad_w_down, weighted, grad_gate_pre, grad_up_pre, routed = experts(
        ids, second_blocks, grad_all, back, expert_gate, expert_up
    )
    sums = lax.psum((grad_w_gate, grad_w_up, grad_w_down), ("z", "y"))
    own, other = experts_back(
        at, grad_gate_pre, grad_up_pre, routed, expert_gate, expert_up, ()
    )
    near = near_sum(own, other)
    near, weighted = tied(near, weighted)
    terms = exchange(near)
    own_out, other_out = combine(at, weighted, expert_down)

    grad_hidden, heads, grad_gain_two, grad_router = middle(
        out_all, terms, out_grad, hidden, gates, narrow, own_out
    )
    grad_heads = lax.all_to_all(heads, ("x", "core"), 0, 0, tiled=True)
    near_out = near_sum(own_out, other_out)
    grad_qkv, own, other, grad_gain_one = attend_backward(
        at, grad_heads, q01, q2k, val, lse, cos, sin, starts, normed, qkv_w, narrow
    )
    table = weight_grads(
        normed, grad_qkv, mixed_all, grad_heads, grad_gain_one, grad_gain_two, grad_router
    )
    near_out, table = tied(near_out, table)
    output = (hidden + residual_scale * total_of(exchange_apart(near_out))).astype(bf16)
    normed_mine = total_of(exchange_apart(near_sum(own, other)))
    inputs = tokens.astype(f32)
    scale_one = inverse_rms(inputs)
    scaled_one = normed_mine * narrow[64:65, :]
    grad_inputs = (
        grad_hidden
        + scale_one * scaled_one
        - inputs * scale_one**3 * jnp.mean(inputs * scaled_one, axis=-1, keepdims=True)
    )

    pieces = lax.all_to_all(table, ("z", "y"), 0, 0, tiled=True)
    pieces, output, grad_inputs = tied(pieces, output, grad_inputs)
    lines = both_cores(gather_x(sum_pieces(pieces)))
    grad_gate, grad_up, grad_down = widen(*sums)
    lines[0], grad_down = tied(lines[0], grad_down)
    grad_q, grad_k, grad_v, grad_o, gain_a, gain_b, router = assemble(ids, lines)
    return (
        output,
        grad_inputs,
        gain_a.reshape(-1),
        grad_q,
        grad_k,
        grad_v,
        grad_o,
        gain_b.reshape(-1),
        router.T,
        grad_gate,
        grad_up,
        grad_down,
    )


def solution(mesh):
    fine = Mesh(mesh.devices.reshape(4, 4, 4, 2), ("z", "y", "x", "core"))
    dp, expert, both = ("z", "y"), ("x", "core"), ("z", "y", "x", "core")
    placed = (
        P(both, None),
        P(both),
        P(both, None),
        P(dp),
        P(dp, None),
        P(dp, None),
        P(dp, None),
        P(dp, None),
        P(dp),
        P(dp, None),
        P(expert, None, None),
        P(expert, None, None),
        P(expert, None, None),
    )
    return jax.shard_map(
        per_device,
        mesh=fine,
        in_specs=placed + (P(both, None),),
        out_specs=(P(both, None),) * 2 + placed[3:],
        check_vma=False,
    )
```

```python
import jax
import jax.numpy as jnp
from jax import lax
from jax.experimental import pallas as pl
from jax.experimental.pallas import tpu as pltpu
from jax.sharding import Mesh, PartitionSpec as P

HEADS = 24
KV_HEADS = 8
HEAD_DIM = 64
GROUP = HEADS // KV_HEADS
TOP = 8
EXPERTS = 16

eps = 1e-06
residual_scale = 0.22
score_scale = 0.015625
rope_base = 10000.0
doc_slots = 3
MIB = 1024 * 1024

bf16 = jnp.bfloat16
f32 = jnp.float32


def mm(a, b):
    return lax.dot_general(a, b, (((1,), (0,)), ((), ())), preferred_element_type=f32)


def mm_nt(a, b):
    return lax.dot_general(a, b, (((1,), (1,)), ((), ())), preferred_element_type=f32)


def low_half(value):
    lane = lax.broadcasted_iota(jnp.int32, value.shape, 1)
    return jnp.where(lane < 64, value, jnp.zeros_like(value))


def high_half(value):
    lane = lax.broadcasted_iota(jnp.int32, value.shape, 1)
    return jnp.where(lane >= 64, value, jnp.zeros_like(value))


def quarter(value):
    lane = lax.broadcasted_iota(jnp.int32, value.shape, 1)
    up, down = pltpu.roll(value, 96, 1), pltpu.roll(value, 32, 1)
    return jnp.where(lane % 64 < 32, -up, down)


def visible(chunk, starts):
    keys = 256 * (chunk + 1)
    place = (256 * chunk + lax.broadcasted_iota(jnp.int32, (1, 256), 1)).astype(f32)
    one = jnp.concatenate([starts[0:1], starts[0:1]], axis=1)
    two = jnp.concatenate([starts[1:2], starts[1:2]], axis=1)
    begin = jnp.where(place >= two, two, jnp.where(place >= one, one, jnp.zeros_like(one)))
    at = lax.broadcasted_iota(jnp.int32, (keys, 256), 0).astype(f32)
    return (at <= place) & (at >= begin)


def attend_body(ids, *refs):
    blocks = refs[:8]
    (w, cos_t, sin_t, freq, _, normed, narrow, q01, q2k, val, lse, cos_o, sin_o, starts, mixed, ka, kb, vt) = refs[8:]
    one = jnp.zeros((1, 128), f32)
    two = jnp.zeros((1, 128), f32)
    for b in range(8):
        seg = blocks[b][:, 1536:1664].astype(f32)
        one = one + jnp.sum(jnp.where(seg < 0.5, 1.0, 0.0), axis=0, keepdims=True)
        two = two + jnp.sum(jnp.where(seg < 1.5, 1.0, 0.0), axis=0, keepdims=True)
    starts[...] = jnp.concatenate([one, two, jnp.zeros((6, 128), f32)], axis=0)
    begin_rows = jnp.concatenate([one, two, jnp.zeros((6, 128), f32)], axis=0)
    angles = begin_rows * freq[...]
    cos_b, sin_b = jnp.cos(angles), jnp.sin(angles)
    narrow[...] = w[:, 256:384].astype(f32).T
    gain = narrow[64:65, :]
    for b in range(8):
        x = blocks[b][:, 0:1536].astype(f32)
        r = lax.rsqrt(jnp.mean(x * x, axis=1, keepdims=True) + eps)
        at = pl.ds(pl.multiple_of(ids[b] * 128, 128), 128)
        normed[at, :] = (x * r * gain).astype(bf16)
    def project(c, carry):
        at = pl.ds(pl.multiple_of(c * 256, 256), 256)
        u = mm(normed[at, :], w[...])
        place = (lax.broadcasted_iota(jnp.int32, (256, 128), 0) + c * 256).astype(f32)
        in_two, in_one = place >= two, place >= one
        cb = jnp.where(in_two, cos_b[1:2], jnp.where(in_one, cos_b[0:1], 1.0))
        sb = jnp.where(in_two, sin_b[1:2], jnp.where(in_one, sin_b[0:1], 0.0))
        ct, st = cos_t[at, :], sin_t[at, :]
        cc = ct * cb + st * sb
        ss = st * cb - ct * sb
        cos_o[at, :] = cc
        sin_o[at, :] = ss
        a, bq, v = u[:, 0:128], u[:, 128:256], u[:, 256:384]
        a = a * cc + quarter(a) * ss
        bq = bq * cc + quarter(bq) * ss
        v = low_half(v)
        q01[at, :] = a.astype(bf16)
        q2k[at, :] = bq.astype(bf16)
        val[at, :] = v.astype(bf16)
        k = high_half(bq) * score_scale
        kb[at, :] = k.astype(bf16)
        ka[at, :] = pltpu.roll(k, 64, 1).astype(bf16)
        vt[:, at] = v.T.astype(bf16)
        return carry

    lax.fori_loop(0, 4, project, 0)

    for c in range(4):
        at, seen = slice(256 * c, 256 * (c + 1)), slice(0, 256 * (c + 1))
        allowed = visible(c, starts)
        outs = []
        for h in range(3):
            q = q2k[at, :] if h == 2 else q01[at, :]
            kk = kb if h == 1 else ka
            s = mm_nt(kk[seen, :], q)
            s = jnp.where(allowed, s, -1e30)
            top = jnp.max(s, axis=0, keepdims=True)
            p = jnp.exp(s - top)
            total = jnp.sum(p, axis=0, keepdims=True)
            lse[h : h + 1, at] = top + jnp.log(total)
            pb = (p * (1.0 / total)).astype(bf16)
            outs.append(mm(vt[0:64, seen], pb))
        out = jnp.concatenate(outs + [jnp.zeros((64, 256), f32)], axis=0).T.astype(bf16)
        mixed[2 * c] = out[0:128]
        mixed[2 * c + 1] = out[128:256]


def attend_forward(ids, blocks, w, cos_t, sin_t, freq, held):
    vm = pl.BlockSpec(memory_space=pltpu.VMEM)
    shape = jax.ShapeDtypeStruct
    return pl.pallas_call(
        attend_body,
        out_shape=(
            shape((1024, 1536), bf16),
            shape((128, 1536), f32),
            shape((1024, 128), bf16),
            shape((1024, 128), bf16),
            shape((1024, 128), bf16),
            shape((8, 1024), f32),
            shape((1024, 128), f32),
            shape((1024, 128), f32),
            shape((8, 128), f32),
            shape((8, 128, 256), bf16),
        ),
        in_specs=[pl.BlockSpec(memory_space=pltpu.SMEM)]
        + [vm] * 12
        + [pl.BlockSpec(memory_space=pl.ANY)],
        out_specs=(vm,) * 10,
        scratch_shapes=[
            pltpu.VMEM((1024, 128), bf16),
            pltpu.VMEM((1024, 128), bf16),
            pltpu.VMEM((128, 1024), bf16),
        ],
        compiler_params=pltpu.CompilerParams(vmem_limit_bytes=56 * MIB),
        cost_estimate=pl.CostEstimate(flops=14_000_000_000, bytes_accessed=12_000_000, transcendentals=3_200_000),
        name="attend_forward",
    )(ids, *blocks, w, cos_t, sin_t, freq, held)


def attend_back_body(
    here, w, gm, q01, q2k, val, lse, cc, ss, starts, normed, narrow,
    dqkv, own, other, grad_gain, ka, kb, vb, kt, do01, do2, dk, dv, d01, dq2,
):
    k = high_half(q2k[...].astype(f32)) * score_scale
    kb[...] = k.astype(bf16)
    k_low = pltpu.roll(k, 64, 1)
    ka[...] = k_low.astype(bf16)
    kt[...] = k_low.T.astype(bf16)
    vb[...] = pltpu.roll(val[...].astype(f32), 64, 1).astype(bf16)
    for b in range(8):
        do01[b * 128 : (b + 1) * 128, :] = gm[b, :, 0:128]
        do2[b * 128 : (b + 1) * 128, :] = gm[b, :, 128:256]
    dk[...] = jnp.zeros_like(dk)
    dv[...] = jnp.zeros_like(dv)

    for c in range(4):
        at, seen = slice(256 * c, 256 * (c + 1)), slice(0, 256 * (c + 1))
        allowed = visible(c, starts)
        qa, qb = q01[at, :], q2k[at, :]
        da, db = do01[at, :], do2[at, :]
        outs = []
        for h in range(3):
            q = qb if h == 2 else qa
            kk = kb if h == 1 else ka
            s = mm_nt(kk[seen, :], q)
            p = jnp.where(allowed, jnp.exp(s - lse[h : h + 1, at]), 0.0)
            d = db if h == 2 else da
            vv = vb if h == 1 else val
            dp = mm_nt(vv[seen, :], d)
            delta = jnp.sum(p * dp, axis=0, keepdims=True)
            ds = (p * (dp - delta)).astype(bf16)
            outs.append(mm(kt[0:64, seen], ds))
            half = high_half if h == 1 else low_half
            dk[seen, :] += mm(ds, half(q))
            dv[seen, :] += mm(p.astype(bf16), half(d))
        out = jnp.concatenate(outs + [jnp.zeros((64, 256), f32)], axis=0).T
        d01[at, :] = out[:, 0:128]
        dq2[at, :] = out[:, 128:256]

    def finish(c, total):
        at = pl.ds(pl.multiple_of(c * 256, 256), 256)
        dkk = dk[at, :]
        dkk = (dkk + pltpu.roll(dkk, 64, 1)) * score_scale
        dvv = dv[at, :]
        dvv = low_half(dvv + pltpu.roll(dvv, 64, 1))
        a = d01[at, :]
        lane = lax.broadcasted_iota(jnp.int32, (256, 128), 1)
        b = jnp.where(lane < 64, dq2[at, :], dkk)
        cos, sin = cc[at, :], ss[at, :]
        a = a * cos - quarter(a) * sin
        b = b * cos - quarter(b) * sin
        row = jnp.concatenate([a, b, dvv], axis=1).astype(bf16)
        dqkv[at, :] = row
        whole = mm_nt(row, w[...])
        total = total + jnp.sum(whole * normed[at, :].astype(f32), axis=0, keepdims=True)
        low = whole.astype(bf16)
        own[c] = jnp.where(here[1] == 0, low[0:128], low[128:256])
        other[c] = jnp.where(here[1] == 0, low[128:256], low[0:128])
        return total

    total = lax.fori_loop(0, 4, finish, jnp.zeros((1, 1536), f32))
    grad_gain[...] = total / narrow[64:65, :]


def attend_backward(here, gm, q01, q2k, val, lse, cc, ss, starts, normed, w, narrow):
    vm = pl.BlockSpec(memory_space=pltpu.VMEM)
    shape = jax.ShapeDtypeStruct
    half = pltpu.VMEM((1024, 128), bf16)
    full = pltpu.VMEM((1024, 128), f32)
    return pl.pallas_call(
        attend_back_body,
        out_shape=(
            shape((1024, 384), bf16),
            shape((4, 128, 1536), bf16),
            shape((4, 128, 1536), bf16),
            shape((1, 1536), f32),
        ),
        in_specs=[pl.BlockSpec(memory_space=pltpu.SMEM)] + [vm] * 11,
        out_specs=(vm,) * 4,
        scratch_shapes=[
            half, half, half, pltpu.VMEM((128, 1024), bf16), half, half, full, full, full, full,
        ],
        compiler_params=pltpu.CompilerParams(vmem_limit_bytes=56 * MIB),
        cost_estimate=pl.CostEstimate(flops=1_000_000, bytes_accessed=100_000, transcendentals=0),
        name="attend_backward",
    )(here, w, gm, q01, q2k, val, lse, cc, ss, starts, normed, narrow)


def experts_body(ids, *refs):
    blocks = refs[:8]
    (grads, back, gate_w, up_w, d_gate, d_up, d_down, aw, gg, gu, routed, second, st, col) = refs[8:]
    e, c = pl.program_id(0), pl.program_id(1)
    first = (e == 0) & (c == 0)

    @pl.when(first)
    def _():
        for b in range(8):
            second[pl.ds(pl.multiple_of(ids[b] * 128, 128), 128), :] = blocks[b][...]
        for b in range(8):
            at = slice(128 * b, 128 * (b + 1))
            st[:, at] = second[at, 0:1536].T
        routed[...] = jnp.zeros_like(routed)

    @pl.when(c == 0)
    def _():
        lane = lax.broadcasted_iota(jnp.int32, (128, 128), 1)
        name = 2 * ids[0] + e
        hit = (lane == name) | (lane == name + 16)
        for b in range(8):
            at = slice(128 * b, 128 * (b + 1))
            table = second[at, 1536:1664].astype(f32)
            w = jnp.sum(jnp.where(hit, table, 0.0), axis=1, keepdims=True)
            col[at, :] = jnp.broadcast_to(w, (128, 128))

    x = second[:, 0:1536]
    gated = mm(x, gate_w[0])
    upper = mm(x, up_w[0])
    h = back[...].astype(f32)
    w = jnp.concatenate([col[...]] * 2, axis=1)
    sig = 1.0 / (1.0 + jnp.exp(-gated))
    silu = gated * sig
    act = silu * upper
    aw[...] = (act * w).astype(bf16)
    dots = residual_scale * jnp.sum(act * h, axis=1, keepdims=True)
    lane = lax.broadcasted_iota(jnp.int32, (1024, 128), 1)
    routed[...] += jnp.where(lane == 2 * ids[0] + e, dots, 0.0)
    ga = h * (w * residual_scale)
    gg[...] = (ga * upper * (sig * (1.0 + gated * (1.0 - sig)))).astype(bf16)
    gu[...] = (ga * silu).astype(bf16)

    d_gate[0] = mm(st[...], gg[...]).astype(bf16)
    d_up[0] = mm(st[...], gu[...]).astype(bf16)
    d_down[0] = (mm(aw[...].T, grads[...]) * residual_scale).astype(bf16)


def experts(ids, blocks, grads, back, gate_w, up_w):
    vm = pl.BlockSpec(memory_space=pltpu.VMEM)
    shape = jax.ShapeDtypeStruct
    wide = pl.BlockSpec((1, 1536, 256), lambda e, c: (e, 0, c))
    tall = pl.BlockSpec((1, 256, 1536), lambda e, c: (e, c, 0))
    line = pl.BlockSpec((1024, 256), lambda e, c: (0, 2 * e + c))
    return pl.pallas_call(
        experts_body,
        grid=(2, 2),
        out_shape=(
            shape((2, 1536, 512), bf16),
            shape((2, 1536, 512), bf16),
            shape((2, 512, 1536), bf16),
            shape((1024, 1024), bf16),
            shape((1024, 1024), bf16),
            shape((1024, 1024), bf16),
            shape((1024, 128), f32),
        ),
        in_specs=[pl.BlockSpec(memory_space=pltpu.SMEM)] + [vm] * 9 + [line, wide, wide],
        out_specs=(wide, wide, tall, line, line, line, vm),
        scratch_shapes=[
            pltpu.VMEM((1024, 1664), bf16),
            pltpu.VMEM((1536, 1024), bf16),
            pltpu.VMEM((1024, 128), f32),
        ],
        compiler_params=pltpu.CompilerParams(vmem_limit_bytes=60 * MIB),
        cost_estimate=pl.CostEstimate(flops=16_000_000_000, bytes_accessed=34_000_000, transcendentals=1_000_000),
        name="experts",
    )(ids, *blocks, grads, back, gate_w, up_w)


def split_cores(here, value, own, other):
    first = here[1] == 0
    own[0] = jnp.where(first, value[0:128], value[128:256])
    other[0] = jnp.where(first, value[128:256], value[0:128])


def by_chip(here, body, width, name, rows, whole, held, flops):
    out = pl.BlockSpec((1, 128, width), lambda m, here: (m, 0, 0))
    shape = jax.ShapeDtypeStruct((4, 128, width), bf16)
    lines = [
        pl.BlockSpec((256, a.shape[1]), lambda m, here: (m, 0)) for a in rows
    ]
    return pl.pallas_call(
        body,
        grid_spec=pltpu.PrefetchScalarGridSpec(
            num_scalar_prefetch=1,
            grid=(4,),
            in_specs=lines
            + [pl.BlockSpec(memory_space=pltpu.VMEM)] * len(whole)
            + [pl.BlockSpec(memory_space=pl.ANY)] * len(held),
            out_specs=(out, out),
        ),
        out_shape=(shape, shape),
        compiler_params=pltpu.CompilerParams(vmem_limit_bytes=56 * MIB),
        cost_estimate=pl.CostEstimate(flops=flops, bytes_accessed=100_000, transcendentals=0),
        name=name,
    )(here, *rows, *whole, *held)


def back_body(here, gg, gu, routed, gate_w, up_w, *refs):
    own, other = refs[-2:]
    total = mm_nt(gg[:, 0:512], gate_w[0]) + mm_nt(gg[:, 512:1024], gate_w[1])
    total = total + mm_nt(gu[:, 0:512], up_w[0]) + mm_nt(gu[:, 512:1024], up_w[1])
    table = routed[...]
    high = table.astype(bf16).astype(f32)
    low = pltpu.roll(table - high, 16, 1)
    lane = lax.broadcasted_iota(jnp.int32, table.shape, 1)
    tail = jnp.where(lane < 16, high, low)
    split_cores(here, jnp.concatenate([total, tail], axis=1).astype(bf16), own, other)


def experts_back(here, gg, gu, routed, gate_w, up_w, held):
    rows, whole = (gg, gu, routed), (gate_w, up_w)
    return by_chip(here, back_body, 1664, "experts_back", rows, whole, held, 10**6)


def combine_body(here, aw, down_w, own, other):
    total = mm(aw[:, 0:512], down_w[0]) + mm(aw[:, 512:1024], down_w[1])
    split_cores(here, total.astype(bf16), own, other)


def combine(here, aw, down_w):
    return by_chip(here, combine_body, 1536, "combine", (aw,), (down_w,), (), 8 * 10**9)


def widen_body(a, b, c, x, y, z, *refs):
    held, grown, got, sent = refs[0:3], refs[3:6], refs[6], refs[7]
    work = []
    for k, (source, target) in enumerate(((a, x), (b, y), (c, z))):
        half = source.shape[1] // 2
        for e in range(2):
            for i in range(2):
                j = 2 * e + i
                at = pl.ds(half * i, half)
                load = pltpu.make_async_copy(
                    source.at[e, at], held[k].at[j], got.at[4 * k + j]
                )
                store = pltpu.make_async_copy(
                    grown[k].at[j], target.at[e, at], sent.at[4 * k + j]
                )
                load.start()
                work.append((k, j, load, store))
    for k, j, load, store in work:
        load.wait()
        grown[k][j] = held[k][j].astype(f32)
        store.start()
    for _, _, _, store in work:
        store.wait()


def widen(a, b, c):
    hbm = pl.BlockSpec(memory_space=pl.ANY)
    shapes = [(4, v.shape[1] // 2, v.shape[2]) for v in (a, b, c)]
    return pl.pallas_call(
        widen_body,
        out_shape=tuple(jax.ShapeDtypeStruct(v.shape, f32) for v in (a, b, c)),
        in_specs=[hbm] * 3,
        out_specs=(hbm,) * 3,
        scratch_shapes=[pltpu.VMEM(s, bf16) for s in shapes]
        + [pltpu.VMEM(s, f32) for s in shapes]
        + [pltpu.SemaphoreType.DMA((12,)), pltpu.SemaphoreType.DMA((12,))],
        compiler_params=pltpu.CompilerParams(vmem_limit_bytes=56 * MIB),
        cost_estimate=pl.CostEstimate(flops=1_000_000, bytes_accessed=28_000_000, transcendentals=0),
        name="widen",
    )(a, b, c)


def back_rows_body(ids, *refs):
    blocks, (down_w, grads, back) = refs[:8], refs[8:]

    @pl.when(pl.program_id(0) == 0)
    def _():
        for b in range(8):
            grads[pl.ds(pl.multiple_of(ids[b] * 128, 128), 128), :] = blocks[b][...]

    back[...] = mm_nt(grads[...], down_w[0]).astype(bf16)


def back_rows(ids, blocks, down_w):
    vm = pl.BlockSpec(memory_space=pltpu.VMEM)
    shape = jax.ShapeDtypeStruct
    return pl.pallas_call(
        back_rows_body,
        grid=(2,),
        out_shape=(shape((1024, 1536), bf16), shape((1024, 1024), bf16)),
        in_specs=[pl.BlockSpec(memory_space=pltpu.SMEM)]
        + [vm] * 8
        + [pl.BlockSpec((1, 512, 1536), lambda e: (e, 0, 0))],
        out_specs=(vm, pl.BlockSpec((1024, 512), lambda e: (0, e))),
        compiler_params=pltpu.CompilerParams(vmem_limit_bytes=56 * MIB),
        cost_estimate=pl.CostEstimate(flops=8_000_000_000, bytes_accessed=11_000_000, transcendentals=0),
        name="back_rows",
    )(ids, *blocks, down_w)


def weight_body(normed, grad_qkv, mixed, branch, gain_a, gain_b, router, out):
    first = mm(normed[...].T, grad_qkv[...])
    cols = jnp.concatenate([branch[b, :, 256:512] for b in range(8)], axis=0)
    second = mm(mixed[...].T, cols)
    last = jnp.concatenate([first[:, 256:320], second[:, 0:192]], axis=1)
    zero = jnp.zeros((1, 32), f32)
    for y in range(4):
        rows, lanes = slice(96 * y, 96 * (y + 1)), slice(96 * y, 96 * (y + 1))
        gains = jnp.concatenate(
            [gain_a[:, lanes], zero, gain_b[:, lanes], zero], axis=1
        )
        small = jnp.concatenate([router[:, lanes], jnp.zeros((16, 160), f32)], axis=1)
        row = lax.broadcasted_iota(jnp.int32, (16, 256), 0)
        extra = jnp.where(row == 0, jnp.broadcast_to(gains, (16, 256)), 0.0)
        out[y, 0:96, 0:256] = first[rows, 0:256].astype(bf16)
        out[y, 96:112, 0:256] = small.astype(bf16)
        out[y, 0:96, 256:512] = last[rows].astype(bf16)
        out[y, 96:112, 256:512] = extra.astype(bf16)


def weight_grads(normed, grad_qkv, mixed, branch, gain_a, gain_b, router):
    vm = pl.BlockSpec(memory_space=pltpu.VMEM)
    slab = pl.BlockSpec((1024, 384), lambda i: (0, i))
    flat = pl.BlockSpec((1, 384), lambda i: (0, i))
    return pl.pallas_call(
        weight_body,
        grid=(4,),
        out_shape=jax.ShapeDtypeStruct((16, 112, 512), bf16),
        in_specs=[slab, vm, slab, vm, flat, flat, pl.BlockSpec((16, 384), lambda i: (0, i))],
        out_specs=pl.BlockSpec((4, 112, 512), lambda i: (i, 0, 0)),
        compiler_params=pltpu.CompilerParams(vmem_limit_bytes=56 * MIB),
        cost_estimate=pl.CostEstimate(flops=1_000_000, bytes_accessed=100_000, transcendentals=0),
        name="weight_grads",
    )(normed, grad_qkv, mixed, branch, gain_a, gain_b, router)


def sum_body(pieces, out):
    total = pieces[0].astype(f32)
    for i in range(1, pieces.shape[0]):
        total = total + pieces[i].astype(f32)
    out[...] = total.astype(bf16)


def sum_pieces(pieces):
    vm = pl.BlockSpec(memory_space=pltpu.VMEM)
    return pl.pallas_call(
        sum_body,
        out_shape=jax.ShapeDtypeStruct(pieces.shape[1:], bf16),
        in_specs=[vm],
        out_specs=vm,
        cost_estimate=pl.CostEstimate(flops=1_000_000, bytes_accessed=100_000, transcendentals=0),
        name="sum_pieces",
    )(pieces)


def assemble_body(ids, *refs):
    blocks, (query, key, value, out, gain_a, gain_b, router) = refs[:8], refs[8:]
    total = jnp.zeros((16, 512), f32)
    for m in range(4):
        here, there = blocks[2 * m][...].astype(f32), blocks[2 * m + 1][...].astype(f32)
        total = total + here[96:112] + there[96:112]
        first = ids[2 * m] < ids[2 * m + 1]
        a, b = jnp.where(first, here, there)[0:96], jnp.where(first, there, here)[0:96]
        chip = ids[2 * m] // 2
        wide = pl.ds(pl.multiple_of(chip * 384, 128), 384)
        slim = pl.ds(pl.multiple_of(chip * 128, 128), 128)
        query[:, wide] = jnp.concatenate([a[:, 0:192], b[:, 0:192]], axis=1)
        key[:, slim] = jnp.concatenate([a[:, 192:256], b[:, 192:256]], axis=1)
        value[:, slim] = jnp.concatenate([a[:, 256:320], b[:, 256:320]], axis=1)
        out[:, wide] = jnp.concatenate([a[:, 320:512], b[:, 320:512]], axis=1)
    router[...] = total[:, 0:96]
    gain_a[...] = total[0:1, 256:352]
    gain_b[...] = total[0:1, 384:480]


def assemble(ids, blocks):
    vm = pl.BlockSpec(memory_space=pltpu.VMEM)
    shape = jax.ShapeDtypeStruct
    return pl.pallas_call(
        assemble_body,
        out_shape=(
            shape((96, 1536), f32),
            shape((96, 512), f32),
            shape((96, 512), f32),
            shape((96, 1536), f32),
            shape((1, 96), f32),
            shape((1, 96), f32),
            shape((16, 96), f32),
        ),
        in_specs=[pl.BlockSpec(memory_space=pltpu.SMEM)] + [vm] * 8,
        out_specs=(vm,) * 7,
        cost_estimate=pl.CostEstimate(flops=1_000_000, bytes_accessed=100_000, transcendentals=0),
        name="assemble",
    )(ids, *blocks)


def column(row):
    n = row.shape[1]
    down = lax.broadcasted_iota(jnp.int32, (n, n), 0)
    along = lax.broadcasted_iota(jnp.int32, (n, n), 1)
    return jnp.sum(jnp.where(down == along, row.astype(f32), 0.0), axis=1, keepdims=True)


def pack_body(
    at, w_query, w_key, w_value, gain_a, gain_b, router, tokens, seg, share, sent
):
    first = at[1] == 0
    x = at[0]
    wide = w_query[:, pl.ds(pl.multiple_of(x * 384, 128), 384)].astype(f32)
    slim = pl.ds(pl.multiple_of(x * 128, 128), 128)
    key, value = w_key[:, slim].astype(f32), w_value[:, slim].astype(f32)
    columns = jnp.concatenate(
        [
            jnp.where(first, wide[:, 0:192], wide[:, 192:384]),
            jnp.where(first, key[:, 0:64], key[:, 64:128]),
            jnp.where(first, value[:, 0:64], value[:, 64:128]),
            column(gain_a[...]),
            column(gain_b[...]),
            router[...].astype(f32).T,
            jnp.zeros((96, 46), f32),
        ],
        axis=1,
    ).astype(bf16)
    for i in range(16):
        share[i] = columns
    sent[:, 0:1536] = tokens[...]
    sent[:, 1536:1664] = jnp.broadcast_to(column(seg[...]), (128, 128)).astype(bf16)


def pack(at, w_query, w_key, w_value, gain_a, gain_b, router, tokens, seg):
    vm = pl.BlockSpec(memory_space=pltpu.VMEM)
    shape = jax.ShapeDtypeStruct
    return pl.pallas_call(
        pack_body,
        out_shape=(shape((16, 96, 384), bf16), shape((128, 1664), bf16)),
        in_specs=[pl.BlockSpec(memory_space=pltpu.SMEM)] + [vm] * 8,
        out_specs=(vm,) * 2,
        cost_estimate=pl.CostEstimate(flops=1_000_000, bytes_accessed=2_000_000, transcendentals=0),
        name="pack",
    )(at, w_query, w_key, w_value, gain_a, gain_b, router, tokens, seg)


def project_out_body(mixed, w_out, tokens, narrow, named, sent, hidden, gates, mx):
    for p in range(4):
        mx[:, 384 * p : 384 * (p + 1)] = jnp.concatenate(
            [mixed[2 * p, :, 0:192], mixed[2 * p + 1, :, 0:192]], axis=1
        )
    value = tokens[...].astype(f32) + residual_scale * mm(mx[...], w_out[...])
    hidden[...] = value
    r = lax.rsqrt(jnp.mean(value * value, axis=1, keepdims=True) + eps)
    second = (value * r * narrow[65:66, :]).astype(bf16)
    sent[:, 0:1536] = second
    logits = pltpu.roll(mm_nt(second, narrow[...].astype(bf16)), 62, 1)
    on = named[...] > 0.5
    logits = jnp.where(on, logits, -1e30)
    top = jnp.max(logits, axis=1, keepdims=True)
    e = jnp.where(on, jnp.exp(logits - top), 0.0)
    g = e / jnp.sum(e, axis=1, keepdims=True)
    gates[...] = g
    high = g.astype(bf16)
    low = pltpu.roll(g - high.astype(f32), 16, 1)
    lane = lax.broadcasted_iota(jnp.int32, g.shape, 1)
    sent[:, 1536:1664] = jnp.where(lane < 16, g, low).astype(bf16)


def project_out(mixed, w_out, tokens, narrow, named):
    vm = pl.BlockSpec(memory_space=pltpu.VMEM)
    shape = jax.ShapeDtypeStruct
    return pl.pallas_call(
        project_out_body,
        out_shape=(
            shape((128, 1664), bf16),
            shape((128, 1536), f32),
            shape((128, 128), f32),
            shape((128, 1536), bf16),
        ),
        in_specs=[vm] * 5,
        out_specs=(vm,) * 4,
        compiler_params=pltpu.CompilerParams(vmem_limit_bytes=56 * MIB),
        cost_estimate=pl.CostEstimate(flops=4_000_000_000, bytes_accessed=8_000_000, transcendentals=0),
        name="project_out",
    )(mixed, w_out, tokens, narrow, named)


def middle_body(
    w_out, sums, grads, hidden, gates, narrow, _, grad_hidden, heads, grad_gain, grad_router, gx
):
    gain = narrow[65:66, :]
    total = sums[0].astype(f32)
    for i in range(1, 4):
        total = total + sums[i].astype(f32)
    value = hidden[...]
    r = lax.rsqrt(jnp.mean(value * value, axis=1, keepdims=True) + eps)
    second = (value * r * gain).astype(bf16)
    g = gates[...]
    table = total[:, 1536:1664]
    lane = lax.broadcasted_iota(jnp.int32, g.shape, 1)
    table = jnp.where(lane < 16, table + pltpu.roll(table, 112, 1), 0.0)
    logits = (g * (table - jnp.sum(g * table, axis=1, keepdims=True))).astype(bf16)
    grad_router[...] = mm(logits.astype(f32).T.astype(bf16), second)[0:16]
    router = pltpu.roll(logits.astype(f32), 66, 1).astype(bf16)
    grad_second = total[:, 0:1536] + mm(router, narrow[...].astype(bf16))
    grad_gain[...] = jnp.sum(grad_second * value * r, axis=0, keepdims=True)
    scaled = grad_second * gain
    gh = (
        grads[...].astype(f32)
        + r * scaled
        - value * (r * r * r) * jnp.mean(value * scaled, axis=1, keepdims=True)
    )
    grad_hidden[...] = gh
    low = (residual_scale * gh).astype(bf16)
    gx[...] = mm_nt(low, w_out[...])
    zero = jnp.zeros((128, 64), f32)
    low = low.astype(f32)
    for j in range(8):
        cols = slice(192 * j, 192 * (j + 1))
        heads[j] = jnp.concatenate([gx[:, cols], zero, low[:, cols], zero], axis=1).astype(bf16)


def middle(w_out, sums, grads, hidden, gates, narrow, held):
    vm = pl.BlockSpec(memory_space=pltpu.VMEM)
    shape = jax.ShapeDtypeStruct
    return pl.pallas_call(
        middle_body,
        out_shape=(
            shape((128, 1536), f32),
            shape((8, 128, 512), bf16),
            shape((1, 1536), f32),
            shape((16, 1536), f32),
        ),
        in_specs=[vm] * 6 + [pl.BlockSpec(memory_space=pl.ANY)],
        out_specs=(vm,) * 4,
        scratch_shapes=[pltpu.VMEM((128, 1536), f32)],
        compiler_params=pltpu.CompilerParams(vmem_limit_bytes=56 * MIB),
        cost_estimate=pl.CostEstimate(flops=1_000_000, bytes_accessed=100_000, transcendentals=0),
        name="middle",
    )(w_out, sums, grads, hidden, gates, narrow, held)


def shift(value, axis, amount):
    size = lax.axis_size(axis)
    return lax.ppermute(value, axis, [((i + amount) % size, i) for i in range(size)])


def swap(value):
    return lax.ppermute(value, "core", [(0, 1), (1, 0)])


def tied(*values):
    return lax.optimization_barrier(values)


def gather_x(block):
    return [block] + [shift(block, "x", m) for m in (1, 2, 3)]


def both_cores(blocks):
    return [each for block in blocks for each in (block, swap(block))]


def near_sum(own, other):
    return (own.astype(f32) + swap(other).astype(f32)).astype(bf16)


def exchange(near):
    return lax.all_to_all(near, "x", 0, 0, tiled=True)


def exchange_apart(near):
    x = lax.axis_index("x")
    pieces = [lax.dynamic_index_in_dim(near, (x + m) % 4, 0, False) for m in range(4)]
    return [pieces[0]] + [shift(pieces[m], "x", -m) for m in (2, 1, 3)]


def total_of(terms):
    total = terms[0].astype(f32)
    for term in terms[1:]:
        total = total + term.astype(f32)
    return total


def inverse_rms(values):
    return lax.rsqrt(jnp.mean(values * values, axis=-1, keepdims=True) + eps)


def per_device(
    tokens,
    segments,
    routes,
    gain_attn,
    w_query,
    w_key,
    w_value,
    w_out,
    gain_moe,
    w_router,
    expert_gate,
    expert_up,
    expert_down,
    out_grad,
):
    rows, width = tokens.shape
    parts = 8
    seq = rows * parts
    x, core = lax.axis_index("x"), lax.axis_index("core")
    me = x * 2 + core
    z = lax.axis_index("z")
    at = jnp.stack([x, core, z])

    share, sent = pack(
        at,
        w_query,
        w_key,
        w_value,
        gain_attn[None, :],
        gain_moe[None, :],
        w_router.T,
        tokens,
        segments[None, :],
    )
    out_all = lax.all_gather(w_out, ("z", "y"), axis=0, tiled=True)
    qkv_w = lax.all_to_all(share, ("z", "y"), 0, 0, tiled=True).reshape(width, 384)
    far = gather_x(sent)
    far[1], grads_sent = tied(far[1], out_grad)
    blocks = both_cores(far)
    grads_far = gather_x(grads_sent)
    lane = jnp.arange(128, dtype=jnp.int32)

    chips = (x + jnp.arange(4, dtype=jnp.int32)) % 4
    cores = jnp.bitwise_xor(core, jnp.arange(2, dtype=jnp.int32))
    ids = (chips[:, None] * 2 + cores[None, :]).reshape(parts)
    place = jnp.arange(seq, dtype=jnp.int32)
    freq = rope_base ** (
        -(jnp.arange(128, dtype=jnp.int32) % 32).astype(f32) * 2.0 / HEAD_DIM
    )[None, :]
    angles = place.astype(f32)[:, None] * freq

    named = jnp.any(routes[:, :, None] == lane[None, None, :], axis=1).astype(f32)

    normed, narrow, q01, q2k, val, lse, cos, sin, starts, mixed_head = attend_forward(
        ids, blocks, qkv_w, jnp.cos(angles), jnp.sin(angles), freq, named
    )
    mixed_head, *grads_far = tied(mixed_head, *grads_far)
    grad_blocks = both_cores(grads_far)
    mixed = lax.all_to_all(mixed_head, ("x", "core"), 0, 0, tiled=True)
    sent_two, hidden, gates, mixed = project_out(
        mixed, out_all, tokens, narrow, named
    )
    far_two = gather_x(sent_two)
    grad_all, back = back_rows(ids, grad_blocks, expert_down)
    far_two[2], back = tied(far_two[2], back)
    mixed, *far_two = tied(mixed, *far_two)
    second_blocks = both_cores(far_two)
    mixed_all = lax.all_gather(mixed, ("x", "core"), axis=0, tiled=True)

    grad_w_gate, grad_w_up, grad_w_down, weighted, grad_gate_pre, grad_up_pre, routed = experts(
        ids, second_blocks, grad_all, back, expert_gate, expert_up
    )
    sums = lax.psum((grad_w_gate, grad_w_up, grad_w_down), ("z", "y"))
    own, other = experts_back(
        at, grad_gate_pre, grad_up_pre, routed, expert_gate, expert_up, ()
    )
    near = near_sum(own, other)
    near, weighted = tied(near, weighted)
    terms = exchange(near)
    own_out, other_out = combine(at, weighted, expert_down)

    grad_hidden, heads, grad_gain_two, grad_router = middle(
        out_all, terms, out_grad, hidden, gates, narrow, own_out
    )
    grad_heads = lax.all_to_all(heads, ("x", "core"), 0, 0, tiled=True)
    near_out = near_sum(own_out, other_out)
    grad_qkv, own, other, grad_gain_one = attend_backward(
        at, grad_heads, q01, q2k, val, lse, cos, sin, starts, normed, qkv_w, narrow
    )
    table = weight_grads(
        normed, grad_qkv, mixed_all, grad_heads, grad_gain_one, grad_gain_two, grad_router
    )
    near_out, table = tied(near_out, table)
    output = (hidden + residual_scale * total_of(exchange_apart(near_out))).astype(bf16)
    normed_mine = total_of(exchange_apart(near_sum(own, other)))
    inputs = tokens.astype(f32)
    scale_one = inverse_rms(inputs)
    scaled_one = normed_mine * narrow[64:65, :]
    grad_inputs = (
        grad_hidden
        + scale_one * scaled_one
        - inputs * scale_one**3 * jnp.mean(inputs * scaled_one, axis=-1, keepdims=True)
    )

    pieces = lax.all_to_all(table, ("z", "y"), 0, 0, tiled=True)
    pieces, output, grad_inputs = tied(pieces, output, grad_inputs)
    lines = both_cores(gather_x(sum_pieces(pieces)))
    grad_gate, grad_up, grad_down = widen(*sums)
    grad_q, grad_k, grad_v, grad_o, gain_a, gain_b, router = assemble(ids, lines)
    return (
        output,
        grad_inputs,
        gain_a.reshape(-1),
        grad_q,
        grad_k,
        grad_v,
        grad_o,
        gain_b.reshape(-1),
        router.T,
        grad_gate,
        grad_up,
        grad_down,
    )


def solution(mesh):
    fine = Mesh(mesh.devices.reshape(4, 4, 4, 2), ("z", "y", "x", "core"))
    dp, expert, both = ("z", "y"), ("x", "core"), ("z", "y", "x", "core")
    placed = (
        P(both, None),
        P(both),
        P(both, None),
        P(dp),
        P(dp, None),
        P(dp, None),
        P(dp, None),
        P(dp, None),
        P(dp),
        P(dp, None),
        P(expert, None, None),
        P(expert, None, None),
        P(expert, None, None),
    )
    return jax.shard_map(
        per_device,
        mesh=fine,
        in_specs=placed + (P(both, None),),
        out_specs=(P(both, None),) * 2 + placed[3:],
        check_vma=False,
    )
```

```python
import jax
import jax.numpy as jnp
from jax import lax
from jax.experimental import pallas as pl
from jax.experimental.pallas import tpu as pltpu
from jax.sharding import Mesh, PartitionSpec as P

HEADS = 24
KV_HEADS = 8
HEAD_DIM = 64
GROUP = HEADS // KV_HEADS
TOP = 8
EXPERTS = 16

eps = 1e-06
residual_scale = 0.22
score_scale = 0.015625
rope_base = 10000.0
doc_slots = 3
MIB = 1024 * 1024

bf16 = jnp.bfloat16
f32 = jnp.float32


def mm(a, b):
    return lax.dot_general(a, b, (((1,), (0,)), ((), ())), preferred_element_type=f32)


def mm_nt(a, b):
    return lax.dot_general(a, b, (((1,), (1,)), ((), ())), preferred_element_type=f32)


def low_half(value):
    lane = lax.broadcasted_iota(jnp.int32, value.shape, 1)
    return jnp.where(lane < 64, value, jnp.zeros_like(value))


def high_half(value):
    lane = lax.broadcasted_iota(jnp.int32, value.shape, 1)
    return jnp.where(lane >= 64, value, jnp.zeros_like(value))


def quarter(value):
    lane = lax.broadcasted_iota(jnp.int32, value.shape, 1)
    up, down = pltpu.roll(value, 96, 1), pltpu.roll(value, 32, 1)
    return jnp.where(lane % 64 < 32, -up, down)


def visible(chunk, starts):
    keys = 256 * (chunk + 1)
    place = (256 * chunk + lax.broadcasted_iota(jnp.int32, (1, 256), 1)).astype(f32)
    one = jnp.concatenate([starts[0:1], starts[0:1]], axis=1)
    two = jnp.concatenate([starts[1:2], starts[1:2]], axis=1)
    begin = jnp.where(place >= two, two, jnp.where(place >= one, one, jnp.zeros_like(one)))
    at = lax.broadcasted_iota(jnp.int32, (keys, 256), 0).astype(f32)
    return (at <= place) & (at >= begin)


def attend_body(ids, *refs):
    blocks = refs[:8]
    (w, cos_t, sin_t, freq, _, normed, narrow, q01, q2k, val, lse, cos_o, sin_o, starts, mixed, ka, kb, vt) = refs[8:]
    one = jnp.zeros((1, 128), f32)
    two = jnp.zeros((1, 128), f32)
    for b in range(8):
        seg = blocks[b][:, 1536:1664].astype(f32)
        one = one + jnp.sum(jnp.where(seg < 0.5, 1.0, 0.0), axis=0, keepdims=True)
        two = two + jnp.sum(jnp.where(seg < 1.5, 1.0, 0.0), axis=0, keepdims=True)
    starts[...] = jnp.concatenate([one, two, jnp.zeros((6, 128), f32)], axis=0)
    begin_rows = jnp.concatenate([one, two, jnp.zeros((6, 128), f32)], axis=0)
    angles = begin_rows * freq[...]
    cos_b, sin_b = jnp.cos(angles), jnp.sin(angles)
    narrow[...] = w[:, 256:384].astype(f32).T
    gain = narrow[64:65, :]
    for b in range(8):
        x = blocks[b][:, 0:1536].astype(f32)
        r = lax.rsqrt(jnp.mean(x * x, axis=1, keepdims=True) + eps)
        at = pl.ds(pl.multiple_of(ids[b] * 128, 128), 128)
        normed[at, :] = (x * r * gain).astype(bf16)
    def project(c, carry):
        at = pl.ds(pl.multiple_of(c * 256, 256), 256)
        u = mm(normed[at, :], w[...])
        place = (lax.broadcasted_iota(jnp.int32, (256, 128), 0) + c * 256).astype(f32)
        in_two, in_one = place >= two, place >= one
        cb = jnp.where(in_two, cos_b[1:2], jnp.where(in_one, cos_b[0:1], 1.0))
        sb = jnp.where(in_two, sin_b[1:2], jnp.where(in_one, sin_b[0:1], 0.0))
        ct, st = cos_t[at, :], sin_t[at, :]
        cc = ct * cb + st * sb
        ss = st * cb - ct * sb
        cos_o[at, :] = cc
        sin_o[at, :] = ss
        a, bq, v = u[:, 0:128], u[:, 128:256], u[:, 256:384]
        a = a * cc + quarter(a) * ss
        bq = bq * cc + quarter(bq) * ss
        v = low_half(v)
        q01[at, :] = a.astype(bf16)
        q2k[at, :] = bq.astype(bf16)
        val[at, :] = v.astype(bf16)
        k = high_half(bq) * score_scale
        kb[at, :] = k.astype(bf16)
        ka[at, :] = pltpu.roll(k, 64, 1).astype(bf16)
        vt[:, at] = v.T.astype(bf16)
        return carry

    lax.fori_loop(0, 4, project, 0)

    for c in range(4):
        at, seen = slice(256 * c, 256 * (c + 1)), slice(0, 256 * (c + 1))
        allowed = visible(c, starts)
        outs = []
        for h in range(3):
            q = q2k[at, :] if h == 2 else q01[at, :]
            kk = kb if h == 1 else ka
            s = mm_nt(kk[seen, :], q)
            s = jnp.where(allowed, s, -1e30)
            top = jnp.max(s, axis=0, keepdims=True)
            p = jnp.exp(s - top)
            total = jnp.sum(p, axis=0, keepdims=True)
            lse[h : h + 1, at] = top + jnp.log(total)
            pb = (p * (1.0 / total)).astype(bf16)
            outs.append(mm(vt[0:64, seen], pb))
        out = jnp.concatenate(outs + [jnp.zeros((64, 256), f32)], axis=0).T.astype(bf16)
        mixed[2 * c] = out[0:128]
        mixed[2 * c + 1] = out[128:256]


def attend_forward(ids, blocks, w, cos_t, sin_t, freq, held):
    vm = pl.BlockSpec(memory_space=pltpu.VMEM)
    shape = jax.ShapeDtypeStruct
    return pl.pallas_call(
        attend_body,
        out_shape=(
            shape((1024, 1536), bf16),
            shape((128, 1536), f32),
            shape((1024, 128), bf16),
            shape((1024, 128), bf16),
            shape((1024, 128), bf16),
            shape((8, 1024), f32),
            shape((1024, 128), f32),
            shape((1024, 128), f32),
            shape((8, 128), f32),
            shape((8, 128, 256), bf16),
        ),
        in_specs=[pl.BlockSpec(memory_space=pltpu.SMEM)]
        + [vm] * 12
        + [pl.BlockSpec(memory_space=pl.ANY)],
        out_specs=(vm,) * 10,
        scratch_shapes=[
            pltpu.VMEM((1024, 128), bf16),
            pltpu.VMEM((1024, 128), bf16),
            pltpu.VMEM((128, 1024), bf16),
        ],
        compiler_params=pltpu.CompilerParams(vmem_limit_bytes=56 * MIB),
        cost_estimate=pl.CostEstimate(flops=14_000_000_000, bytes_accessed=12_000_000, transcendentals=3_200_000),
        name="attend_forward",
    )(ids, *blocks, w, cos_t, sin_t, freq, held)


def attend_back_body(
    here, w, gm, q01, q2k, val, lse, cc, ss, starts, normed_hbm, narrow,
    dqkv, own_hbm, other_hbm, grad_gain, ka, kb, vb, kt, do01, do2, dk, dv, d01, dq2,
    normed, own, other, got, sent,
):
    load = pltpu.make_async_copy(normed_hbm, normed, got)
    load.start()
    k = high_half(q2k[...].astype(f32)) * score_scale
    kb[...] = k.astype(bf16)
    k_low = pltpu.roll(k, 64, 1)
    ka[...] = k_low.astype(bf16)
    kt[...] = k_low.T.astype(bf16)
    vb[...] = pltpu.roll(val[...].astype(f32), 64, 1).astype(bf16)
    for b in range(8):
        do01[b * 128 : (b + 1) * 128, :] = gm[b, :, 0:128]
        do2[b * 128 : (b + 1) * 128, :] = low_half(gm[b, :, 128:256])
    dk[...] = jnp.zeros_like(dk)
    dv[...] = jnp.zeros_like(dv)

    for c in range(4):
        at, seen = slice(256 * c, 256 * (c + 1)), slice(0, 256 * (c + 1))
        allowed = visible(c, starts)
        qa, qb = q01[at, :], q2k[at, :]
        da, db = do01[at, :], do2[at, :]
        outs = []
        for h in range(3):
            q = qb if h == 2 else qa
            kk = kb if h == 1 else ka
            s = mm_nt(kk[seen, :], q)
            p = jnp.where(allowed, jnp.exp(s - lse[h : h + 1, at]), 0.0)
            d = db if h == 2 else da
            vv = vb if h == 1 else val
            dp = mm_nt(vv[seen, :], d)
            delta = jnp.sum(p * dp, axis=0, keepdims=True)
            ds = (p * (dp - delta)).astype(bf16)
            outs.append(mm(kt[0:64, seen], ds))
            half = high_half if h == 1 else low_half
            dk[seen, :] += mm(ds, half(q))
            dv[seen, :] += mm(p.astype(bf16), half(d))
        out = jnp.concatenate(outs + [jnp.zeros((64, 256), f32)], axis=0).T
        d01[at, :] = out[:, 0:128]
        dq2[at, :] = out[:, 128:256]

    load.wait()

    def store(c):
        return (
            pltpu.make_async_copy(own.at[c], own_hbm.at[c], sent.at[0, c]),
            pltpu.make_async_copy(other.at[c], other_hbm.at[c], sent.at[1, c]),
        )

    def finish(c, total):
        at = pl.ds(pl.multiple_of(c * 256, 256), 256)
        dkk = dk[at, :]
        dkk = (dkk + pltpu.roll(dkk, 64, 1)) * score_scale
        dvv = dv[at, :]
        dvv = low_half(dvv + pltpu.roll(dvv, 64, 1))
        a = d01[at, :]
        lane = lax.broadcasted_iota(jnp.int32, (256, 128), 1)
        b = jnp.where(lane < 64, dq2[at, :], dkk)
        cos, sin = cc[at, :], ss[at, :]
        a = a * cos - quarter(a) * sin
        b = b * cos - quarter(b) * sin
        row = jnp.concatenate([a, b, dvv], axis=1).astype(bf16)
        dqkv[at, :] = row
        whole = mm_nt(row, w[...])
        total = total + jnp.sum(whole * normed[at, :].astype(f32), axis=0, keepdims=True)
        low = whole.astype(bf16)
        own[c] = jnp.where(here[1] == 0, low[0:128], low[128:256])
        other[c] = jnp.where(here[1] == 0, low[128:256], low[0:128])
        for copy in store(c):
            copy.start()
        return total

    total = lax.fori_loop(0, 4, finish, jnp.zeros((1, 1536), f32))
    grad_gain[...] = total / narrow[64:65, :]
    for c in range(4):
        for copy in store(c):
            copy.wait()


def attend_backward(here, gm, q01, q2k, val, lse, cc, ss, starts, normed, w, narrow):
    vm, hbm = pl.BlockSpec(memory_space=pltpu.VMEM), pl.BlockSpec(memory_space=pl.ANY)
    rows = pltpu.VMEM((4, 128, 1536), bf16)
    shape = jax.ShapeDtypeStruct
    half = pltpu.VMEM((1024, 128), bf16)
    full = pltpu.VMEM((1024, 128), f32)
    return pl.pallas_call(
        attend_back_body,
        out_shape=(
            shape((1024, 384), bf16),
            shape((4, 128, 1536), bf16),
            shape((4, 128, 1536), bf16),
            shape((1, 1536), f32),
        ),
        in_specs=[pl.BlockSpec(memory_space=pltpu.SMEM)] + [vm] * 9 + [hbm, vm],
        out_specs=(vm, hbm, hbm, vm),
        scratch_shapes=[
            half, half, half, pltpu.VMEM((128, 1024), bf16), half, half, full, full, full, full,
            pltpu.VMEM((1024, 1536), bf16), rows, rows,
            pltpu.SemaphoreType.DMA, pltpu.SemaphoreType.DMA((2, 4)),
        ],
        compiler_params=pltpu.CompilerParams(vmem_limit_bytes=56 * MIB),
        cost_estimate=pl.CostEstimate(flops=1_000_000, bytes_accessed=100_000, transcendentals=0),
        name="attend_backward",
    )(here, w, gm, q01, q2k, val, lse, cc, ss, starts, normed, narrow)


def experts_body(ids, *refs):
    blocks = refs[:8]
    (grads, back, gate_w, up_w, d_gate, d_up, d_down, aw, gg, gu, routed, second, st, col) = refs[8:]
    e, c = pl.program_id(0), pl.program_id(1)
    first = (e == 0) & (c == 0)

    @pl.when(first)
    def _():
        for b in range(8):
            second[pl.ds(pl.multiple_of(ids[b] * 128, 128), 128), :] = blocks[b][...]
        for b in range(8):
            at = slice(128 * b, 128 * (b + 1))
            st[:, at] = second[at, 0:1536].T
        routed[...] = jnp.zeros_like(routed)

    @pl.when(c == 0)
    def _():
        lane = lax.broadcasted_iota(jnp.int32, (128, 128), 1)
        name = 2 * ids[0] + e
        hit = (lane == name) | (lane == name + 16)
        for b in range(8):
            at = slice(128 * b, 128 * (b + 1))
            table = second[at, 1536:1664].astype(f32)
            w = jnp.sum(jnp.where(hit, table, 0.0), axis=1, keepdims=True)
            col[at, :] = jnp.broadcast_to(w, (128, 128))

    x = second[:, 0:1536]
    gated = mm(x, gate_w[0])
    upper = mm(x, up_w[0])
    h = back[...].astype(f32)
    w = jnp.concatenate([col[...]] * 2, axis=1)
    sig = 1.0 / (1.0 + jnp.exp(-gated))
    silu = gated * sig
    act = silu * upper
    aw[...] = (act * w).astype(bf16)
    dots = residual_scale * jnp.sum(act * h, axis=1, keepdims=True)
    lane = lax.broadcasted_iota(jnp.int32, (1024, 128), 1)
    routed[...] += jnp.where(lane == 2 * ids[0] + e, dots, 0.0)
    ga = h * (w * residual_scale)
    gg[...] = (ga * upper * (sig * (1.0 + gated * (1.0 - sig)))).astype(bf16)
    gu[...] = (ga * silu).astype(bf16)

    d_gate[0] = mm(st[...], gg[...]).astype(bf16)
    d_up[0] = mm(st[...], gu[...]).astype(bf16)
    d_down[0] = (mm(aw[...].T, grads[...]) * residual_scale).astype(bf16)


def experts(ids, blocks, grads, back, gate_w, up_w):
    vm = pl.BlockSpec(memory_space=pltpu.VMEM)
    shape = jax.ShapeDtypeStruct
    wide = pl.BlockSpec((1, 1536, 256), lambda e, c: (e, 0, c))
    tall = pl.BlockSpec((1, 256, 1536), lambda e, c: (e, c, 0))
    line = pl.BlockSpec((1024, 256), lambda e, c: (0, 2 * e + c))
    return pl.pallas_call(
        experts_body,
        grid=(2, 2),
        out_shape=(
            shape((2, 1536, 512), bf16),
            shape((2, 1536, 512), bf16),
            shape((2, 512, 1536), bf16),
            shape((1024, 1024), bf16),
            shape((1024, 1024), bf16),
            shape((1024, 1024), bf16),
            shape((1024, 128), f32),
        ),
        in_specs=[pl.BlockSpec(memory_space=pltpu.SMEM)] + [vm] * 9 + [line, wide, wide],
        out_specs=(wide, wide, tall, line, line, line, vm),
        scratch_shapes=[
            pltpu.VMEM((1024, 1664), bf16),
            pltpu.VMEM((1536, 1024), bf16),
            pltpu.VMEM((1024, 128), f32),
        ],
        compiler_params=pltpu.CompilerParams(vmem_limit_bytes=60 * MIB),
        cost_estimate=pl.CostEstimate(flops=16_000_000_000, bytes_accessed=34_000_000, transcendentals=1_000_000),
        name="experts",
    )(ids, *blocks, grads, back, gate_w, up_w)


def split_cores(here, value, own, other):
    first = here[1] == 0
    own[0] = jnp.where(first, value[0:128], value[128:256])
    other[0] = jnp.where(first, value[128:256], value[0:128])


def by_chip(here, body, width, name, rows, whole, held, flops):
    out = pl.BlockSpec((1, 128, width), lambda m, here: (m, 0, 0))
    shape = jax.ShapeDtypeStruct((4, 128, width), bf16)
    lines = [
        pl.BlockSpec((256, a.shape[1]), lambda m, here: (m, 0)) for a in rows
    ]
    return pl.pallas_call(
        body,
        grid_spec=pltpu.PrefetchScalarGridSpec(
            num_scalar_prefetch=1,
            grid=(4,),
            in_specs=lines
            + [pl.BlockSpec(memory_space=pltpu.VMEM)] * len(whole)
            + [pl.BlockSpec(memory_space=pl.ANY)] * len(held),
            out_specs=(out, out),
        ),
        out_shape=(shape, shape),
        compiler_params=pltpu.CompilerParams(vmem_limit_bytes=56 * MIB),
        cost_estimate=pl.CostEstimate(flops=flops, bytes_accessed=100_000, transcendentals=0),
        name=name,
    )(here, *rows, *whole, *held)


def back_body(here, gg, gu, routed, gate_w, up_w, *refs):
    own, other = refs[-2:]
    total = mm_nt(gg[:, 0:512], gate_w[0]) + mm_nt(gg[:, 512:1024], gate_w[1])
    total = total + mm_nt(gu[:, 0:512], up_w[0]) + mm_nt(gu[:, 512:1024], up_w[1])
    table = routed[...]
    high = table.astype(bf16).astype(f32)
    low = pltpu.roll(table - high, 16, 1)
    lane = lax.broadcasted_iota(jnp.int32, table.shape, 1)
    tail = jnp.where(lane < 16, high, low)
    split_cores(here, jnp.concatenate([total, tail], axis=1).astype(bf16), own, other)


def experts_back(here, gg, gu, routed, gate_w, up_w, held):
    rows, whole = (gg, gu, routed), (gate_w, up_w)
    return by_chip(here, back_body, 1664, "experts_back", rows, whole, held, 10**6)


def combine_body(here, aw, down_w, own, other):
    total = mm(aw[:, 0:512], down_w[0]) + mm(aw[:, 512:1024], down_w[1])
    split_cores(here, total.astype(bf16), own, other)


def combine(here, aw, down_w):
    return by_chip(here, combine_body, 1536, "combine", (aw,), (down_w,), (), 8 * 10**9)


def widen_body(a, b, c, x, y, z, *refs):
    held, grown, got, sent = refs[0:3], refs[3:6], refs[6], refs[7]
    work = []
    for k, (source, target) in enumerate(((a, x), (b, y), (c, z))):
        half = source.shape[1] // 2
        for e in range(2):
            for i in range(2):
                j = 2 * e + i
                at = pl.ds(half * i, half)
                load = pltpu.make_async_copy(
                    source.at[e, at], held[k].at[j], got.at[4 * k + j]
                )
                store = pltpu.make_async_copy(
                    grown[k].at[j], target.at[e, at], sent.at[4 * k + j]
                )
                load.start()
                work.append((k, j, load, store))
    for k, j, load, store in work:
        load.wait()
        grown[k][j] = held[k][j].astype(f32)
        store.start()
    for _, _, _, store in work:
        store.wait()


def widen(a, b, c):
    hbm = pl.BlockSpec(memory_space=pl.ANY)
    shapes = [(4, v.shape[1] // 2, v.shape[2]) for v in (a, b, c)]
    return pl.pallas_call(
        widen_body,
        out_shape=tuple(jax.ShapeDtypeStruct(v.shape, f32) for v in (a, b, c)),
        in_specs=[hbm] * 3,
        out_specs=(hbm,) * 3,
        scratch_shapes=[pltpu.VMEM(s, bf16) for s in shapes]
        + [pltpu.VMEM(s, f32) for s in shapes]
        + [pltpu.SemaphoreType.DMA((12,)), pltpu.SemaphoreType.DMA((12,))],
        compiler_params=pltpu.CompilerParams(vmem_limit_bytes=56 * MIB),
        cost_estimate=pl.CostEstimate(flops=1_000_000, bytes_accessed=28_000_000, transcendentals=0),
        name="widen",
    )(a, b, c)


def back_rows_body(ids, *refs):
    blocks, (down_w, grads, back) = refs[:8], refs[8:]

    @pl.when(pl.program_id(0) == 0)
    def _():
        for b in range(8):
            grads[pl.ds(pl.multiple_of(ids[b] * 128, 128), 128), :] = blocks[b][...]

    back[...] = mm_nt(grads[...], down_w[0]).astype(bf16)


def back_rows(ids, blocks, down_w):
    vm = pl.BlockSpec(memory_space=pltpu.VMEM)
    shape = jax.ShapeDtypeStruct
    return pl.pallas_call(
        back_rows_body,
        grid=(2,),
        out_shape=(shape((1024, 1536), bf16), shape((1024, 1024), bf16)),
        in_specs=[pl.BlockSpec(memory_space=pltpu.SMEM)]
        + [vm] * 8
        + [pl.BlockSpec((1, 512, 1536), lambda e: (e, 0, 0))],
        out_specs=(vm, pl.BlockSpec((1024, 512), lambda e: (0, e))),
        compiler_params=pltpu.CompilerParams(vmem_limit_bytes=56 * MIB),
        cost_estimate=pl.CostEstimate(flops=8_000_000_000, bytes_accessed=11_000_000, transcendentals=0),
        name="back_rows",
    )(ids, *blocks, down_w)


def weight_body(normed, grad_qkv, mixed, branch, gain_a, gain_b, router, out):
    first = mm(normed[...].T, grad_qkv[...])
    cols = jnp.concatenate([branch[b, :, 192:384] for b in range(8)], axis=0)
    second = mm(mixed[...].T, cols)
    last = jnp.concatenate([first[:, 256:320], second], axis=1)
    zero = jnp.zeros((1, 32), f32)
    for y in range(4):
        rows, lanes = slice(96 * y, 96 * (y + 1)), slice(96 * y, 96 * (y + 1))
        gains = jnp.concatenate(
            [gain_a[:, lanes], zero, gain_b[:, lanes], zero], axis=1
        )
        small = jnp.concatenate([router[:, lanes], jnp.zeros((16, 160), f32)], axis=1)
        row = lax.broadcasted_iota(jnp.int32, (16, 256), 0)
        extra = jnp.where(row == 0, jnp.broadcast_to(gains, (16, 256)), 0.0)
        out[y, 0:96, 0:256] = first[rows, 0:256].astype(bf16)
        out[y, 96:112, 0:256] = small.astype(bf16)
        out[y, 0:96, 256:512] = last[rows].astype(bf16)
        out[y, 96:112, 256:512] = extra.astype(bf16)


def weight_grads(normed, grad_qkv, mixed, branch, gain_a, gain_b, router):
    vm = pl.BlockSpec(memory_space=pltpu.VMEM)
    slab = pl.BlockSpec((1024, 384), lambda i: (0, i))
    flat = pl.BlockSpec((1, 384), lambda i: (0, i))
    return pl.pallas_call(
        weight_body,
        grid=(4,),
        out_shape=jax.ShapeDtypeStruct((16, 112, 512), bf16),
        in_specs=[slab, vm, slab, vm, flat, flat, pl.BlockSpec((16, 384), lambda i: (0, i))],
        out_specs=pl.BlockSpec((4, 112, 512), lambda i: (i, 0, 0)),
        compiler_params=pltpu.CompilerParams(vmem_limit_bytes=56 * MIB),
        cost_estimate=pl.CostEstimate(flops=1_000_000, bytes_accessed=100_000, transcendentals=0),
        name="weight_grads",
    )(normed, grad_qkv, mixed, branch, gain_a, gain_b, router)


def sum_body(pieces, out):
    total = pieces[0].astype(f32)
    for i in range(1, pieces.shape[0]):
        total = total + pieces[i].astype(f32)
    out[...] = total.astype(bf16)


def sum_pieces(pieces):
    vm = pl.BlockSpec(memory_space=pltpu.VMEM)
    return pl.pallas_call(
        sum_body,
        out_shape=jax.ShapeDtypeStruct(pieces.shape[1:], bf16),
        in_specs=[vm],
        out_specs=vm,
        cost_estimate=pl.CostEstimate(flops=1_000_000, bytes_accessed=100_000, transcendentals=0),
        name="sum_pieces",
    )(pieces)


def assemble_body(ids, *refs):
    blocks, (query, key, value, out, gain_a, gain_b, router) = refs[:8], refs[8:]
    total = jnp.zeros((16, 512), f32)
    for m in range(4):
        here, there = blocks[2 * m][...].astype(f32), blocks[2 * m + 1][...].astype(f32)
        total = total + here[96:112] + there[96:112]
        first = ids[2 * m] < ids[2 * m + 1]
        a, b = jnp.where(first, here, there)[0:96], jnp.where(first, there, here)[0:96]
        chip = ids[2 * m] // 2
        wide = pl.ds(pl.multiple_of(chip * 384, 128), 384)
        slim = pl.ds(pl.multiple_of(chip * 128, 128), 128)
        query[:, wide] = jnp.concatenate([a[:, 0:192], b[:, 0:192]], axis=1)
        key[:, slim] = jnp.concatenate([a[:, 192:256], b[:, 192:256]], axis=1)
        value[:, slim] = jnp.concatenate([a[:, 256:320], b[:, 256:320]], axis=1)
        out[:, wide] = jnp.concatenate([a[:, 320:512], b[:, 320:512]], axis=1)
    router[...] = total[:, 0:96]
    gain_a[...] = total[0:1, 256:352]
    gain_b[...] = total[0:1, 384:480]


def assemble(ids, blocks):
    vm = pl.BlockSpec(memory_space=pltpu.VMEM)
    shape = jax.ShapeDtypeStruct
    return pl.pallas_call(
        assemble_body,
        out_shape=(
            shape((96, 1536), f32),
            shape((96, 512), f32),
            shape((96, 512), f32),
            shape((96, 1536), f32),
            shape((1, 96), f32),
            shape((1, 96), f32),
            shape((16, 96), f32),
        ),
        in_specs=[pl.BlockSpec(memory_space=pltpu.SMEM)] + [vm] * 8,
        out_specs=(vm,) * 7,
        cost_estimate=pl.CostEstimate(flops=1_000_000, bytes_accessed=100_000, transcendentals=0),
        name="assemble",
    )(ids, *blocks)


def column(row):
    n = row.shape[1]
    down = lax.broadcasted_iota(jnp.int32, (n, n), 0)
    along = lax.broadcasted_iota(jnp.int32, (n, n), 1)
    return jnp.sum(jnp.where(down == along, row.astype(f32), 0.0), axis=1, keepdims=True)


def pack_body(
    at, w_query, w_key, w_value, gain_a, gain_b, router, tokens, seg, share, sent
):
    first = at[1] == 0
    x = at[0]
    wide = w_query[:, pl.ds(pl.multiple_of(x * 384, 128), 384)].astype(f32)
    slim = pl.ds(pl.multiple_of(x * 128, 128), 128)
    key, value = w_key[:, slim].astype(f32), w_value[:, slim].astype(f32)
    columns = jnp.concatenate(
        [
            jnp.where(first, wide[:, 0:192], wide[:, 192:384]),
            jnp.where(first, key[:, 0:64], key[:, 64:128]),
            jnp.where(first, value[:, 0:64], value[:, 64:128]),
            column(gain_a[...]),
            column(gain_b[...]),
            router[...].astype(f32).T,
            jnp.zeros((96, 46), f32),
        ],
        axis=1,
    ).astype(bf16)
    for i in range(16):
        share[i] = columns
    sent[:, 0:1536] = tokens[...]
    sent[:, 1536:1664] = jnp.broadcast_to(column(seg[...]), (128, 128)).astype(bf16)


def pack(at, w_query, w_key, w_value, gain_a, gain_b, router, tokens, seg):
    vm = pl.BlockSpec(memory_space=pltpu.VMEM)
    shape = jax.ShapeDtypeStruct
    return pl.pallas_call(
        pack_body,
        out_shape=(shape((16, 96, 384), bf16), shape((128, 1664), bf16)),
        in_specs=[pl.BlockSpec(memory_space=pltpu.SMEM)] + [vm] * 8,
        out_specs=(vm,) * 2,
        cost_estimate=pl.CostEstimate(flops=1_000_000, bytes_accessed=2_000_000, transcendentals=0),
        name="pack",
    )(at, w_query, w_key, w_value, gain_a, gain_b, router, tokens, seg)


def project_out_body(mixed, w_out, tokens, narrow, named, sent, hidden, gates, mx):
    for p in range(4):
        mx[:, 384 * p : 384 * (p + 1)] = jnp.concatenate(
            [mixed[2 * p, :, 0:192], mixed[2 * p + 1, :, 0:192]], axis=1
        )
    value = tokens[...].astype(f32) + residual_scale * mm(mx[...], w_out[...])
    hidden[...] = value
    r = lax.rsqrt(jnp.mean(value * value, axis=1, keepdims=True) + eps)
    second = (value * r * narrow[65:66, :]).astype(bf16)
    sent[:, 0:1536] = second
    logits = pltpu.roll(mm_nt(second, narrow[...].astype(bf16)), 62, 1)
    on = named[...] > 0.5
    logits = jnp.where(on, logits, -1e30)
    top = jnp.max(logits, axis=1, keepdims=True)
    e = jnp.where(on, jnp.exp(logits - top), 0.0)
    g = e / jnp.sum(e, axis=1, keepdims=True)
    gates[...] = g
    high = g.astype(bf16)
    low = pltpu.roll(g - high.astype(f32), 16, 1)
    lane = lax.broadcasted_iota(jnp.int32, g.shape, 1)
    sent[:, 1536:1664] = jnp.where(lane < 16, g, low).astype(bf16)


def project_out(mixed, w_out, tokens, narrow, named):
    vm = pl.BlockSpec(memory_space=pltpu.VMEM)
    shape = jax.ShapeDtypeStruct
    return pl.pallas_call(
        project_out_body,
        out_shape=(
            shape((128, 1664), bf16),
            shape((128, 1536), f32),
            shape((128, 128), f32),
            shape((128, 1536), bf16),
        ),
        in_specs=[vm] * 5,
        out_specs=(vm,) * 4,
        compiler_params=pltpu.CompilerParams(vmem_limit_bytes=56 * MIB),
        cost_estimate=pl.CostEstimate(flops=4_000_000_000, bytes_accessed=8_000_000, transcendentals=0),
        name="project_out",
    )(mixed, w_out, tokens, narrow, named)


def middle_body(
    w_out, sums, grads, hidden, gates, narrow, _, grad_hidden, heads, grad_gain, grad_router, gx
):
    gain = narrow[65:66, :]
    total = sums[0].astype(f32)
    for i in range(1, 4):
        total = total + sums[i].astype(f32)
    value = hidden[...]
    r = lax.rsqrt(jnp.mean(value * value, axis=1, keepdims=True) + eps)
    second = (value * r * gain).astype(bf16)
    g = gates[...]
    table = total[:, 1536:1664]
    lane = lax.broadcasted_iota(jnp.int32, g.shape, 1)
    table = jnp.where(lane < 16, table + pltpu.roll(table, 112, 1), 0.0)
    logits = (g * (table - jnp.sum(g * table, axis=1, keepdims=True))).astype(bf16)
    grad_router[...] = mm(logits.astype(f32).T.astype(bf16), second)[0:16]
    router = pltpu.roll(logits.astype(f32), 66, 1).astype(bf16)
    grad_second = total[:, 0:1536] + mm(router, narrow[...].astype(bf16))
    grad_gain[...] = jnp.sum(grad_second * value * r, axis=0, keepdims=True)
    scaled = grad_second * gain
    gh = (
        grads[...].astype(f32)
        + r * scaled
        - value * (r * r * r) * jnp.mean(value * scaled, axis=1, keepdims=True)
    )
    grad_hidden[...] = gh
    low = (residual_scale * gh).astype(bf16)
    gx[...] = mm_nt(low, w_out[...])
    low = low.astype(f32)
    for j in range(8):
        cols = slice(192 * j, 192 * (j + 1))
        heads[j] = jnp.concatenate([gx[:, cols], low[:, cols]], axis=1).astype(bf16)


def middle(w_out, sums, grads, hidden, gates, narrow, held):
    vm = pl.BlockSpec(memory_space=pltpu.VMEM)
    shape = jax.ShapeDtypeStruct
    return pl.pallas_call(
        middle_body,
        out_shape=(
            shape((128, 1536), f32),
            shape((8, 128, 384), bf16),
            shape((1, 1536), f32),
            shape((16, 1536), f32),
        ),
        in_specs=[vm] * 6 + [pl.BlockSpec(memory_space=pl.ANY)],
        out_specs=(vm,) * 4,
        scratch_shapes=[pltpu.VMEM((128, 1536), f32)],
        compiler_params=pltpu.CompilerParams(vmem_limit_bytes=56 * MIB),
        cost_estimate=pl.CostEstimate(flops=1_000_000, bytes_accessed=100_000, transcendentals=0),
        name="middle",
    )(w_out, sums, grads, hidden, gates, narrow, held)


def shift(value, axis, amount):
    size = lax.axis_size(axis)
    return lax.ppermute(value, axis, [((i + amount) % size, i) for i in range(size)])


def swap(value):
    return lax.ppermute(value, "core", [(0, 1), (1, 0)])


def tied(*values):
    return lax.optimization_barrier(values)


def gather_x(block):
    return [block] + [shift(block, "x", m) for m in (1, 2, 3)]


def both_cores(blocks):
    return [each for block in blocks for each in (block, swap(block))]


def near_sum(own, other):
    return (own.astype(f32) + swap(other).astype(f32)).astype(bf16)


def exchange(near):
    return lax.all_to_all(near, "x", 0, 0, tiled=True)


def exchange_apart(near):
    x = lax.axis_index("x")
    pieces = [lax.dynamic_index_in_dim(near, (x + m) % 4, 0, False) for m in range(4)]
    return [pieces[0]] + [shift(pieces[m], "x", -m) for m in (2, 1, 3)]


def total_of(terms):
    total = terms[0].astype(f32)
    for term in terms[1:]:
        total = total + term.astype(f32)
    return total


def inverse_rms(values):
    return lax.rsqrt(jnp.mean(values * values, axis=-1, keepdims=True) + eps)


def per_device(
    tokens,
    segments,
    routes,
    gain_attn,
    w_query,
    w_key,
    w_value,
    w_out,
    gain_moe,
    w_router,
    expert_gate,
    expert_up,
    expert_down,
    out_grad,
):
    rows, width = tokens.shape
    parts = 8
    seq = rows * parts
    x, core = lax.axis_index("x"), lax.axis_index("core")
    me = x * 2 + core
    z = lax.axis_index("z")
    at = jnp.stack([x, core, z])

    share, sent = pack(
        at,
        w_query,
        w_key,
        w_value,
        gain_attn[None, :],
        gain_moe[None, :],
        w_router.T,
        tokens,
        segments[None, :],
    )
    out_all = lax.all_gather(w_out, ("z", "y"), axis=0, tiled=True)
    qkv_w = lax.all_to_all(share, ("z", "y"), 0, 0, tiled=True).reshape(width, 384)
    far = gather_x(sent)
    far[1], grads_sent = tied(far[1], out_grad)
    blocks = both_cores(far)
    grads_far = gather_x(grads_sent)
    lane = jnp.arange(128, dtype=jnp.int32)

    chips = (x + jnp.arange(4, dtype=jnp.int32)) % 4
    cores = jnp.bitwise_xor(core, jnp.arange(2, dtype=jnp.int32))
    ids = (chips[:, None] * 2 + cores[None, :]).reshape(parts)
    place = jnp.arange(seq, dtype=jnp.int32)
    freq = rope_base ** (
        -(jnp.arange(128, dtype=jnp.int32) % 32).astype(f32) * 2.0 / HEAD_DIM
    )[None, :]
    angles = place.astype(f32)[:, None] * freq

    named = jnp.any(routes[:, :, None] == lane[None, None, :], axis=1).astype(f32)

    normed, narrow, q01, q2k, val, lse, cos, sin, starts, mixed_head = attend_forward(
        ids, blocks, qkv_w, jnp.cos(angles), jnp.sin(angles), freq, named
    )
    mixed_head, *grads_far = tied(mixed_head, *grads_far)
    grad_blocks = both_cores(grads_far)
    mixed = lax.all_to_all(mixed_head, ("x", "core"), 0, 0, tiled=True)
    sent_two, hidden, gates, mixed = project_out(
        mixed, out_all, tokens, narrow, named
    )
    far_two = gather_x(sent_two)
    grad_all, back = back_rows(ids, grad_blocks, expert_down)
    twins = [swap(block) for block in far_two]
    mixed, back, *far_two = tied(mixed, back, *far_two)
    second_blocks = [each for pair in zip(far_two, twins) for each in pair]
    mixed_all = lax.all_gather(mixed, ("x", "core"), axis=0, tiled=True)

    grad_w_gate, grad_w_up, grad_w_down, weighted, grad_gate_pre, grad_up_pre, routed = experts(
        ids, second_blocks, grad_all, back, expert_gate, expert_up
    )
    sums = lax.psum((grad_w_gate, grad_w_up, grad_w_down), ("z", "y"))
    own, other = experts_back(
        at, grad_gate_pre, grad_up_pre, routed, expert_gate, expert_up, ()
    )
    near = near_sum(own, other)
    near, weighted = tied(near, weighted)
    terms = exchange(near)
    own_out, other_out = combine(at, weighted, expert_down)

    grad_hidden, heads, grad_gain_two, grad_router = middle(
        out_all, terms, out_grad, hidden, gates, narrow, own_out
    )
    grad_heads = lax.all_to_all(heads, ("x", "core"), 0, 0, tiled=True)
    grad_qkv, own, other, grad_gain_one = attend_backward(
        at, grad_heads, q01, q2k, val, lse, cos, sin, starts, normed, qkv_w, narrow
    )
    table = weight_grads(
        normed, grad_qkv, mixed_all, grad_heads, grad_gain_one, grad_gain_two, grad_router
    )
    own_out, table = tied(own_out, table)
    near_out = near_sum(own_out, other_out)
    output = (hidden + residual_scale * total_of(exchange_apart(near_out))).astype(bf16)
    normed_mine = total_of(exchange_apart(near_sum(own, other)))
    inputs = tokens.astype(f32)
    scale_one = inverse_rms(inputs)
    scaled_one = normed_mine * narrow[64:65, :]
    grad_inputs = (
        grad_hidden
        + scale_one * scaled_one
        - inputs * scale_one**3 * jnp.mean(inputs * scaled_one, axis=-1, keepdims=True)
    )

    pieces = lax.all_to_all(table, ("z", "y"), 0, 0, tiled=True)
    pieces, output, grad_inputs = tied(pieces, output, grad_inputs)
    lines = both_cores(gather_x(sum_pieces(pieces)))
    grad_gate, grad_up, grad_down = widen(*sums)
    grad_q, grad_k, grad_v, grad_o, gain_a, gain_b, router = assemble(ids, lines)
    return (
        output,
        grad_inputs,
        gain_a.reshape(-1),
        grad_q,
        grad_k,
        grad_v,
        grad_o,
        gain_b.reshape(-1),
        router.T,
        grad_gate,
        grad_up,
        grad_down,
    )


def solution(mesh):
    fine = Mesh(mesh.devices.reshape(4, 4, 4, 2), ("z", "y", "x", "core"))
    dp, expert, both = ("z", "y"), ("x", "core"), ("z", "y", "x", "core")
    placed = (
        P(both, None),
        P(both),
        P(both, None),
        P(dp),
        P(dp, None),
        P(dp, None),
        P(dp, None),
        P(dp, None),
        P(dp),
        P(dp, None),
        P(expert, None, None),
        P(expert, None, None),
        P(expert, None, None),
    )
    return jax.shard_map(
        per_device,
        mesh=fine,
        in_specs=placed + (P(both, None),),
        out_specs=(P(both, None),) * 2 + placed[3:],
        check_vma=False,
    )
```

```python
import jax
import jax.numpy as jnp
from jax import lax
from jax.experimental import pallas as pl
from jax.experimental.pallas import tpu as pltpu
from jax.sharding import Mesh, PartitionSpec as P

HEADS = 24
KV_HEADS = 8
HEAD_DIM = 64
GROUP = HEADS // KV_HEADS
TOP = 8
EXPERTS = 16

eps = 1e-06
residual_scale = 0.22
score_scale = 0.015625
rope_base = 10000.0
doc_slots = 3
MIB = 1024 * 1024

bf16 = jnp.bfloat16
f32 = jnp.float32


def mm(a, b):
    return lax.dot_general(a, b, (((1,), (0,)), ((), ())), preferred_element_type=f32)


def mm_nt(a, b):
    return lax.dot_general(a, b, (((1,), (1,)), ((), ())), preferred_element_type=f32)


def low_half(value):
    lane = lax.broadcasted_iota(jnp.int32, value.shape, 1)
    return jnp.where(lane < 64, value, jnp.zeros_like(value))


def high_half(value):
    lane = lax.broadcasted_iota(jnp.int32, value.shape, 1)
    return jnp.where(lane >= 64, value, jnp.zeros_like(value))


def quarter(value):
    lane = lax.broadcasted_iota(jnp.int32, value.shape, 1)
    up, down = pltpu.roll(value, 96, 1), pltpu.roll(value, 32, 1)
    return jnp.where(lane % 64 < 32, -up, down)


def visible(chunk, starts):
    keys = 256 * (chunk + 1)
    place = (256 * chunk + lax.broadcasted_iota(jnp.int32, (1, 256), 1)).astype(f32)
    one = jnp.concatenate([starts[0:1], starts[0:1]], axis=1)
    two = jnp.concatenate([starts[1:2], starts[1:2]], axis=1)
    begin = jnp.where(place >= two, two, jnp.where(place >= one, one, jnp.zeros_like(one)))
    at = lax.broadcasted_iota(jnp.int32, (keys, 256), 0).astype(f32)
    return (at <= place) & (at >= begin)


def attend_body(ids, *refs):
    blocks = refs[:8]
    (w, cos_t, sin_t, freq, _, normed, narrow, gain_row, q01, q2k, val, lse, cos_o, sin_o, starts, mixed,
     ka, kb, vt) = refs[8:]
    one = jnp.zeros((1, 128), f32)
    two = jnp.zeros((1, 128), f32)
    for b in range(8):
        seg = blocks[b][:, 1536:1664].astype(f32)
        one = one + jnp.sum(jnp.where(seg < 0.5, 1.0, 0.0), axis=0, keepdims=True)
        two = two + jnp.sum(jnp.where(seg < 1.5, 1.0, 0.0), axis=0, keepdims=True)
    starts[...] = jnp.concatenate([one, two, jnp.zeros((6, 128), f32)], axis=0)
    begin_rows = jnp.concatenate([one, two, jnp.zeros((6, 128), f32)], axis=0)
    angles = begin_rows * freq[...]
    cos_b, sin_b = jnp.cos(angles), jnp.sin(angles)
    last = w[:, 256:384].astype(f32).T
    narrow[...] = last[64:128].astype(bf16)
    gain = last[64:65]
    gain_row[...] = gain
    for b in range(8):
        x = blocks[b][:, 0:1536].astype(f32)
        r = lax.rsqrt(jnp.mean(x * x, axis=1, keepdims=True) + eps)
        at = pl.ds(pl.multiple_of(ids[b] * 128, 128), 128)
        normed[at, :] = (x * r * gain).astype(bf16)
    def project(c, carry):
        at = pl.ds(pl.multiple_of(c * 256, 256), 256)
        u = mm(normed[at, :], w[...])
        place = (lax.broadcasted_iota(jnp.int32, (256, 128), 0) + c * 256).astype(f32)
        in_two, in_one = place >= two, place >= one
        cb = jnp.where(in_two, cos_b[1:2], jnp.where(in_one, cos_b[0:1], 1.0))
        sb = jnp.where(in_two, sin_b[1:2], jnp.where(in_one, sin_b[0:1], 0.0))
        ct, st = cos_t[at, :], sin_t[at, :]
        cc = ct * cb + st * sb
        ss = st * cb - ct * sb
        cos_o[at, :] = cc
        sin_o[at, :] = ss
        a, bq, v = u[:, 0:128], u[:, 128:256], u[:, 256:384]
        a = a * cc + quarter(a) * ss
        bq = bq * cc + quarter(bq) * ss
        v = low_half(v)
        q01[at, :] = a.astype(bf16)
        q2k[at, :] = bq.astype(bf16)
        val[at, :] = v.astype(bf16)
        k = high_half(bq) * score_scale
        kb[at, :] = k.astype(bf16)
        ka[at, :] = pltpu.roll(k, 64, 1).astype(bf16)
        vt[:, at] = v.T.astype(bf16)
        return carry

    lax.fori_loop(0, 4, project, 0)

    for c in range(4):
        at, seen = slice(256 * c, 256 * (c + 1)), slice(0, 256 * (c + 1))
        allowed = visible(c, starts)
        outs = []
        for h in range(3):
            q = q2k[at, :] if h == 2 else q01[at, :]
            kk = kb if h == 1 else ka
            s = mm_nt(kk[seen, :], q)
            s = jnp.where(allowed, s, -1e30)
            top = jnp.max(s, axis=0, keepdims=True)
            p = jnp.exp(s - top)
            total = jnp.sum(p, axis=0, keepdims=True)
            lse[h : h + 1, at] = top + jnp.log(total)
            pb = (p * (1.0 / total)).astype(bf16)
            outs.append(mm(vt[0:64, seen], pb))
        out = jnp.concatenate(outs + [jnp.zeros((64, 256), f32)], axis=0).T.astype(bf16)
        mixed[2 * c] = out[0:128]
        mixed[2 * c + 1] = out[128:256]


def attend_forward(ids, blocks, w, cos_t, sin_t, freq, held):
    vm = pl.BlockSpec(memory_space=pltpu.VMEM)
    shape = jax.ShapeDtypeStruct
    return pl.pallas_call(
        attend_body,
        out_shape=(
            shape((1024, 1536), bf16),
            shape((64, 1536), bf16),
            shape((1, 1536), f32),
            shape((1024, 128), bf16),
            shape((1024, 128), bf16),
            shape((1024, 128), bf16),
            shape((8, 1024), f32),
            shape((1024, 128), f32),
            shape((1024, 128), f32),
            shape((8, 128), f32),
            shape((8, 128, 256), bf16),
        ),
        in_specs=[pl.BlockSpec(memory_space=pltpu.SMEM)]
        + [vm] * 12
        + [pl.BlockSpec(memory_space=pl.ANY)],
        out_specs=(vm,) * 11,
        scratch_shapes=[
            pltpu.VMEM((1024, 128), bf16),
            pltpu.VMEM((1024, 128), bf16),
            pltpu.VMEM((128, 1024), bf16),
        ],
        compiler_params=pltpu.CompilerParams(vmem_limit_bytes=56 * MIB),
        cost_estimate=pl.CostEstimate(flops=14_000_000_000, bytes_accessed=12_000_000, transcendentals=3_200_000),
        name="attend_forward",
    )(ids, *blocks, w, cos_t, sin_t, freq, held)


def attend_back_body(
    here, w, gm, q01, q2k, val, lse, cc, ss, starts, normed_hbm, gain,
    dqkv, own_hbm, other_hbm, grad_gain, ka, kb, vb, kt, do01, do2, dk, dv, d01, dq2,
    normed, own, other, got, sent,
):
    load = pltpu.make_async_copy(normed_hbm, normed, got)
    load.start()
    k = high_half(q2k[...].astype(f32)) * score_scale
    kb[...] = k.astype(bf16)
    k_low = pltpu.roll(k, 64, 1)
    ka[...] = k_low.astype(bf16)
    kt[...] = k_low.T.astype(bf16)
    vb[...] = pltpu.roll(val[...].astype(f32), 64, 1).astype(bf16)
    for b in range(8):
        do01[b * 128 : (b + 1) * 128, :] = gm[b, :, 0:128]
        do2[b * 128 : (b + 1) * 128, :] = low_half(gm[b, :, 128:256])
    dk[...] = jnp.zeros_like(dk)
    dv[...] = jnp.zeros_like(dv)

    for c in range(4):
        at, seen = slice(256 * c, 256 * (c + 1)), slice(0, 256 * (c + 1))
        allowed = visible(c, starts)
        qa, qb = q01[at, :], q2k[at, :]
        da, db = do01[at, :], do2[at, :]
        outs = []
        for h in range(3):
            q = qb if h == 2 else qa
            kk = kb if h == 1 else ka
            s = mm_nt(kk[seen, :], q)
            p = jnp.where(allowed, jnp.exp(s - lse[h : h + 1, at]), 0.0)
            d = db if h == 2 else da
            vv = vb if h == 1 else val
            dp = mm_nt(vv[seen, :], d)
            delta = jnp.sum(p * dp, axis=0, keepdims=True)
            ds = (p * (dp - delta)).astype(bf16)
            outs.append(mm(kt[0:64, seen], ds))
            half = high_half if h == 1 else low_half
            dk[seen, :] += mm(ds, half(q))
            dv[seen, :] += mm(p.astype(bf16), half(d))
        out = jnp.concatenate(outs + [jnp.zeros((64, 256), f32)], axis=0).T
        d01[at, :] = out[:, 0:128]
        dq2[at, :] = out[:, 128:256]

    load.wait()

    def store(c):
        return (
            pltpu.make_async_copy(own.at[c], own_hbm.at[c], sent.at[0, c]),
            pltpu.make_async_copy(other.at[c], other_hbm.at[c], sent.at[1, c]),
        )

    def finish(c, total):
        at = pl.ds(pl.multiple_of(c * 256, 256), 256)
        dkk = dk[at, :]
        dkk = (dkk + pltpu.roll(dkk, 64, 1)) * score_scale
        dvv = dv[at, :]
        dvv = low_half(dvv + pltpu.roll(dvv, 64, 1))
        a = d01[at, :]
        lane = lax.broadcasted_iota(jnp.int32, (256, 128), 1)
        b = jnp.where(lane < 64, dq2[at, :], dkk)
        cos, sin = cc[at, :], ss[at, :]
        a = a * cos - quarter(a) * sin
        b = b * cos - quarter(b) * sin
        row = jnp.concatenate([a, b, dvv], axis=1).astype(bf16)
        dqkv[at, :] = row
        whole = mm_nt(row, w[...])
        total = total + jnp.sum(whole * normed[at, :].astype(f32), axis=0, keepdims=True)
        low = whole.astype(bf16)
        own[c] = jnp.where(here[1] == 0, low[0:128], low[128:256])
        other[c] = jnp.where(here[1] == 0, low[128:256], low[0:128])
        for copy in store(c):
            copy.start()
        return total

    total = lax.fori_loop(0, 4, finish, jnp.zeros((1, 1536), f32))
    grad_gain[...] = total / gain[...]
    for c in range(4):
        for copy in store(c):
            copy.wait()


def attend_backward(here, gm, q01, q2k, val, lse, cc, ss, starts, normed, w, gain):
    vm, hbm = pl.BlockSpec(memory_space=pltpu.VMEM), pl.BlockSpec(memory_space=pl.ANY)
    rows = pltpu.VMEM((4, 128, 1536), bf16)
    shape = jax.ShapeDtypeStruct
    half = pltpu.VMEM((1024, 128), bf16)
    full = pltpu.VMEM((1024, 128), f32)
    return pl.pallas_call(
        attend_back_body,
        out_shape=(
            shape((1024, 384), bf16),
            shape((4, 128, 1536), bf16),
            shape((4, 128, 1536), bf16),
            shape((1, 1536), f32),
        ),
        in_specs=[pl.BlockSpec(memory_space=pltpu.SMEM)] + [vm] * 9 + [hbm, vm],
        out_specs=(vm, hbm, hbm, vm),
        scratch_shapes=[
            half, half, half, pltpu.VMEM((128, 1024), bf16), half, half, full, full, full, full,
            pltpu.VMEM((1024, 1536), bf16), rows, rows,
            pltpu.SemaphoreType.DMA, pltpu.SemaphoreType.DMA((2, 4)),
        ],
        compiler_params=pltpu.CompilerParams(vmem_limit_bytes=56 * MIB),
        cost_estimate=pl.CostEstimate(flops=1_000_000, bytes_accessed=100_000, transcendentals=0),
        name="attend_backward",
    )(here, w, gm, q01, q2k, val, lse, cc, ss, starts, normed, gain)


def experts_body(ids, *refs):
    blocks = refs[:8]
    (grads, back, gate_w, up_w, d_gate, d_up, d_down, aw, gg, gu, routed, second, st, col) = refs[8:]
    e, c = pl.program_id(0), pl.program_id(1)
    first = (e == 0) & (c == 0)

    @pl.when(first)
    def _():
        for b in range(8):
            second[pl.ds(pl.multiple_of(ids[b] * 128, 128), 128), :] = blocks[b][...]
        for b in range(8):
            at = slice(128 * b, 128 * (b + 1))
            st[:, at] = second[at, 0:1536].T
        routed[...] = jnp.zeros_like(routed)

    @pl.when(c == 0)
    def _():
        lane = lax.broadcasted_iota(jnp.int32, (128, 128), 1)
        name = 2 * ids[0] + e
        hit = (lane == name) | (lane == name + 16)
        for b in range(8):
            at = slice(128 * b, 128 * (b + 1))
            table = second[at, 1536:1664].astype(f32)
            w = jnp.sum(jnp.where(hit, table, 0.0), axis=1, keepdims=True)
            col[at, :] = jnp.broadcast_to(w, (128, 128))

    x = second[:, 0:1536]
    gated = mm(x, gate_w[0])
    upper = mm(x, up_w[0])
    h = back[...].astype(f32)
    w = jnp.concatenate([col[...]] * 2, axis=1)
    sig = 1.0 / (1.0 + jnp.exp(-gated))
    silu = gated * sig
    act = silu * upper
    aw[...] = (act * w).astype(bf16)
    dots = residual_scale * jnp.sum(act * h, axis=1, keepdims=True)
    lane = lax.broadcasted_iota(jnp.int32, (1024, 128), 1)
    routed[...] += jnp.where(lane == 2 * ids[0] + e, dots, 0.0)
    ga = h * (w * residual_scale)
    gg[...] = (ga * upper * (sig * (1.0 + gated * (1.0 - sig)))).astype(bf16)
    gu[...] = (ga * silu).astype(bf16)

    d_gate[0] = mm(st[...], gg[...]).astype(bf16)
    d_up[0] = mm(st[...], gu[...]).astype(bf16)
    d_down[0] = (mm(aw[...].T, grads[...]) * residual_scale).astype(bf16)


def experts(ids, blocks, grads, back, gate_w, up_w):
    vm = pl.BlockSpec(memory_space=pltpu.VMEM)
    shape = jax.ShapeDtypeStruct
    wide = pl.BlockSpec((1, 1536, 256), lambda e, c: (e, 0, c))
    tall = pl.BlockSpec((1, 256, 1536), lambda e, c: (e, c, 0))
    line = pl.BlockSpec((1024, 256), lambda e, c: (0, 2 * e + c))
    return pl.pallas_call(
        experts_body,
        grid=(2, 2),
        out_shape=(
            shape((2, 1536, 512), bf16),
            shape((2, 1536, 512), bf16),
            shape((2, 512, 1536), bf16),
            shape((1024, 1024), bf16),
            shape((1024, 1024), bf16),
            shape((1024, 1024), bf16),
            shape((1024, 128), f32),
        ),
        in_specs=[pl.BlockSpec(memory_space=pltpu.SMEM)] + [vm] * 9 + [line, wide, wide],
        out_specs=(wide, wide, tall, line, line, line, vm),
        scratch_shapes=[
            pltpu.VMEM((1024, 1664), bf16),
            pltpu.VMEM((1536, 1024), bf16),
            pltpu.VMEM((1024, 128), f32),
        ],
        compiler_params=pltpu.CompilerParams(vmem_limit_bytes=60 * MIB),
        cost_estimate=pl.CostEstimate(flops=16_000_000_000, bytes_accessed=34_000_000, transcendentals=1_000_000),
        name="experts",
    )(ids, *blocks, grads, back, gate_w, up_w)


def split_cores(here, value, own, other):
    first = here[1] == 0
    own[0] = jnp.where(first, value[0:128], value[128:256])
    other[0] = jnp.where(first, value[128:256], value[0:128])


def by_chip(here, body, width, name, rows, whole, held, flops):
    out = pl.BlockSpec((1, 128, width), lambda m, here: (m, 0, 0))
    shape = jax.ShapeDtypeStruct((4, 128, width), bf16)
    lines = [
        pl.BlockSpec((256, a.shape[1]), lambda m, here: (m, 0)) for a in rows
    ]
    return pl.pallas_call(
        body,
        grid_spec=pltpu.PrefetchScalarGridSpec(
            num_scalar_prefetch=1,
            grid=(4,),
            in_specs=lines
            + [pl.BlockSpec(memory_space=pltpu.VMEM)] * len(whole)
            + [pl.BlockSpec(memory_space=pl.ANY)] * len(held),
            out_specs=(out, out),
        ),
        out_shape=(shape, shape),
        compiler_params=pltpu.CompilerParams(vmem_limit_bytes=56 * MIB),
        cost_estimate=pl.CostEstimate(flops=flops, bytes_accessed=100_000, transcendentals=0),
        name=name,
    )(here, *rows, *whole, *held)


def back_body(here, gg, gu, routed, gate_w, up_w, *refs):
    own, other = refs[-2:]
    total = mm_nt(gg[:, 0:512], gate_w[0]) + mm_nt(gg[:, 512:1024], gate_w[1])
    total = total + mm_nt(gu[:, 0:512], up_w[0]) + mm_nt(gu[:, 512:1024], up_w[1])
    table = routed[...]
    high = table.astype(bf16).astype(f32)
    low = pltpu.roll(table - high, 16, 1)
    lane = lax.broadcasted_iota(jnp.int32, table.shape, 1)
    tail = jnp.where(lane < 16, high, low)
    split_cores(here, jnp.concatenate([total, tail], axis=1).astype(bf16), own, other)


def experts_back(here, gg, gu, routed, gate_w, up_w, held):
    rows, whole = (gg, gu, routed), (gate_w, up_w)
    return by_chip(here, back_body, 1664, "experts_back", rows, whole, held, 10**6)


def combine_body(here, aw, down_w, own, other):
    total = mm(aw[:, 0:512], down_w[0]) + mm(aw[:, 512:1024], down_w[1])
    split_cores(here, total.astype(bf16), own, other)


def combine(here, aw, down_w):
    return by_chip(here, combine_body, 1536, "combine", (aw,), (down_w,), (), 8 * 10**9)


def widen_body(a, b, c, x, y, z, *refs):
    held, grown, got, sent = refs[0:3], refs[3:6], refs[6], refs[7]
    work = []
    for k, (source, target) in enumerate(((a, x), (b, y), (c, z))):
        half = source.shape[1] // 2
        for e in range(2):
            for i in range(2):
                j = 2 * e + i
                at = pl.ds(half * i, half)
                load = pltpu.make_async_copy(
                    source.at[e, at], held[k].at[j], got.at[4 * k + j]
                )
                store = pltpu.make_async_copy(
                    grown[k].at[j], target.at[e, at], sent.at[4 * k + j]
                )
                load.start()
                work.append((k, j, load, store))
    for k, j, load, store in work:
        load.wait()
        grown[k][j] = held[k][j].astype(f32)
        store.start()
    for _, _, _, store in work:
        store.wait()


def widen(a, b, c):
    hbm = pl.BlockSpec(memory_space=pl.ANY)
    shapes = [(4, v.shape[1] // 2, v.shape[2]) for v in (a, b, c)]
    return pl.pallas_call(
        widen_body,
        out_shape=tuple(jax.ShapeDtypeStruct(v.shape, f32) for v in (a, b, c)),
        in_specs=[hbm] * 3,
        out_specs=(hbm,) * 3,
        scratch_shapes=[pltpu.VMEM(s, bf16) for s in shapes]
        + [pltpu.VMEM(s, f32) for s in shapes]
        + [pltpu.SemaphoreType.DMA((12,)), pltpu.SemaphoreType.DMA((12,))],
        compiler_params=pltpu.CompilerParams(vmem_limit_bytes=56 * MIB),
        cost_estimate=pl.CostEstimate(flops=1_000_000, bytes_accessed=28_000_000, transcendentals=0),
        name="widen",
    )(a, b, c)


def back_rows_body(ids, *refs):
    blocks, (down_w, grads, back) = refs[:8], refs[8:]

    @pl.when(pl.program_id(0) == 0)
    def _():
        for b in range(8):
            grads[pl.ds(pl.multiple_of(ids[b] * 128, 128), 128), :] = blocks[b][...]

    back[...] = mm_nt(grads[...], down_w[0]).astype(bf16)


def back_rows(ids, blocks, down_w):
    vm = pl.BlockSpec(memory_space=pltpu.VMEM)
    shape = jax.ShapeDtypeStruct
    return pl.pallas_call(
        back_rows_body,
        grid=(2,),
        out_shape=(shape((1024, 1536), bf16), shape((1024, 1024), bf16)),
        in_specs=[pl.BlockSpec(memory_space=pltpu.SMEM)]
        + [vm] * 8
        + [pl.BlockSpec((1, 512, 1536), lambda e: (e, 0, 0))],
        out_specs=(vm, pl.BlockSpec((1024, 512), lambda e: (0, e))),
        compiler_params=pltpu.CompilerParams(vmem_limit_bytes=56 * MIB),
        cost_estimate=pl.CostEstimate(flops=8_000_000_000, bytes_accessed=11_000_000, transcendentals=0),
        name="back_rows",
    )(ids, *blocks, down_w)


def weight_body(normed, grad_qkv, mixed, branch, gain_a, gain_b, router, out):
    first = mm(normed[...].T, grad_qkv[...])
    cols = jnp.concatenate([branch[b, :, 192:384] for b in range(8)], axis=0)
    second = mm(mixed[...].T, cols)
    last = jnp.concatenate([first[:, 256:320], second], axis=1)
    zero = jnp.zeros((1, 32), f32)
    for y in range(4):
        rows, lanes = slice(96 * y, 96 * (y + 1)), slice(96 * y, 96 * (y + 1))
        gains = jnp.concatenate(
            [gain_a[:, lanes], zero, gain_b[:, lanes], zero], axis=1
        )
        small = jnp.concatenate([router[:, lanes], jnp.zeros((16, 160), f32)], axis=1)
        row = lax.broadcasted_iota(jnp.int32, (16, 256), 0)
        extra = jnp.where(row == 0, jnp.broadcast_to(gains, (16, 256)), 0.0)
        out[y, 0:96, 0:256] = first[rows, 0:256].astype(bf16)
        out[y, 96:112, 0:256] = small.astype(bf16)
        out[y, 0:96, 256:512] = last[rows].astype(bf16)
        out[y, 96:112, 256:512] = extra.astype(bf16)


def weight_grads(normed, grad_qkv, mixed, branch, gain_a, gain_b, router):
    vm = pl.BlockSpec(memory_space=pltpu.VMEM)
    slab = pl.BlockSpec((1024, 384), lambda i: (0, i))
    flat = pl.BlockSpec((1, 384), lambda i: (0, i))
    return pl.pallas_call(
        weight_body,
        grid=(4,),
        out_shape=jax.ShapeDtypeStruct((16, 112, 512), bf16),
        in_specs=[slab, vm, slab, vm, flat, flat, pl.BlockSpec((16, 384), lambda i: (0, i))],
        out_specs=pl.BlockSpec((4, 112, 512), lambda i: (i, 0, 0)),
        compiler_params=pltpu.CompilerParams(vmem_limit_bytes=56 * MIB),
        cost_estimate=pl.CostEstimate(flops=1_000_000, bytes_accessed=100_000, transcendentals=0),
        name="weight_grads",
    )(normed, grad_qkv, mixed, branch, gain_a, gain_b, router)


def sum_body(pieces, out):
    total = pieces[0].astype(f32)
    for i in range(1, pieces.shape[0]):
        total = total + pieces[i].astype(f32)
    out[...] = total.astype(bf16)


def sum_pieces(pieces):
    vm = pl.BlockSpec(memory_space=pltpu.VMEM)
    return pl.pallas_call(
        sum_body,
        out_shape=jax.ShapeDtypeStruct(pieces.shape[1:], bf16),
        in_specs=[vm],
        out_specs=vm,
        cost_estimate=pl.CostEstimate(flops=1_000_000, bytes_accessed=100_000, transcendentals=0),
        name="sum_pieces",
    )(pieces)


def assemble_body(ids, *refs):
    blocks, (query, key, value, out, gain_a, gain_b, router) = refs[:8], refs[8:]
    total = jnp.zeros((16, 512), f32)
    for m in range(4):
        here, there = blocks[2 * m][...].astype(f32), blocks[2 * m + 1][...].astype(f32)
        total = total + here[96:112] + there[96:112]
        first = ids[2 * m] < ids[2 * m + 1]
        a, b = jnp.where(first, here, there)[0:96], jnp.where(first, there, here)[0:96]
        chip = ids[2 * m] // 2
        wide = pl.ds(pl.multiple_of(chip * 384, 128), 384)
        slim = pl.ds(pl.multiple_of(chip * 128, 128), 128)
        query[:, wide] = jnp.concatenate([a[:, 0:192], b[:, 0:192]], axis=1)
        key[:, slim] = jnp.concatenate([a[:, 192:256], b[:, 192:256]], axis=1)
        value[:, slim] = jnp.concatenate([a[:, 256:320], b[:, 256:320]], axis=1)
        out[:, wide] = jnp.concatenate([a[:, 320:512], b[:, 320:512]], axis=1)
    router[...] = total[:, 0:96]
    gain_a[...] = total[0:1, 256:352]
    gain_b[...] = total[0:1, 384:480]


def assemble(ids, blocks):
    vm = pl.BlockSpec(memory_space=pltpu.VMEM)
    shape = jax.ShapeDtypeStruct
    return pl.pallas_call(
        assemble_body,
        out_shape=(
            shape((96, 1536), f32),
            shape((96, 512), f32),
            shape((96, 512), f32),
            shape((96, 1536), f32),
            shape((1, 96), f32),
            shape((1, 96), f32),
            shape((16, 96), f32),
        ),
        in_specs=[pl.BlockSpec(memory_space=pltpu.SMEM)] + [vm] * 8,
        out_specs=(vm,) * 7,
        cost_estimate=pl.CostEstimate(flops=1_000_000, bytes_accessed=100_000, transcendentals=0),
        name="assemble",
    )(ids, *blocks)


def column(row):
    n = row.shape[1]
    down = lax.broadcasted_iota(jnp.int32, (n, n), 0)
    along = lax.broadcasted_iota(jnp.int32, (n, n), 1)
    return jnp.sum(jnp.where(down == along, row.astype(f32), 0.0), axis=1, keepdims=True)


def pack_body(
    at, w_query, w_key, w_value, gain_a, gain_b, router, tokens, seg, share, sent
):
    first = at[1] == 0
    x = at[0]
    wide = w_query[:, pl.ds(pl.multiple_of(x * 384, 128), 384)].astype(f32)
    slim = pl.ds(pl.multiple_of(x * 128, 128), 128)
    key, value = w_key[:, slim].astype(f32), w_value[:, slim].astype(f32)
    columns = jnp.concatenate(
        [
            jnp.where(first, wide[:, 0:192], wide[:, 192:384]),
            jnp.where(first, key[:, 0:64], key[:, 64:128]),
            jnp.where(first, value[:, 0:64], value[:, 64:128]),
            column(gain_a[...]),
            column(gain_b[...]),
            router[...].astype(f32).T,
            jnp.zeros((96, 46), f32),
        ],
        axis=1,
    ).astype(bf16)
    for i in range(16):
        share[i] = columns
    sent[:, 0:1536] = tokens[...]
    sent[:, 1536:1664] = jnp.broadcast_to(column(seg[...]), (128, 128)).astype(bf16)


def pack(at, w_query, w_key, w_value, gain_a, gain_b, router, tokens, seg):
    vm = pl.BlockSpec(memory_space=pltpu.VMEM)
    shape = jax.ShapeDtypeStruct
    return pl.pallas_call(
        pack_body,
        out_shape=(shape((16, 96, 384), bf16), shape((128, 1664), bf16)),
        in_specs=[pl.BlockSpec(memory_space=pltpu.SMEM)] + [vm] * 8,
        out_specs=(vm,) * 2,
        cost_estimate=pl.CostEstimate(flops=1_000_000, bytes_accessed=2_000_000, transcendentals=0),
        name="pack",
    )(at, w_query, w_key, w_value, gain_a, gain_b, router, tokens, seg)


def project_out_body(mixed, w_out, tokens, narrow, named, sent, hidden, gates, mx):
    for p in range(4):
        mx[:, 384 * p : 384 * (p + 1)] = jnp.concatenate(
            [mixed[2 * p, :, 0:192], mixed[2 * p + 1, :, 0:192]], axis=1
        )
    value = tokens[...].astype(f32) + residual_scale * mm(mx[...], w_out[...])
    hidden[...] = value
    r = lax.rsqrt(jnp.mean(value * value, axis=1, keepdims=True) + eps)
    gain = narrow[0:16, :].astype(f32)[1:2]
    second = (value * r * gain).astype(bf16)
    sent[:, 0:1536] = second
    logits = mm_nt(second, narrow[...])
    logits = pltpu.roll(jnp.concatenate([logits, jnp.zeros_like(logits)], axis=1), 126, 1)
    on = named[...] > 0.5
    logits = jnp.where(on, logits, -1e30)
    top = jnp.max(logits, axis=1, keepdims=True)
    e = jnp.where(on, jnp.exp(logits - top), 0.0)
    g = e / jnp.sum(e, axis=1, keepdims=True)
    gates[...] = g
    high = g.astype(bf16)
    low = pltpu.roll(g - high.astype(f32), 16, 1)
    lane = lax.broadcasted_iota(jnp.int32, g.shape, 1)
    sent[:, 1536:1664] = jnp.where(lane < 16, g, low).astype(bf16)


def project_out(mixed, w_out, tokens, narrow, named):
    vm = pl.BlockSpec(memory_space=pltpu.VMEM)
    shape = jax.ShapeDtypeStruct
    return pl.pallas_call(
        project_out_body,
        out_shape=(
            shape((128, 1664), bf16),
            shape((128, 1536), f32),
            shape((128, 128), f32),
            shape((128, 1536), bf16),
        ),
        in_specs=[vm] * 5,
        out_specs=(vm,) * 4,
        compiler_params=pltpu.CompilerParams(vmem_limit_bytes=56 * MIB),
        cost_estimate=pl.CostEstimate(flops=4_000_000_000, bytes_accessed=8_000_000, transcendentals=0),
        name="project_out",
    )(mixed, w_out, tokens, narrow, named)


def middle_body(
    w_out, sums, grads, hidden, gates, narrow, _, grad_hidden, heads, grad_gain, grad_router, gx
):
    gain = narrow[0:16, :].astype(f32)[1:2]
    total = sums[0].astype(f32)
    for i in range(1, 4):
        total = total + sums[i].astype(f32)
    value = hidden[...]
    r = lax.rsqrt(jnp.mean(value * value, axis=1, keepdims=True) + eps)
    second = (value * r * gain).astype(bf16)
    g = gates[...]
    table = total[:, 1536:1664]
    lane = lax.broadcasted_iota(jnp.int32, g.shape, 1)
    table = jnp.where(lane < 16, table + pltpu.roll(table, 112, 1), 0.0)
    logits = (g * (table - jnp.sum(g * table, axis=1, keepdims=True))).astype(bf16)
    grad_router[...] = mm(logits.astype(f32).T.astype(bf16), second)[0:16]
    router = pltpu.roll(logits.astype(f32), 2, 1)[:, 0:64].astype(bf16)
    grad_second = total[:, 0:1536] + mm(router, narrow[...])
    grad_gain[...] = jnp.sum(grad_second * value * r, axis=0, keepdims=True)
    scaled = grad_second * gain
    gh = (
        grads[...].astype(f32)
        + r * scaled
        - value * (r * r * r) * jnp.mean(value * scaled, axis=1, keepdims=True)
    )
    grad_hidden[...] = gh
    low = (residual_scale * gh).astype(bf16)
    gx[...] = mm_nt(low, w_out[...])
    low = low.astype(f32)
    for j in range(8):
        cols = slice(192 * j, 192 * (j + 1))
        heads[j] = jnp.concatenate([gx[:, cols], low[:, cols]], axis=1).astype(bf16)


def middle(w_out, sums, grads, hidden, gates, narrow, held):
    vm = pl.BlockSpec(memory_space=pltpu.VMEM)
    shape = jax.ShapeDtypeStruct
    return pl.pallas_call(
        middle_body,
        out_shape=(
            shape((128, 1536), f32),
            shape((8, 128, 384), bf16),
            shape((1, 1536), f32),
            shape((16, 1536), f32),
        ),
        in_specs=[vm] * 6 + [pl.BlockSpec(memory_space=pl.ANY)],
        out_specs=(vm,) * 4,
        scratch_shapes=[pltpu.VMEM((128, 1536), f32)],
        compiler_params=pltpu.CompilerParams(vmem_limit_bytes=56 * MIB),
        cost_estimate=pl.CostEstimate(flops=1_000_000, bytes_accessed=100_000, transcendentals=0),
        name="middle",
    )(w_out, sums, grads, hidden, gates, narrow, held)


def shift(value, axis, amount):
    size = lax.axis_size(axis)
    return lax.ppermute(value, axis, [((i + amount) % size, i) for i in range(size)])


def swap(value):
    return lax.ppermute(value, "core", [(0, 1), (1, 0)])


def tied(*values):
    return lax.optimization_barrier(values)


def gather_x(block):
    return [block] + [shift(block, "x", m) for m in (1, 2, 3)]


def both_cores(blocks):
    return [each for block in blocks for each in (block, swap(block))]


def near_sum(own, other):
    return (own.astype(f32) + swap(other).astype(f32)).astype(bf16)


def exchange(near):
    return lax.all_to_all(near, "x", 0, 0, tiled=True)


def exchange_apart(near):
    x = lax.axis_index("x")
    pieces = [lax.dynamic_index_in_dim(near, (x + m) % 4, 0, False) for m in range(4)]
    return [pieces[0]] + [shift(pieces[m], "x", -m) for m in (2, 1, 3)]


def total_of(terms):
    total = terms[0].astype(f32)
    for term in terms[1:]:
        total = total + term.astype(f32)
    return total


def inverse_rms(values):
    return lax.rsqrt(jnp.mean(values * values, axis=-1, keepdims=True) + eps)


def per_device(
    tokens,
    segments,
    routes,
    gain_attn,
    w_query,
    w_key,
    w_value,
    w_out,
    gain_moe,
    w_router,
    expert_gate,
    expert_up,
    expert_down,
    out_grad,
):
    rows, width = tokens.shape
    parts = 8
    seq = rows * parts
    x, core = lax.axis_index("x"), lax.axis_index("core")
    me = x * 2 + core
    z = lax.axis_index("z")
    at = jnp.stack([x, core, z])

    share, sent = pack(
        at,
        w_query,
        w_key,
        w_value,
        gain_attn[None, :],
        gain_moe[None, :],
        w_router.T,
        tokens,
        segments[None, :],
    )
    out_all = lax.all_gather(w_out, ("z", "y"), axis=0, tiled=True)
    qkv_w = lax.all_to_all(share, ("z", "y"), 0, 0, tiled=True).reshape(width, 384)
    far = gather_x(sent)
    far[1], grads_sent = tied(far[1], out_grad)
    blocks = both_cores(far)
    grads_far = gather_x(grads_sent)
    lane = jnp.arange(128, dtype=jnp.int32)

    chips = (x + jnp.arange(4, dtype=jnp.int32)) % 4
    cores = jnp.bitwise_xor(core, jnp.arange(2, dtype=jnp.int32))
    ids = (chips[:, None] * 2 + cores[None, :]).reshape(parts)
    place = jnp.arange(seq, dtype=jnp.int32)
    freq = rope_base ** (
        -(jnp.arange(128, dtype=jnp.int32) % 32).astype(f32) * 2.0 / HEAD_DIM
    )[None, :]
    angles = place.astype(f32)[:, None] * freq

    named = jnp.any(routes[:, :, None] == lane[None, None, :], axis=1).astype(f32)

    normed, narrow, gain_one, q01, q2k, val, lse, cos, sin, starts, mixed_head = attend_forward(
        ids, blocks, qkv_w, jnp.cos(angles), jnp.sin(angles), freq, named
    )
    mixed_head, *grads_far = tied(mixed_head, *grads_far)
    grad_blocks = both_cores(grads_far)
    mixed = lax.all_to_all(mixed_head, ("x", "core"), 0, 0, tiled=True)
    sent_two, hidden, gates, mixed = project_out(
        mixed, out_all, tokens, narrow, named
    )
    far_two = gather_x(sent_two)
    grad_all, back = back_rows(ids, grad_blocks, expert_down)
    twins = [swap(block) for block in far_two]
    mixed, back, *far_two = tied(mixed, back, *far_two)
    second_blocks = [each for pair in zip(far_two, twins) for each in pair]
    mixed_all = lax.all_gather(mixed, ("x", "core"), axis=0, tiled=True)

    grad_w_gate, grad_w_up, grad_w_down, weighted, grad_gate_pre, grad_up_pre, routed = experts(
        ids, second_blocks, grad_all, back, expert_gate, expert_up
    )
    sums = lax.psum((grad_w_gate, grad_w_up, grad_w_down), ("z", "y"))
    own, other = experts_back(
        at, grad_gate_pre, grad_up_pre, routed, expert_gate, expert_up, ()
    )
    near = near_sum(own, other)
    near, weighted = tied(near, weighted)
    terms = exchange(near)
    own_out, other_out = combine(at, weighted, expert_down)

    grad_hidden, heads, grad_gain_two, grad_router = middle(
        out_all, terms, out_grad, hidden, gates, narrow, own_out
    )
    grad_heads = lax.all_to_all(heads, ("x", "core"), 0, 0, tiled=True)
    grad_qkv, own, other, grad_gain_one = attend_backward(
        at, grad_heads, q01, q2k, val, lse, cos, sin, starts, normed, qkv_w, gain_one
    )
    table = weight_grads(
        normed, grad_qkv, mixed_all, grad_heads, grad_gain_one, grad_gain_two, grad_router
    )
    own_out, table = tied(own_out, table)
    near_out = near_sum(own_out, other_out)
    output = (hidden + residual_scale * total_of(exchange_apart(near_out))).astype(bf16)
    normed_mine = total_of(exchange_apart(near_sum(own, other)))
    inputs = tokens.astype(f32)
    scale_one = inverse_rms(inputs)
    scaled_one = normed_mine * gain_one
    grad_inputs = (
        grad_hidden
        + scale_one * scaled_one
        - inputs * scale_one**3 * jnp.mean(inputs * scaled_one, axis=-1, keepdims=True)
    )

    pieces = lax.all_to_all(table, ("z", "y"), 0, 0, tiled=True)
    pieces, output, grad_inputs = tied(pieces, output, grad_inputs)
    lines = both_cores(gather_x(sum_pieces(pieces)))
    grad_gate, grad_up, grad_down = widen(*sums)
    grad_q, grad_k, grad_v, grad_o, gain_a, gain_b, router = assemble(ids, lines)
    return (
        output,
        grad_inputs,
        gain_a.reshape(-1),
        grad_q,
        grad_k,
        grad_v,
        grad_o,
        gain_b.reshape(-1),
        router.T,
        grad_gate,
        grad_up,
        grad_down,
    )


def solution(mesh):
    fine = Mesh(mesh.devices.reshape(4, 4, 4, 2), ("z", "y", "x", "core"))
    dp, expert, both = ("z", "y"), ("x", "core"), ("z", "y", "x", "core")
    placed = (
        P(both, None),
        P(both),
        P(both, None),
        P(dp),
        P(dp, None),
        P(dp, None),
        P(dp, None),
        P(dp, None),
        P(dp),
        P(dp, None),
        P(expert, None, None),
        P(expert, None, None),
        P(expert, None, None),
    )
    return jax.shard_map(
        per_device,
        mesh=fine,
        in_specs=placed + (P(both, None),),
        out_specs=(P(both, None),) * 2 + placed[3:],
        check_vma=False,
    )
```

```python
import jax
import jax.numpy as jnp
from jax import lax
from jax.experimental import pallas as pl
from jax.experimental.pallas import tpu as pltpu
from jax.sharding import Mesh, PartitionSpec as P

HEADS = 24
KV_HEADS = 8
HEAD_DIM = 64
GROUP = HEADS // KV_HEADS
TOP = 8
EXPERTS = 16

eps = 1e-06
residual_scale = 0.22
score_scale = 0.015625
rope_base = 10000.0
doc_slots = 3
MIB = 1024 * 1024

bf16 = jnp.bfloat16
f32 = jnp.float32


def mm(a, b):
    return lax.dot_general(a, b, (((1,), (0,)), ((), ())), preferred_element_type=f32)


def mm_nt(a, b):
    return lax.dot_general(a, b, (((1,), (1,)), ((), ())), preferred_element_type=f32)


def low_half(value):
    lane = lax.broadcasted_iota(jnp.int32, value.shape, 1)
    return jnp.where(lane < 64, value, jnp.zeros_like(value))


def high_half(value):
    lane = lax.broadcasted_iota(jnp.int32, value.shape, 1)
    return jnp.where(lane >= 64, value, jnp.zeros_like(value))


def quarter(value):
    lane = lax.broadcasted_iota(jnp.int32, value.shape, 1)
    up, down = pltpu.roll(value, 96, 1), pltpu.roll(value, 32, 1)
    return jnp.where(lane % 64 < 32, -up, down)


def visible(chunk, starts):
    keys = 256 * (chunk + 1)
    place = (256 * chunk + lax.broadcasted_iota(jnp.int32, (1, 256), 1)).astype(f32)
    one = jnp.concatenate([starts[0:1], starts[0:1]], axis=1)
    two = jnp.concatenate([starts[1:2], starts[1:2]], axis=1)
    begin = jnp.where(place >= two, two, jnp.where(place >= one, one, jnp.zeros_like(one)))
    at = lax.broadcasted_iota(jnp.int32, (keys, 256), 0).astype(f32)
    return (at <= place) & (at >= begin)


def attend_body(ids, *refs):
    blocks = refs[:8]
    (w, cos_t, sin_t, freq, _, normed, narrow, gain_row, q01, q2k, val, lse, cos_o, sin_o, starts, mixed,
     ka, kb, vt) = refs[8:]
    one = jnp.zeros((1, 128), f32)
    two = jnp.zeros((1, 128), f32)
    for b in range(8):
        seg = blocks[b][:, 1536:1664].astype(f32)
        one = one + jnp.sum(jnp.where(seg < 0.5, 1.0, 0.0), axis=0, keepdims=True)
        two = two + jnp.sum(jnp.where(seg < 1.5, 1.0, 0.0), axis=0, keepdims=True)
    starts[...] = jnp.concatenate([one, two, jnp.zeros((6, 128), f32)], axis=0)
    begin_rows = jnp.concatenate([one, two, jnp.zeros((6, 128), f32)], axis=0)
    angles = begin_rows * freq[...]
    cos_b, sin_b = jnp.cos(angles), jnp.sin(angles)
    last = w[:, 256:384].astype(f32).T
    narrow[...] = last[64:128].astype(bf16)
    gain = last[64:65]
    gain_row[...] = gain
    for b in range(8):
        x = blocks[b][:, 0:1536].astype(f32)
        r = lax.rsqrt(jnp.mean(x * x, axis=1, keepdims=True) + eps)
        at = pl.ds(pl.multiple_of(ids[b] * 128, 128), 128)
        normed[at, :] = (x * r * gain).astype(bf16)
    def project(c, carry):
        at = pl.ds(pl.multiple_of(c * 256, 256), 256)
        u = mm(normed[at, :], w[...])
        place = (lax.broadcasted_iota(jnp.int32, (256, 128), 0) + c * 256).astype(f32)
        in_two, in_one = place >= two, place >= one
        cb = jnp.where(in_two, cos_b[1:2], jnp.where(in_one, cos_b[0:1], 1.0))
        sb = jnp.where(in_two, sin_b[1:2], jnp.where(in_one, sin_b[0:1], 0.0))
        ct, st = cos_t[at, :], sin_t[at, :]
        cc = ct * cb + st * sb
        ss = st * cb - ct * sb
        cos_o[at, :] = cc
        sin_o[at, :] = ss
        a, bq, v = u[:, 0:128], u[:, 128:256], u[:, 256:384]
        a = a * cc + quarter(a) * ss
        bq = bq * cc + quarter(bq) * ss
        v = low_half(v)
        q01[at, :] = a.astype(bf16)
        q2k[at, :] = bq.astype(bf16)
        val[at, :] = v.astype(bf16)
        k = high_half(bq) * score_scale
        kb[at, :] = k.astype(bf16)
        ka[at, :] = pltpu.roll(k, 64, 1).astype(bf16)
        vt[:, at] = v.T.astype(bf16)
        return carry

    lax.fori_loop(0, 4, project, 0)

    for c in range(4):
        at, seen = slice(256 * c, 256 * (c + 1)), slice(0, 256 * (c + 1))
        allowed = visible(c, starts)
        outs = []
        for h in range(3):
            q = q2k[at, :] if h == 2 else q01[at, :]
            kk = kb if h == 1 else ka
            s = mm_nt(kk[seen, :], q)
            s = jnp.where(allowed, s, -1e30)
            top = jnp.max(s, axis=0, keepdims=True)
            p = jnp.exp(s - top)
            total = jnp.sum(p, axis=0, keepdims=True)
            lse[h : h + 1, at] = top + jnp.log(total)
            pb = (p * (1.0 / total)).astype(bf16)
            outs.append(mm(vt[0:64, seen], pb))
        out = jnp.concatenate(outs + [jnp.zeros((64, 256), f32)], axis=0).T.astype(bf16)
        mixed[2 * c] = out[0:128]
        mixed[2 * c + 1] = out[128:256]


def attend_forward(ids, blocks, w, cos_t, sin_t, freq, held):
    vm = pl.BlockSpec(memory_space=pltpu.VMEM)
    shape = jax.ShapeDtypeStruct
    return pl.pallas_call(
        attend_body,
        out_shape=(
            shape((1024, 1536), bf16),
            shape((64, 1536), bf16),
            shape((1, 1536), f32),
            shape((1024, 128), bf16),
            shape((1024, 128), bf16),
            shape((1024, 128), bf16),
            shape((8, 1024), f32),
            shape((1024, 128), f32),
            shape((1024, 128), f32),
            shape((8, 128), f32),
            shape((8, 128, 256), bf16),
        ),
        in_specs=[pl.BlockSpec(memory_space=pltpu.SMEM)]
        + [vm] * 12
        + [pl.BlockSpec(memory_space=pl.ANY)],
        out_specs=(vm,) * 11,
        scratch_shapes=[
            pltpu.VMEM((1024, 128), bf16),
            pltpu.VMEM((1024, 128), bf16),
            pltpu.VMEM((128, 1024), bf16),
        ],
        compiler_params=pltpu.CompilerParams(vmem_limit_bytes=56 * MIB),
        cost_estimate=pl.CostEstimate(flops=14_000_000_000, bytes_accessed=12_000_000, transcendentals=3_200_000),
        name="attend_forward",
    )(ids, *blocks, w, cos_t, sin_t, freq, held)


def attend_back_body(
    here, w, gm, q01, q2k, val, lse, cc, ss, starts, normed_hbm, gain,
    mixed_hbm, gain_b, router, own_hbm, other_hbm, table,
    ka, kb, vb, kt, do01, do2, dk, dv, d01, dq2, normed, own, other, got, sent, dqkv, mixed,
):
    load = pltpu.make_async_copy(normed_hbm, normed, got.at[0])
    load_mixed = pltpu.make_async_copy(mixed_hbm, mixed, got.at[1])
    load.start()
    load_mixed.start()
    k = high_half(q2k[...].astype(f32)) * score_scale
    kb[...] = k.astype(bf16)
    k_low = pltpu.roll(k, 64, 1)
    ka[...] = k_low.astype(bf16)
    kt[...] = k_low.T.astype(bf16)
    vb[...] = pltpu.roll(val[...].astype(f32), 64, 1).astype(bf16)
    for b in range(8):
        do01[b * 128 : (b + 1) * 128, :] = gm[b, :, 0:128]
        do2[b * 128 : (b + 1) * 128, :] = low_half(gm[b, :, 128:256])
    dk[...] = jnp.zeros_like(dk)
    dv[...] = jnp.zeros_like(dv)

    for c in range(4):
        at, seen = slice(256 * c, 256 * (c + 1)), slice(0, 256 * (c + 1))
        allowed = visible(c, starts)
        qa, qb = q01[at, :], q2k[at, :]
        da, db = do01[at, :], do2[at, :]
        outs = []
        for h in range(3):
            q = qb if h == 2 else qa
            kk = kb if h == 1 else ka
            s = mm_nt(kk[seen, :], q)
            p = jnp.where(allowed, jnp.exp(s - lse[h : h + 1, at]), 0.0)
            d = db if h == 2 else da
            vv = vb if h == 1 else val
            dp = mm_nt(vv[seen, :], d)
            delta = jnp.sum(p * dp, axis=0, keepdims=True)
            ds = (p * (dp - delta)).astype(bf16)
            outs.append(mm(kt[0:64, seen], ds))
            half = high_half if h == 1 else low_half
            dk[seen, :] += mm(ds, half(q))
            dv[seen, :] += mm(p.astype(bf16), half(d))
        out = jnp.concatenate(outs + [jnp.zeros((64, 256), f32)], axis=0).T
        d01[at, :] = out[:, 0:128]
        dq2[at, :] = out[:, 128:256]

    load.wait()

    def store(c):
        return (
            pltpu.make_async_copy(own.at[c], own_hbm.at[c], sent.at[0, c]),
            pltpu.make_async_copy(other.at[c], other_hbm.at[c], sent.at[1, c]),
        )

    def finish(c, total):
        at = pl.ds(pl.multiple_of(c * 256, 256), 256)
        dkk = dk[at, :]
        dkk = (dkk + pltpu.roll(dkk, 64, 1)) * score_scale
        dvv = dv[at, :]
        dvv = low_half(dvv + pltpu.roll(dvv, 64, 1))
        a = d01[at, :]
        lane = lax.broadcasted_iota(jnp.int32, (256, 128), 1)
        b = jnp.where(lane < 64, dq2[at, :], dkk)
        cos, sin = cc[at, :], ss[at, :]
        a = a * cos - quarter(a) * sin
        b = b * cos - quarter(b) * sin
        row = jnp.concatenate([a, b, dvv], axis=1).astype(bf16)
        dqkv[at, :] = row
        whole = mm_nt(row, w[...])
        total = total + jnp.sum(whole * normed[at, :].astype(f32), axis=0, keepdims=True)
        low = whole.astype(bf16)
        own[c] = jnp.where(here[1] == 0, low[0:128], low[128:256])
        other[c] = jnp.where(here[1] == 0, low[128:256], low[0:128])
        for copy in store(c):
            copy.start()
        return total

    total = lax.fori_loop(0, 4, finish, jnp.zeros((1, 1536), f32))
    gain_a = total / gain[...]
    load_mixed.wait()
    branch = jnp.concatenate([gm[b, :, 192:384] for b in range(8)], axis=0)
    row = lax.broadcasted_iota(jnp.int32, (16, 256), 0)
    for z in range(4):
        cols = slice(384 * z, 384 * (z + 1))
        first = mm(normed[:, cols].T, dqkv[...])
        second = mm(mixed[:, cols].T, branch)
        last = jnp.concatenate([first[:, 256:320], second], axis=1)
        for y in range(4):
            here_rows = slice(96 * y, 96 * (y + 1))
            lanes = slice(384 * z + 96 * y, 384 * z + 96 * (y + 1))
            zero = jnp.zeros((1, 32), f32)
            gains = jnp.concatenate([gain_a[:, lanes], zero, gain_b[:, lanes], zero], axis=1)
            small = jnp.concatenate([router[:, lanes], jnp.zeros((16, 160), f32)], axis=1)
            extra = jnp.where(row == 0, jnp.broadcast_to(gains, (16, 256)), 0.0)
            chunk = table.at[4 * z + y]
            chunk[0:96, 0:256] = first[here_rows, 0:256].astype(bf16)
            chunk[96:112, 0:256] = small.astype(bf16)
            chunk[0:96, 256:512] = last[here_rows].astype(bf16)
            chunk[96:112, 256:512] = extra.astype(bf16)
    for c in range(4):
        for copy in store(c):
            copy.wait()


def attend_backward(
    here, gm, q01, q2k, val, lse, cc, ss, starts, normed, w, gain, mixed, gain_b, router
):
    vm, hbm = pl.BlockSpec(memory_space=pltpu.VMEM), pl.BlockSpec(memory_space=pl.ANY)
    rows = pltpu.VMEM((4, 128, 1536), bf16)
    whole = pltpu.VMEM((1024, 1536), bf16)
    shape = jax.ShapeDtypeStruct
    half = pltpu.VMEM((1024, 128), bf16)
    full = pltpu.VMEM((1024, 128), f32)
    return pl.pallas_call(
        attend_back_body,
        out_shape=(
            shape((4, 128, 1536), bf16),
            shape((4, 128, 1536), bf16),
            shape((16, 112, 512), bf16),
        ),
        in_specs=[pl.BlockSpec(memory_space=pltpu.SMEM)] + [vm] * 9 + [hbm, vm, hbm, vm, vm],
        out_specs=(hbm, hbm, vm),
        scratch_shapes=[half, half, half, pltpu.VMEM((128, 1024), bf16), half, half]
        + [full, full, full, full, whole, rows, rows]
        + [pltpu.SemaphoreType.DMA((2,)), pltpu.SemaphoreType.DMA((2, 4))]
        + [pltpu.VMEM((1024, 384), bf16), whole],
        compiler_params=pltpu.CompilerParams(vmem_limit_bytes=56 * MIB),
        cost_estimate=pl.CostEstimate(flops=1_000_000, bytes_accessed=100_000, transcendentals=0),
        name="attend_backward",
    )(here, w, gm, q01, q2k, val, lse, cc, ss, starts, normed, gain, mixed, gain_b, router)


def experts_body(ids, *refs):
    blocks = refs[:8]
    (grads, back, gate_w, up_w, d_gate, d_up, d_down, aw, gg, gu, routed, second, st, col) = refs[8:]
    e, c = pl.program_id(0), pl.program_id(1)
    first = (e == 0) & (c == 0)

    @pl.when(first)
    def _():
        for b in range(8):
            second[pl.ds(pl.multiple_of(ids[b] * 128, 128), 128), :] = blocks[b][...]
        for b in range(8):
            at = slice(128 * b, 128 * (b + 1))
            st[:, at] = second[at, 0:1536].T
        routed[...] = jnp.zeros_like(routed)

    @pl.when(c == 0)
    def _():
        lane = lax.broadcasted_iota(jnp.int32, (128, 128), 1)
        name = 2 * ids[0] + e
        hit = (lane == name) | (lane == name + 16)
        for b in range(8):
            at = slice(128 * b, 128 * (b + 1))
            table = second[at, 1536:1664].astype(f32)
            w = jnp.sum(jnp.where(hit, table, 0.0), axis=1, keepdims=True)
            col[at, :] = jnp.broadcast_to(w, (128, 128))

    x = second[:, 0:1536]
    gated = mm(x, gate_w[0])
    upper = mm(x, up_w[0])
    h = back[...].astype(f32)
    w = jnp.concatenate([col[...]] * 2, axis=1)
    sig = 1.0 / (1.0 + jnp.exp(-gated))
    silu = gated * sig
    act = silu * upper
    aw[...] = (act * w).astype(bf16)
    dots = residual_scale * jnp.sum(act * h, axis=1, keepdims=True)
    lane = lax.broadcasted_iota(jnp.int32, (1024, 128), 1)
    routed[...] += jnp.where(lane == 2 * ids[0] + e, dots, 0.0)
    ga = h * (w * residual_scale)
    gg[...] = (ga * upper * (sig * (1.0 + gated * (1.0 - sig)))).astype(bf16)
    gu[...] = (ga * silu).astype(bf16)

    d_gate[0] = mm(st[...], gg[...]).astype(bf16)
    d_up[0] = mm(st[...], gu[...]).astype(bf16)
    d_down[0] = (mm(aw[...].T, grads[...]) * residual_scale).astype(bf16)


def experts(ids, blocks, grads, back, gate_w, up_w):
    vm = pl.BlockSpec(memory_space=pltpu.VMEM)
    shape = jax.ShapeDtypeStruct
    wide = pl.BlockSpec((1, 1536, 256), lambda e, c: (e, 0, c))
    tall = pl.BlockSpec((1, 256, 1536), lambda e, c: (e, c, 0))
    line = pl.BlockSpec((1024, 256), lambda e, c: (0, 2 * e + c))
    return pl.pallas_call(
        experts_body,
        grid=(2, 2),
        out_shape=(
            shape((2, 1536, 512), bf16),
            shape((2, 1536, 512), bf16),
            shape((2, 512, 1536), bf16),
            shape((1024, 1024), bf16),
            shape((1024, 1024), bf16),
            shape((1024, 1024), bf16),
            shape((1024, 128), f32),
        ),
        in_specs=[pl.BlockSpec(memory_space=pltpu.SMEM)] + [vm] * 9 + [line, wide, wide],
        out_specs=(wide, wide, tall, line, line, line, vm),
        scratch_shapes=[
            pltpu.VMEM((1024, 1664), bf16),
            pltpu.VMEM((1536, 1024), bf16),
            pltpu.VMEM((1024, 128), f32),
        ],
        compiler_params=pltpu.CompilerParams(vmem_limit_bytes=60 * MIB),
        cost_estimate=pl.CostEstimate(flops=16_000_000_000, bytes_accessed=34_000_000, transcendentals=1_000_000),
        name="experts",
    )(ids, *blocks, grads, back, gate_w, up_w)


def split_cores(here, value, own, other):
    first = here[1] == 0
    own[0] = jnp.where(first, value[0:128], value[128:256])
    other[0] = jnp.where(first, value[128:256], value[0:128])


def by_chip(here, body, width, name, rows, whole, held, flops):
    out = pl.BlockSpec((1, 128, width), lambda m, here: (m, 0, 0))
    shape = jax.ShapeDtypeStruct((4, 128, width), bf16)
    lines = [
        pl.BlockSpec((256, a.shape[1]), lambda m, here: (m, 0)) for a in rows
    ]
    return pl.pallas_call(
        body,
        grid_spec=pltpu.PrefetchScalarGridSpec(
            num_scalar_prefetch=1,
            grid=(4,),
            in_specs=lines
            + [pl.BlockSpec(memory_space=pltpu.VMEM)] * len(whole)
            + [pl.BlockSpec(memory_space=pl.ANY)] * len(held),
            out_specs=(out, out),
        ),
        out_shape=(shape, shape),
        compiler_params=pltpu.CompilerParams(vmem_limit_bytes=56 * MIB),
        cost_estimate=pl.CostEstimate(flops=flops, bytes_accessed=100_000, transcendentals=0),
        name=name,
    )(here, *rows, *whole, *held)


def back_body(here, gg, gu, routed, gate_w, up_w, *refs):
    own, other = refs[-2:]
    total = mm_nt(gg[:, 0:512], gate_w[0]) + mm_nt(gg[:, 512:1024], gate_w[1])
    total = total + mm_nt(gu[:, 0:512], up_w[0]) + mm_nt(gu[:, 512:1024], up_w[1])
    table = routed[...]
    high = table.astype(bf16).astype(f32)
    low = pltpu.roll(table - high, 16, 1)
    lane = lax.broadcasted_iota(jnp.int32, table.shape, 1)
    tail = jnp.where(lane < 16, high, low)
    split_cores(here, jnp.concatenate([total, tail], axis=1).astype(bf16), own, other)


def experts_back(here, gg, gu, routed, gate_w, up_w, held):
    rows, whole = (gg, gu, routed), (gate_w, up_w)
    return by_chip(here, back_body, 1664, "experts_back", rows, whole, held, 10**6)


def combine_body(here, aw, down_w, own, other):
    total = mm(aw[:, 0:512], down_w[0]) + mm(aw[:, 512:1024], down_w[1])
    split_cores(here, total.astype(bf16), own, other)


def combine(here, aw, down_w):
    return by_chip(here, combine_body, 1536, "combine", (aw,), (down_w,), (), 8 * 10**9)


def widen_body(a, b, c, x, y, z, *refs):
    held, grown, got, sent = refs[0:3], refs[3:6], refs[6], refs[7]
    work = []
    for k, (source, target) in enumerate(((a, x), (b, y), (c, z))):
        half = source.shape[1] // 2
        for e in range(2):
            for i in range(2):
                j = 2 * e + i
                at = pl.ds(half * i, half)
                load = pltpu.make_async_copy(
                    source.at[e, at], held[k].at[j], got.at[4 * k + j]
                )
                store = pltpu.make_async_copy(
                    grown[k].at[j], target.at[e, at], sent.at[4 * k + j]
                )
                load.start()
                work.append((k, j, load, store))
    for k, j, load, store in work:
        load.wait()
        grown[k][j] = held[k][j].astype(f32)
        store.start()
    for _, _, _, store in work:
        store.wait()


def widen(a, b, c):
    hbm = pl.BlockSpec(memory_space=pl.ANY)
    shapes = [(4, v.shape[1] // 2, v.shape[2]) for v in (a, b, c)]
    return pl.pallas_call(
        widen_body,
        out_shape=tuple(jax.ShapeDtypeStruct(v.shape, f32) for v in (a, b, c)),
        in_specs=[hbm] * 3,
        out_specs=(hbm,) * 3,
        scratch_shapes=[pltpu.VMEM(s, bf16) for s in shapes]
        + [pltpu.VMEM(s, f32) for s in shapes]
        + [pltpu.SemaphoreType.DMA((12,)), pltpu.SemaphoreType.DMA((12,))],
        compiler_params=pltpu.CompilerParams(vmem_limit_bytes=56 * MIB),
        cost_estimate=pl.CostEstimate(flops=1_000_000, bytes_accessed=28_000_000, transcendentals=0),
        name="widen",
    )(a, b, c)


def back_rows_body(ids, *refs):
    blocks, (down_w, grads, back) = refs[:8], refs[8:]

    @pl.when(pl.program_id(0) == 0)
    def _():
        for b in range(8):
            grads[pl.ds(pl.multiple_of(ids[b] * 128, 128), 128), :] = blocks[b][...]

    back[...] = mm_nt(grads[...], down_w[0]).astype(bf16)


def back_rows(ids, blocks, down_w):
    vm = pl.BlockSpec(memory_space=pltpu.VMEM)
    shape = jax.ShapeDtypeStruct
    return pl.pallas_call(
        back_rows_body,
        grid=(2,),
        out_shape=(shape((1024, 1536), bf16), shape((1024, 1024), bf16)),
        in_specs=[pl.BlockSpec(memory_space=pltpu.SMEM)]
        + [vm] * 8
        + [pl.BlockSpec((1, 512, 1536), lambda e: (e, 0, 0))],
        out_specs=(vm, pl.BlockSpec((1024, 512), lambda e: (0, e))),
        compiler_params=pltpu.CompilerParams(vmem_limit_bytes=56 * MIB),
        cost_estimate=pl.CostEstimate(flops=8_000_000_000, bytes_accessed=11_000_000, transcendentals=0),
        name="back_rows",
    )(ids, *blocks, down_w)


def sum_body(pieces, out):
    total = pieces[0].astype(f32)
    for i in range(1, pieces.shape[0]):
        total = total + pieces[i].astype(f32)
    out[...] = total.astype(bf16)


def sum_pieces(pieces):
    vm = pl.BlockSpec(memory_space=pltpu.VMEM)
    return pl.pallas_call(
        sum_body,
        out_shape=jax.ShapeDtypeStruct(pieces.shape[1:], bf16),
        in_specs=[vm],
        out_specs=vm,
        cost_estimate=pl.CostEstimate(flops=1_000_000, bytes_accessed=100_000, transcendentals=0),
        name="sum_pieces",
    )(pieces)


def assemble_body(ids, *refs):
    blocks, (query, key, value, out, gain_a, gain_b, router) = refs[:8], refs[8:]
    total = jnp.zeros((16, 512), f32)
    for m in range(4):
        here, there = blocks[2 * m][...].astype(f32), blocks[2 * m + 1][...].astype(f32)
        total = total + here[96:112] + there[96:112]
        first = ids[2 * m] < ids[2 * m + 1]
        a, b = jnp.where(first, here, there)[0:96], jnp.where(first, there, here)[0:96]
        chip = ids[2 * m] // 2
        wide = pl.ds(pl.multiple_of(chip * 384, 128), 384)
        slim = pl.ds(pl.multiple_of(chip * 128, 128), 128)
        query[:, wide] = jnp.concatenate([a[:, 0:192], b[:, 0:192]], axis=1)
        key[:, slim] = jnp.concatenate([a[:, 192:256], b[:, 192:256]], axis=1)
        value[:, slim] = jnp.concatenate([a[:, 256:320], b[:, 256:320]], axis=1)
        out[:, wide] = jnp.concatenate([a[:, 320:512], b[:, 320:512]], axis=1)
    router[...] = total[:, 0:96]
    gain_a[...] = total[0:1, 256:352]
    gain_b[...] = total[0:1, 384:480]


def assemble(ids, blocks):
    vm = pl.BlockSpec(memory_space=pltpu.VMEM)
    shape = jax.ShapeDtypeStruct
    return pl.pallas_call(
        assemble_body,
        out_shape=(
            shape((96, 1536), f32),
            shape((96, 512), f32),
            shape((96, 512), f32),
            shape((96, 1536), f32),
            shape((1, 96), f32),
            shape((1, 96), f32),
            shape((16, 96), f32),
        ),
        in_specs=[pl.BlockSpec(memory_space=pltpu.SMEM)] + [vm] * 8,
        out_specs=(vm,) * 7,
        cost_estimate=pl.CostEstimate(flops=1_000_000, bytes_accessed=100_000, transcendentals=0),
        name="assemble",
    )(ids, *blocks)


def column(row):
    n = row.shape[1]
    down = lax.broadcasted_iota(jnp.int32, (n, n), 0)
    along = lax.broadcasted_iota(jnp.int32, (n, n), 1)
    return jnp.sum(jnp.where(down == along, row.astype(f32), 0.0), axis=1, keepdims=True)


def pack_body(
    at, w_query, w_key, w_value, gain_a, gain_b, router, tokens, seg, share, sent
):
    first = at[1] == 0
    x = at[0]
    wide = w_query[:, pl.ds(pl.multiple_of(x * 384, 128), 384)].astype(f32)
    slim = pl.ds(pl.multiple_of(x * 128, 128), 128)
    key, value = w_key[:, slim].astype(f32), w_value[:, slim].astype(f32)
    columns = jnp.concatenate(
        [
            jnp.where(first, wide[:, 0:192], wide[:, 192:384]),
            jnp.where(first, key[:, 0:64], key[:, 64:128]),
            jnp.where(first, value[:, 0:64], value[:, 64:128]),
            column(gain_a[...]),
            column(gain_b[...]),
            router[...].astype(f32).T,
            jnp.zeros((96, 46), f32),
        ],
        axis=1,
    ).astype(bf16)
    for i in range(16):
        share[i] = columns
    sent[:, 0:1536] = tokens[...]
    sent[:, 1536:1664] = jnp.broadcast_to(column(seg[...]), (128, 128)).astype(bf16)


def pack(at, w_query, w_key, w_value, gain_a, gain_b, router, tokens, seg):
    vm = pl.BlockSpec(memory_space=pltpu.VMEM)
    shape = jax.ShapeDtypeStruct
    return pl.pallas_call(
        pack_body,
        out_shape=(shape((16, 96, 384), bf16), shape((128, 1664), bf16)),
        in_specs=[pl.BlockSpec(memory_space=pltpu.SMEM)] + [vm] * 8,
        out_specs=(vm,) * 2,
        cost_estimate=pl.CostEstimate(flops=1_000_000, bytes_accessed=2_000_000, transcendentals=0),
        name="pack",
    )(at, w_query, w_key, w_value, gain_a, gain_b, router, tokens, seg)


def project_out_body(mixed, w_out, tokens, narrow, named, sent, hidden, gates, mx):
    for p in range(4):
        mx[:, 384 * p : 384 * (p + 1)] = jnp.concatenate(
            [mixed[2 * p, :, 0:192], mixed[2 * p + 1, :, 0:192]], axis=1
        )
    value = tokens[...].astype(f32) + residual_scale * mm(mx[...], w_out[...])
    hidden[...] = value
    r = lax.rsqrt(jnp.mean(value * value, axis=1, keepdims=True) + eps)
    gain = narrow[0:16, :].astype(f32)[1:2]
    second = (value * r * gain).astype(bf16)
    sent[:, 0:1536] = second
    logits = mm_nt(second, narrow[...])
    logits = pltpu.roll(jnp.concatenate([logits, jnp.zeros_like(logits)], axis=1), 126, 1)
    on = named[...] > 0.5
    logits = jnp.where(on, logits, -1e30)
    top = jnp.max(logits, axis=1, keepdims=True)
    e = jnp.where(on, jnp.exp(logits - top), 0.0)
    g = e / jnp.sum(e, axis=1, keepdims=True)
    gates[...] = g
    high = g.astype(bf16)
    low = pltpu.roll(g - high.astype(f32), 16, 1)
    lane = lax.broadcasted_iota(jnp.int32, g.shape, 1)
    sent[:, 1536:1664] = jnp.where(lane < 16, g, low).astype(bf16)


def project_out(mixed, w_out, tokens, narrow, named):
    vm = pl.BlockSpec(memory_space=pltpu.VMEM)
    shape = jax.ShapeDtypeStruct
    return pl.pallas_call(
        project_out_body,
        out_shape=(
            shape((128, 1664), bf16),
            shape((128, 1536), f32),
            shape((128, 128), f32),
            shape((128, 1536), bf16),
        ),
        in_specs=[vm] * 5,
        out_specs=(vm,) * 4,
        compiler_params=pltpu.CompilerParams(vmem_limit_bytes=56 * MIB),
        cost_estimate=pl.CostEstimate(flops=4_000_000_000, bytes_accessed=8_000_000, transcendentals=0),
        name="project_out",
    )(mixed, w_out, tokens, narrow, named)


def middle_body(
    w_out, sums, grads, hidden, gates, narrow, _, grad_hidden, heads, grad_gain, grad_router, gx
):
    gain = narrow[0:16, :].astype(f32)[1:2]
    total = sums[0].astype(f32)
    for i in range(1, 4):
        total = total + sums[i].astype(f32)
    value = hidden[...]
    r = lax.rsqrt(jnp.mean(value * value, axis=1, keepdims=True) + eps)
    second = (value * r * gain).astype(bf16)
    g = gates[...]
    table = total[:, 1536:1664]
    lane = lax.broadcasted_iota(jnp.int32, g.shape, 1)
    table = jnp.where(lane < 16, table + pltpu.roll(table, 112, 1), 0.0)
    logits = (g * (table - jnp.sum(g * table, axis=1, keepdims=True))).astype(bf16)
    grad_router[...] = mm(logits.astype(f32).T.astype(bf16), second)[0:16]
    router = pltpu.roll(logits.astype(f32), 2, 1)[:, 0:64].astype(bf16)
    grad_second = total[:, 0:1536] + mm(router, narrow[...])
    grad_gain[...] = jnp.sum(grad_second * value * r, axis=0, keepdims=True)
    scaled = grad_second * gain
    gh = (
        grads[...].astype(f32)
        + r * scaled
        - value * (r * r * r) * jnp.mean(value * scaled, axis=1, keepdims=True)
    )
    grad_hidden[...] = gh
    low = (residual_scale * gh).astype(bf16)
    gx[...] = mm_nt(low, w_out[...])
    low = low.astype(f32)
    for j in range(8):
        cols = slice(192 * j, 192 * (j + 1))
        heads[j] = jnp.concatenate([gx[:, cols], low[:, cols]], axis=1).astype(bf16)


def middle(w_out, sums, grads, hidden, gates, narrow, held):
    vm = pl.BlockSpec(memory_space=pltpu.VMEM)
    shape = jax.ShapeDtypeStruct
    return pl.pallas_call(
        middle_body,
        out_shape=(
            shape((128, 1536), f32),
            shape((8, 128, 384), bf16),
            shape((1, 1536), f32),
            shape((16, 1536), f32),
        ),
        in_specs=[vm] * 6 + [pl.BlockSpec(memory_space=pl.ANY)],
        out_specs=(vm,) * 4,
        scratch_shapes=[pltpu.VMEM((128, 1536), f32)],
        compiler_params=pltpu.CompilerParams(vmem_limit_bytes=56 * MIB),
        cost_estimate=pl.CostEstimate(flops=1_000_000, bytes_accessed=100_000, transcendentals=0),
        name="middle",
    )(w_out, sums, grads, hidden, gates, narrow, held)


def shift(value, axis, amount):
    size = lax.axis_size(axis)
    return lax.ppermute(value, axis, [((i + amount) % size, i) for i in range(size)])


def swap(value):
    return lax.ppermute(value, "core", [(0, 1), (1, 0)])


def tied(*values):
    return lax.optimization_barrier(values)


def gather_x(block):
    return [block] + [shift(block, "x", m) for m in (1, 2, 3)]


def both_cores(blocks):
    return [each for block in blocks for each in (block, swap(block))]


def near_sum(own, other):
    return (own.astype(f32) + swap(other).astype(f32)).astype(bf16)


def exchange(near):
    return lax.all_to_all(near, "x", 0, 0, tiled=True)


def exchange_apart(near):
    x = lax.axis_index("x")
    pieces = [lax.dynamic_index_in_dim(near, (x + m) % 4, 0, False) for m in range(4)]
    return [pieces[0]] + [shift(pieces[m], "x", -m) for m in (2, 1, 3)]


def total_of(terms):
    total = terms[0].astype(f32)
    for term in terms[1:]:
        total = total + term.astype(f32)
    return total


def inverse_rms(values):
    return lax.rsqrt(jnp.mean(values * values, axis=-1, keepdims=True) + eps)


def per_device(
    tokens,
    segments,
    routes,
    gain_attn,
    w_query,
    w_key,
    w_value,
    w_out,
    gain_moe,
    w_router,
    expert_gate,
    expert_up,
    expert_down,
    out_grad,
):
    rows, width = tokens.shape
    parts = 8
    seq = rows * parts
    x, core = lax.axis_index("x"), lax.axis_index("core")
    me = x * 2 + core
    z = lax.axis_index("z")
    at = jnp.stack([x, core, z])

    share, sent = pack(
        at,
        w_query,
        w_key,
        w_value,
        gain_attn[None, :],
        gain_moe[None, :],
        w_router.T,
        tokens,
        segments[None, :],
    )
    out_all = lax.all_gather(w_out, ("z", "y"), axis=0, tiled=True)
    qkv_w = lax.all_to_all(share, ("z", "y"), 0, 0, tiled=True).reshape(width, 384)
    far = gather_x(sent)
    far[1], grads_sent = tied(far[1], out_grad)
    blocks = both_cores(far)
    grads_far = gather_x(grads_sent)
    lane = jnp.arange(128, dtype=jnp.int32)

    chips = (x + jnp.arange(4, dtype=jnp.int32)) % 4
    cores = jnp.bitwise_xor(core, jnp.arange(2, dtype=jnp.int32))
    ids = (chips[:, None] * 2 + cores[None, :]).reshape(parts)
    place = jnp.arange(seq, dtype=jnp.int32)
    freq = rope_base ** (
        -(jnp.arange(128, dtype=jnp.int32) % 32).astype(f32) * 2.0 / HEAD_DIM
    )[None, :]
    angles = place.astype(f32)[:, None] * freq

    named = jnp.any(routes[:, :, None] == lane[None, None, :], axis=1).astype(f32)

    normed, narrow, gain_one, q01, q2k, val, lse, cos, sin, starts, mixed_head = attend_forward(
        ids, blocks, qkv_w, jnp.cos(angles), jnp.sin(angles), freq, named
    )
    mixed_head, *grads_far = tied(mixed_head, *grads_far)
    grad_blocks = both_cores(grads_far)
    mixed = lax.all_to_all(mixed_head, ("x", "core"), 0, 0, tiled=True)
    sent_two, hidden, gates, mixed = project_out(
        mixed, out_all, tokens, narrow, named
    )
    far_two = gather_x(sent_two)
    grad_all, back = back_rows(ids, grad_blocks, expert_down)
    twins = [swap(block) for block in far_two]
    mixed, back, *far_two = tied(mixed, back, *far_two)
    second_blocks = [each for pair in zip(far_two, twins) for each in pair]
    mixed_all = lax.all_gather(mixed, ("x", "core"), axis=0, tiled=True)

    grad_w_gate, grad_w_up, grad_w_down, weighted, grad_gate_pre, grad_up_pre, routed = experts(
        ids, second_blocks, grad_all, back, expert_gate, expert_up
    )
    sums = lax.psum((grad_w_gate, grad_w_up, grad_w_down), ("z", "y"))
    own, other = experts_back(
        at, grad_gate_pre, grad_up_pre, routed, expert_gate, expert_up, ()
    )
    near = near_sum(own, other)
    near, weighted = tied(near, weighted)
    terms = exchange(near)
    own_out, other_out = combine(at, weighted, expert_down)

    grad_hidden, heads, grad_gain_two, grad_router = middle(
        out_all, terms, out_grad, hidden, gates, narrow, own_out
    )
    grad_heads = lax.all_to_all(heads, ("x", "core"), 0, 0, tiled=True)
    own, other, table = attend_backward(
        at,
        grad_heads,
        q01,
        q2k,
        val,
        lse,
        cos,
        sin,
        starts,
        normed,
        qkv_w,
        gain_one,
        mixed_all,
        grad_gain_two,
        grad_router,
    )
    own_out, table = tied(own_out, table)
    near_out = near_sum(own_out, other_out)
    output = (hidden + residual_scale * total_of(exchange_apart(near_out))).astype(bf16)
    normed_mine = total_of(exchange_apart(near_sum(own, other)))
    inputs = tokens.astype(f32)
    scale_one = inverse_rms(inputs)
    scaled_one = normed_mine * gain_one
    grad_inputs = (
        grad_hidden
        + scale_one * scaled_one
        - inputs * scale_one**3 * jnp.mean(inputs * scaled_one, axis=-1, keepdims=True)
    )

    pieces = lax.all_to_all(table, ("z", "y"), 0, 0, tiled=True)
    pieces, output, grad_inputs = tied(pieces, output, grad_inputs)
    lines = both_cores(gather_x(sum_pieces(pieces)))
    grad_gate, grad_up, grad_down = widen(*sums)
    grad_q, grad_k, grad_v, grad_o, gain_a, gain_b, router = assemble(ids, lines)
    return (
        output,
        grad_inputs,
        gain_a.reshape(-1),
        grad_q,
        grad_k,
        grad_v,
        grad_o,
        gain_b.reshape(-1),
        router.T,
        grad_gate,
        grad_up,
        grad_down,
    )


def solution(mesh):
    fine = Mesh(mesh.devices.reshape(4, 4, 4, 2), ("z", "y", "x", "core"))
    dp, expert, both = ("z", "y"), ("x", "core"), ("z", "y", "x", "core")
    placed = (
        P(both, None),
        P(both),
        P(both, None),
        P(dp),
        P(dp, None),
        P(dp, None),
        P(dp, None),
        P(dp, None),
        P(dp),
        P(dp, None),
        P(expert, None, None),
        P(expert, None, None),
        P(expert, None, None),
    )
    return jax.shard_map(
        per_device,
        mesh=fine,
        in_specs=placed + (P(both, None),),
        out_specs=(P(both, None),) * 2 + placed[3:],
        check_vma=False,
    )
```

```python
import jax
import jax.numpy as jnp
from jax import lax
from jax.experimental import pallas as pl
from jax.experimental.pallas import tpu as pltpu
from jax.sharding import Mesh, PartitionSpec as P

HEADS = 24
KV_HEADS = 8
HEAD_DIM = 64
GROUP = HEADS // KV_HEADS
TOP = 8
EXPERTS = 16

eps = 1e-06
residual_scale = 0.22
score_scale = 0.015625
rope_base = 10000.0
doc_slots = 3
MIB = 1024 * 1024

bf16 = jnp.bfloat16
f32 = jnp.float32


def mm(a, b):
    return lax.dot_general(a, b, (((1,), (0,)), ((), ())), preferred_element_type=f32)


def mm_nt(a, b):
    return lax.dot_general(a, b, (((1,), (1,)), ((), ())), preferred_element_type=f32)


def low_half(value):
    lane = lax.broadcasted_iota(jnp.int32, value.shape, 1)
    return jnp.where(lane < 64, value, jnp.zeros_like(value))


def high_half(value):
    lane = lax.broadcasted_iota(jnp.int32, value.shape, 1)
    return jnp.where(lane >= 64, value, jnp.zeros_like(value))


def quarter(value):
    lane = lax.broadcasted_iota(jnp.int32, value.shape, 1)
    up, down = pltpu.roll(value, 96, 1), pltpu.roll(value, 32, 1)
    return jnp.where(lane % 64 < 32, -up, down)


def visible(chunk, starts):
    keys = 256 * (chunk + 1)
    place = (256 * chunk + lax.broadcasted_iota(jnp.int32, (1, 256), 1)).astype(f32)
    one = jnp.concatenate([starts[0:1], starts[0:1]], axis=1)
    two = jnp.concatenate([starts[1:2], starts[1:2]], axis=1)
    begin = jnp.where(place >= two, two, jnp.where(place >= one, one, jnp.zeros_like(one)))
    at = lax.broadcasted_iota(jnp.int32, (keys, 256), 0).astype(f32)
    return (at <= place) & (at >= begin)


def attend_body(ids, *refs):
    blocks = refs[:8]
    (w, cos_t, sin_t, freq, _, normed, narrow, gain_row, q01, q2k, val, lse, cos_o, sin_o, starts, mixed,
     ka, kb, vt) = refs[8:]
    one = jnp.zeros((1, 128), f32)
    two = jnp.zeros((1, 128), f32)
    for b in range(8):
        seg = blocks[b][:, 1536:1664].astype(f32)
        one = one + jnp.sum(jnp.where(seg < 0.5, 1.0, 0.0), axis=0, keepdims=True)
        two = two + jnp.sum(jnp.where(seg < 1.5, 1.0, 0.0), axis=0, keepdims=True)
    starts[...] = jnp.concatenate([one, two, jnp.zeros((6, 128), f32)], axis=0)
    begin_rows = jnp.concatenate([one, two, jnp.zeros((6, 128), f32)], axis=0)
    angles = begin_rows * freq[...]
    cos_b, sin_b = jnp.cos(angles), jnp.sin(angles)
    last = w[:, 256:384].astype(f32).T
    narrow[...] = last[64:128].astype(bf16)
    gain = last[64:65]
    gain_row[...] = gain
    for b in range(8):
        x = blocks[b][:, 0:1536].astype(f32)
        r = lax.rsqrt(jnp.mean(x * x, axis=1, keepdims=True) + eps)
        at = pl.ds(pl.multiple_of(ids[b] * 128, 128), 128)
        normed[at, :] = (x * r * gain).astype(bf16)
    def project(c, carry):
        at = pl.ds(pl.multiple_of(c * 256, 256), 256)
        u = mm(normed[at, :], w[...])
        place = (lax.broadcasted_iota(jnp.int32, (256, 128), 0) + c * 256).astype(f32)
        in_two, in_one = place >= two, place >= one
        cb = jnp.where(in_two, cos_b[1:2], jnp.where(in_one, cos_b[0:1], 1.0))
        sb = jnp.where(in_two, sin_b[1:2], jnp.where(in_one, sin_b[0:1], 0.0))
        ct, st = cos_t[at, :], sin_t[at, :]
        cc = ct * cb + st * sb
        ss = st * cb - ct * sb
        cos_o[at, :] = cc
        sin_o[at, :] = ss
        a, bq, v = u[:, 0:128], u[:, 128:256], u[:, 256:384]
        a = a * cc + quarter(a) * ss
        bq = bq * cc + quarter(bq) * ss
        v = low_half(v)
        q01[at, :] = a.astype(bf16)
        q2k[at, :] = bq.astype(bf16)
        val[at, :] = v.astype(bf16)
        k = high_half(bq) * score_scale
        kb[at, :] = k.astype(bf16)
        ka[at, :] = pltpu.roll(k, 64, 1).astype(bf16)
        vt[:, at] = v.T.astype(bf16)
        return carry

    lax.fori_loop(0, 4, project, 0)

    for c in range(4):
        at, seen = slice(256 * c, 256 * (c + 1)), slice(0, 256 * (c + 1))
        allowed = visible(c, starts)
        outs = []
        for h in range(3):
            q = q2k[at, :] if h == 2 else q01[at, :]
            kk = kb if h == 1 else ka
            s = mm_nt(kk[seen, :], q)
            s = jnp.where(allowed, s, -1e30)
            top = jnp.max(s, axis=0, keepdims=True)
            p = jnp.exp(s - top)
            total = jnp.sum(p, axis=0, keepdims=True)
            lse[h : h + 1, at] = top + jnp.log(total)
            pb = (p * (1.0 / total)).astype(bf16)
            outs.append(mm(vt[0:64, seen], pb))
        out = jnp.concatenate(outs + [jnp.zeros((64, 256), f32)], axis=0).T.astype(bf16)
        mixed[2 * c] = out[0:128]
        mixed[2 * c + 1] = out[128:256]


def attend_forward(ids, blocks, w, cos_t, sin_t, freq, held):
    vm = pl.BlockSpec(memory_space=pltpu.VMEM)
    shape = jax.ShapeDtypeStruct
    return pl.pallas_call(
        attend_body,
        out_shape=(
            shape((1024, 1536), bf16),
            shape((64, 1536), bf16),
            shape((1, 1536), f32),
            shape((1024, 128), bf16),
            shape((1024, 128), bf16),
            shape((1024, 128), bf16),
            shape((8, 1024), f32),
            shape((1024, 128), f32),
            shape((1024, 128), f32),
            shape((8, 128), f32),
            shape((8, 128, 256), bf16),
        ),
        in_specs=[pl.BlockSpec(memory_space=pltpu.SMEM)]
        + [vm] * 12
        + [pl.BlockSpec(memory_space=pl.ANY)],
        out_specs=(vm,) * 11,
        scratch_shapes=[
            pltpu.VMEM((1024, 128), bf16),
            pltpu.VMEM((1024, 128), bf16),
            pltpu.VMEM((128, 1024), bf16),
        ],
        compiler_params=pltpu.CompilerParams(vmem_limit_bytes=56 * MIB),
        cost_estimate=pl.CostEstimate(flops=14_000_000_000, bytes_accessed=12_000_000, transcendentals=3_200_000),
        name="attend_forward",
    )(ids, *blocks, w, cos_t, sin_t, freq, held)


def attend_back_body(
    here, w, gm, q01, q2k, val, lse, cc, ss, starts, normed_hbm, gain,
    mixed_hbm, gain_b, router, own_hbm, other_hbm, table,
    ka, kb, vb, kt, do01, do2, dk, dv, d01, dq2, normed, own, other, got, sent, dqkv, mixed,
):
    load = pltpu.make_async_copy(normed_hbm, normed, got.at[0])
    load_mixed = pltpu.make_async_copy(mixed_hbm, mixed, got.at[1])
    load.start()
    load_mixed.start()
    k = high_half(q2k[...].astype(f32)) * score_scale
    kb[...] = k.astype(bf16)
    k_low = pltpu.roll(k, 64, 1)
    ka[...] = k_low.astype(bf16)
    kt[...] = k_low.T.astype(bf16)
    vb[...] = pltpu.roll(val[...].astype(f32), 64, 1).astype(bf16)
    for b in range(8):
        do01[b * 128 : (b + 1) * 128, :] = gm[b, :, 0:128]
        do2[b * 128 : (b + 1) * 128, :] = low_half(gm[b, :, 128:256])
    dk[...] = jnp.zeros_like(dk)
    dv[...] = jnp.zeros_like(dv)

    for c in range(4):
        at, seen = slice(256 * c, 256 * (c + 1)), slice(0, 256 * (c + 1))
        allowed = visible(c, starts)
        qa, qb = q01[at, :], q2k[at, :]
        da, db = do01[at, :], do2[at, :]
        outs = []
        for h in range(3):
            q = qb if h == 2 else qa
            kk = kb if h == 1 else ka
            s = mm_nt(kk[seen, :], q)
            p = jnp.where(allowed, jnp.exp(s - lse[h : h + 1, at]), 0.0)
            d = db if h == 2 else da
            vv = vb if h == 1 else val
            dp = mm_nt(vv[seen, :], d)
            delta = jnp.sum(p * dp, axis=0, keepdims=True)
            ds = (p * (dp - delta)).astype(bf16)
            outs.append(mm(kt[0:64, seen], ds))
            half = high_half if h == 1 else low_half
            dk[seen, :] += mm(ds, half(q))
            dv[seen, :] += mm(p.astype(bf16), half(d))
        out = jnp.concatenate(outs + [jnp.zeros((64, 256), f32)], axis=0).T
        d01[at, :] = out[:, 0:128]
        dq2[at, :] = out[:, 128:256]

    load.wait()

    def store(c):
        return (
            pltpu.make_async_copy(own.at[c], own_hbm.at[c], sent.at[0, c]),
            pltpu.make_async_copy(other.at[c], other_hbm.at[c], sent.at[1, c]),
        )

    def finish(c, total):
        at = pl.ds(pl.multiple_of(c * 256, 256), 256)
        dkk = dk[at, :]
        dkk = (dkk + pltpu.roll(dkk, 64, 1)) * score_scale
        dvv = dv[at, :]
        dvv = low_half(dvv + pltpu.roll(dvv, 64, 1))
        a = d01[at, :]
        lane = lax.broadcasted_iota(jnp.int32, (256, 128), 1)
        b = jnp.where(lane < 64, dq2[at, :], dkk)
        cos, sin = cc[at, :], ss[at, :]
        a = a * cos - quarter(a) * sin
        b = b * cos - quarter(b) * sin
        row = jnp.concatenate([a, b, dvv], axis=1).astype(bf16)
        dqkv[at, :] = row
        whole = mm_nt(row, w[...])
        total = total + jnp.sum(whole * normed[at, :].astype(f32), axis=0, keepdims=True)
        low = whole.astype(bf16)
        own[c] = jnp.where(here[1] == 0, low[0:128], low[128:256])
        other[c] = jnp.where(here[1] == 0, low[128:256], low[0:128])
        for copy in store(c):
            copy.start()
        return total

    total = lax.fori_loop(0, 4, finish, jnp.zeros((1, 1536), f32))
    gain_a = total / gain[...]
    load_mixed.wait()
    branch = jnp.concatenate([gm[b, :, 192:384] for b in range(8)], axis=0)
    row = lax.broadcasted_iota(jnp.int32, (16, 256), 0)
    for z in range(4):
        cols = slice(384 * z, 384 * (z + 1))
        first = mm(normed[:, cols].T, dqkv[...])
        second = mm(mixed[:, cols].T, branch)
        last = jnp.concatenate([first[:, 256:320], second], axis=1)
        for y in range(4):
            here_rows = slice(96 * y, 96 * (y + 1))
            lanes = slice(384 * z + 96 * y, 384 * z + 96 * (y + 1))
            zero = jnp.zeros((1, 32), f32)
            gains = jnp.concatenate([gain_a[:, lanes], zero, gain_b[:, lanes], zero], axis=1)
            small = jnp.concatenate([router[:, lanes], jnp.zeros((16, 160), f32)], axis=1)
            extra = jnp.where(row == 0, jnp.broadcast_to(gains, (16, 256)), 0.0)
            chunk = table.at[4 * z + y]
            chunk[0:96, 0:256] = first[here_rows, 0:256].astype(bf16)
            chunk[96:112, 0:256] = small.astype(bf16)
            chunk[0:96, 256:512] = last[here_rows].astype(bf16)
            chunk[96:112, 256:512] = extra.astype(bf16)
    for c in range(4):
        for copy in store(c):
            copy.wait()


def attend_backward(
    here, gm, q01, q2k, val, lse, cc, ss, starts, normed, w, gain, mixed, gain_b, router
):
    vm, hbm = pl.BlockSpec(memory_space=pltpu.VMEM), pl.BlockSpec(memory_space=pl.ANY)
    rows = pltpu.VMEM((4, 128, 1536), bf16)
    whole = pltpu.VMEM((1024, 1536), bf16)
    shape = jax.ShapeDtypeStruct
    half = pltpu.VMEM((1024, 128), bf16)
    full = pltpu.VMEM((1024, 128), f32)
    return pl.pallas_call(
        attend_back_body,
        out_shape=(
            shape((4, 128, 1536), bf16),
            shape((4, 128, 1536), bf16),
            shape((16, 112, 512), bf16),
        ),
        in_specs=[pl.BlockSpec(memory_space=pltpu.SMEM)] + [vm] * 9 + [hbm, vm, hbm, vm, vm],
        out_specs=(hbm, hbm, vm),
        scratch_shapes=[half, half, half, pltpu.VMEM((128, 1024), bf16), half, half]
        + [full, full, full, full, whole, rows, rows]
        + [pltpu.SemaphoreType.DMA((2,)), pltpu.SemaphoreType.DMA((2, 4))]
        + [pltpu.VMEM((1024, 384), bf16), whole],
        compiler_params=pltpu.CompilerParams(vmem_limit_bytes=56 * MIB),
        cost_estimate=pl.CostEstimate(flops=1_000_000, bytes_accessed=100_000, transcendentals=0),
        name="attend_backward",
    )(here, w, gm, q01, q2k, val, lse, cc, ss, starts, normed, gain, mixed, gain_b, router)


def experts_body(ids, *refs):
    blocks = refs[:8]
    (grads, back, gate_w, up_w, d_gate, d_up, d_down, aw, gg, gu, routed, second, st, col) = refs[8:]
    e, c = pl.program_id(0), pl.program_id(1)
    first = (e == 0) & (c == 0)

    @pl.when(first)
    def _():
        for b in range(8):
            second[pl.ds(pl.multiple_of(ids[b] * 128, 128), 128), :] = blocks[b][...]
        for b in range(8):
            at = slice(128 * b, 128 * (b + 1))
            st[:, at] = second[at, 0:1536].T
        routed[...] = jnp.zeros_like(routed)

    @pl.when(c == 0)
    def _():
        lane = lax.broadcasted_iota(jnp.int32, (128, 128), 1)
        name = 2 * ids[0] + e
        hit = (lane == name) | (lane == name + 16)
        for b in range(8):
            at = slice(128 * b, 128 * (b + 1))
            table = second[at, 1536:1664].astype(f32)
            w = jnp.sum(jnp.where(hit, table, 0.0), axis=1, keepdims=True)
            col[at, :] = jnp.broadcast_to(w, (128, 128))

    x = second[:, 0:1536]
    gated = mm(x, gate_w[0])
    upper = mm(x, up_w[0])
    h = back[...].astype(f32)
    w = jnp.concatenate([col[...]] * 2, axis=1)
    sig = 1.0 / (1.0 + jnp.exp(-gated))
    silu = gated * sig
    act = silu * upper
    aw[...] = (act * w).astype(bf16)
    dots = residual_scale * jnp.sum(act * h, axis=1, keepdims=True)
    lane = lax.broadcasted_iota(jnp.int32, (1024, 128), 1)
    routed[...] += jnp.where(lane == 2 * ids[0] + e, dots, 0.0)
    ga = h * (w * residual_scale)
    gg[...] = (ga * upper * (sig * (1.0 + gated * (1.0 - sig)))).astype(bf16)
    gu[...] = (ga * silu).astype(bf16)

    d_gate[0] = mm(st[...], gg[...]).astype(bf16)
    d_up[0] = mm(st[...], gu[...]).astype(bf16)
    d_down[0] = (mm(aw[...].T, grads[...]) * residual_scale).astype(bf16)


def experts(ids, blocks, grads, back, gate_w, up_w):
    vm = pl.BlockSpec(memory_space=pltpu.VMEM)
    shape = jax.ShapeDtypeStruct
    wide = pl.BlockSpec((1, 1536, 256), lambda e, c: (e, 0, c))
    tall = pl.BlockSpec((1, 256, 1536), lambda e, c: (e, c, 0))
    line = pl.BlockSpec((1024, 256), lambda e, c: (0, 2 * e + c))
    return pl.pallas_call(
        experts_body,
        grid=(2, 2),
        out_shape=(
            shape((2, 1536, 512), bf16),
            shape((2, 1536, 512), bf16),
            shape((2, 512, 1536), bf16),
            shape((1024, 1024), bf16),
            shape((1024, 1024), bf16),
            shape((1024, 1024), bf16),
            shape((1024, 128), f32),
        ),
        in_specs=[pl.BlockSpec(memory_space=pltpu.SMEM)] + [vm] * 9 + [line, wide, wide],
        out_specs=(wide, wide, tall, line, line, line, vm),
        scratch_shapes=[
            pltpu.VMEM((1024, 1664), bf16),
            pltpu.VMEM((1536, 1024), bf16),
            pltpu.VMEM((1024, 128), f32),
        ],
        compiler_params=pltpu.CompilerParams(vmem_limit_bytes=60 * MIB),
        cost_estimate=pl.CostEstimate(flops=16_000_000_000, bytes_accessed=34_000_000, transcendentals=1_000_000),
        name="experts",
    )(ids, *blocks, grads, back, gate_w, up_w)


def split_cores(here, value, own, other):
    first = here[1] == 0
    own[0] = jnp.where(first, value[0:128], value[128:256])
    other[0] = jnp.where(first, value[128:256], value[0:128])


def by_chip(here, body, width, name, rows, whole, held, flops):
    out = pl.BlockSpec((1, 128, width), lambda m, here: (m, 0, 0))
    shape = jax.ShapeDtypeStruct((4, 128, width), bf16)
    lines = [
        pl.BlockSpec((256, a.shape[1]), lambda m, here: (m, 0)) for a in rows
    ]
    return pl.pallas_call(
        body,
        grid_spec=pltpu.PrefetchScalarGridSpec(
            num_scalar_prefetch=1,
            grid=(4,),
            in_specs=lines
            + [pl.BlockSpec(memory_space=pltpu.VMEM)] * len(whole)
            + [pl.BlockSpec(memory_space=pl.ANY)] * len(held),
            out_specs=(out, out),
        ),
        out_shape=(shape, shape),
        compiler_params=pltpu.CompilerParams(vmem_limit_bytes=56 * MIB),
        cost_estimate=pl.CostEstimate(flops=flops, bytes_accessed=100_000, transcendentals=0),
        name=name,
    )(here, *rows, *whole, *held)


def back_body(here, gg, gu, routed, gate_w, up_w, *refs):
    own, other = refs[-2:]
    total = mm_nt(gg[:, 0:512], gate_w[0]) + mm_nt(gg[:, 512:1024], gate_w[1])
    total = total + mm_nt(gu[:, 0:512], up_w[0]) + mm_nt(gu[:, 512:1024], up_w[1])
    table = routed[...]
    high = table.astype(bf16).astype(f32)
    low = pltpu.roll(table - high, 16, 1)
    lane = lax.broadcasted_iota(jnp.int32, table.shape, 1)
    tail = jnp.where(lane < 16, high, low)
    split_cores(here, jnp.concatenate([total, tail], axis=1).astype(bf16), own, other)


def experts_back(here, gg, gu, routed, gate_w, up_w, held):
    rows, whole = (gg, gu, routed), (gate_w, up_w)
    return by_chip(here, back_body, 1664, "experts_back", rows, whole, held, 10**6)


def combine_body(here, aw, down_w, own, other):
    total = mm(aw[:, 0:512], down_w[0]) + mm(aw[:, 512:1024], down_w[1])
    split_cores(here, total.astype(bf16), own, other)


def combine(here, aw, down_w):
    return by_chip(here, combine_body, 1536, "combine", (aw,), (down_w,), (), 8 * 10**9)


def widen_body(a, b, c, x, y, z, *refs):
    held, grown, got, sent = refs[0:3], refs[3:6], refs[6], refs[7]
    work = []
    for k, (source, target) in enumerate(((a, x), (b, y), (c, z))):
        half = source.shape[1] // 2
        for e in range(2):
            for i in range(2):
                j = 2 * e + i
                at = pl.ds(half * i, half)
                load = pltpu.make_async_copy(
                    source.at[e, at], held[k].at[j], got.at[4 * k + j]
                )
                store = pltpu.make_async_copy(
                    grown[k].at[j], target.at[e, at], sent.at[4 * k + j]
                )
                load.start()
                work.append((k, j, load, store))
    for k, j, load, store in work:
        load.wait()
        grown[k][j] = held[k][j].astype(f32)
        store.start()
    for _, _, _, store in work:
        store.wait()


def widen(a, b, c):
    hbm = pl.BlockSpec(memory_space=pl.ANY)
    shapes = [(4, v.shape[1] // 2, v.shape[2]) for v in (a, b, c)]
    return pl.pallas_call(
        widen_body,
        out_shape=tuple(jax.ShapeDtypeStruct(v.shape, f32) for v in (a, b, c)),
        in_specs=[hbm] * 3,
        out_specs=(hbm,) * 3,
        scratch_shapes=[pltpu.VMEM(s, bf16) for s in shapes]
        + [pltpu.VMEM(s, f32) for s in shapes]
        + [pltpu.SemaphoreType.DMA((12,)), pltpu.SemaphoreType.DMA((12,))],
        compiler_params=pltpu.CompilerParams(vmem_limit_bytes=56 * MIB),
        cost_estimate=pl.CostEstimate(flops=1_000_000, bytes_accessed=28_000_000, transcendentals=0),
        name="widen",
    )(a, b, c)


def back_rows_body(ids, *refs):
    blocks, (down_w, grads, back) = refs[:8], refs[8:]

    @pl.when(pl.program_id(0) == 0)
    def _():
        for b in range(8):
            grads[pl.ds(pl.multiple_of(ids[b] * 128, 128), 128), :] = blocks[b][...]

    back[...] = mm_nt(grads[...], down_w[0]).astype(bf16)


def back_rows(ids, blocks, down_w):
    vm = pl.BlockSpec(memory_space=pltpu.VMEM)
    shape = jax.ShapeDtypeStruct
    return pl.pallas_call(
        back_rows_body,
        grid=(2,),
        out_shape=(shape((1024, 1536), bf16), shape((1024, 1024), bf16)),
        in_specs=[pl.BlockSpec(memory_space=pltpu.SMEM)]
        + [vm] * 8
        + [pl.BlockSpec((1, 512, 1536), lambda e: (e, 0, 0))],
        out_specs=(vm, pl.BlockSpec((1024, 512), lambda e: (0, e))),
        compiler_params=pltpu.CompilerParams(vmem_limit_bytes=56 * MIB),
        cost_estimate=pl.CostEstimate(flops=8_000_000_000, bytes_accessed=11_000_000, transcendentals=0),
        name="back_rows",
    )(ids, *blocks, down_w)


def sum_body(pieces, out):
    total = pieces[0].astype(f32)
    for i in range(1, pieces.shape[0]):
        total = total + pieces[i].astype(f32)
    out[...] = total.astype(bf16)


def sum_pieces(pieces):
    vm = pl.BlockSpec(memory_space=pltpu.VMEM)
    return pl.pallas_call(
        sum_body,
        out_shape=jax.ShapeDtypeStruct(pieces.shape[1:], bf16),
        in_specs=[vm],
        out_specs=vm,
        cost_estimate=pl.CostEstimate(flops=1_000_000, bytes_accessed=100_000, transcendentals=0),
        name="sum_pieces",
    )(pieces)


def assemble_body(ids, *refs):
    blocks, (query, key, value, out, gain_a, gain_b, router) = refs[:8], refs[8:]
    total = jnp.zeros((16, 512), f32)
    for m in range(4):
        here, there = blocks[2 * m][...].astype(f32), blocks[2 * m + 1][...].astype(f32)
        total = total + here[96:112] + there[96:112]
        first = ids[2 * m] < ids[2 * m + 1]
        a, b = jnp.where(first, here, there)[0:96], jnp.where(first, there, here)[0:96]
        chip = ids[2 * m] // 2
        wide = pl.ds(pl.multiple_of(chip * 384, 128), 384)
        slim = pl.ds(pl.multiple_of(chip * 128, 128), 128)
        query[:, wide] = jnp.concatenate([a[:, 0:192], b[:, 0:192]], axis=1)
        key[:, slim] = jnp.concatenate([a[:, 192:256], b[:, 192:256]], axis=1)
        value[:, slim] = jnp.concatenate([a[:, 256:320], b[:, 256:320]], axis=1)
        out[:, wide] = jnp.concatenate([a[:, 320:512], b[:, 320:512]], axis=1)
    router[...] = total[:, 0:96]
    gain_a[...] = total[0:1, 256:352]
    gain_b[...] = total[0:1, 384:480]


def assemble(ids, blocks):
    vm = pl.BlockSpec(memory_space=pltpu.VMEM)
    shape = jax.ShapeDtypeStruct
    return pl.pallas_call(
        assemble_body,
        out_shape=(
            shape((96, 1536), f32),
            shape((96, 512), f32),
            shape((96, 512), f32),
            shape((96, 1536), f32),
            shape((1, 96), f32),
            shape((1, 96), f32),
            shape((16, 96), f32),
        ),
        in_specs=[pl.BlockSpec(memory_space=pltpu.SMEM)] + [vm] * 8,
        out_specs=(vm,) * 7,
        cost_estimate=pl.CostEstimate(flops=1_000_000, bytes_accessed=100_000, transcendentals=0),
        name="assemble",
    )(ids, *blocks)


def column(row):
    n = row.shape[1]
    down = lax.broadcasted_iota(jnp.int32, (n, n), 0)
    along = lax.broadcasted_iota(jnp.int32, (n, n), 1)
    return jnp.sum(jnp.where(down == along, row.astype(f32), 0.0), axis=1, keepdims=True)


def pack_body(
    at, w_query, w_key, w_value, gain_a, gain_b, router, tokens, seg, share, sent
):
    first = at[1] == 0
    x = at[0]
    wide = w_query[:, pl.ds(pl.multiple_of(x * 384, 128), 384)].astype(f32)
    slim = pl.ds(pl.multiple_of(x * 128, 128), 128)
    key, value = w_key[:, slim].astype(f32), w_value[:, slim].astype(f32)
    columns = jnp.concatenate(
        [
            jnp.where(first, wide[:, 0:192], wide[:, 192:384]),
            jnp.where(first, key[:, 0:64], key[:, 64:128]),
            jnp.where(first, value[:, 0:64], value[:, 64:128]),
            column(gain_a[...]),
            column(gain_b[...]),
            router[...].astype(f32).T,
            jnp.zeros((96, 46), f32),
        ],
        axis=1,
    ).astype(bf16)
    for i in range(16):
        share[i] = columns
    sent[:, 0:1536] = tokens[...]
    sent[:, 1536:1664] = jnp.broadcast_to(column(seg[...]), (128, 128)).astype(bf16)


def pack(at, w_query, w_key, w_value, gain_a, gain_b, router, tokens, seg):
    vm = pl.BlockSpec(memory_space=pltpu.VMEM)
    shape = jax.ShapeDtypeStruct
    return pl.pallas_call(
        pack_body,
        out_shape=(shape((16, 96, 384), bf16), shape((128, 1664), bf16)),
        in_specs=[pl.BlockSpec(memory_space=pltpu.SMEM)] + [vm] * 8,
        out_specs=(vm,) * 2,
        cost_estimate=pl.CostEstimate(flops=1_000_000, bytes_accessed=2_000_000, transcendentals=0),
        name="pack",
    )(at, w_query, w_key, w_value, gain_a, gain_b, router, tokens, seg)


def project_out_body(mixed, w_out, tokens, narrow, named, sent, hidden, gates, mx):
    for p in range(4):
        mx[:, 384 * p : 384 * (p + 1)] = jnp.concatenate(
            [mixed[2 * p, :, 0:192], mixed[2 * p + 1, :, 0:192]], axis=1
        )
    value = tokens[...].astype(f32) + residual_scale * mm(mx[...], w_out[...])
    hidden[...] = value
    r = lax.rsqrt(jnp.mean(value * value, axis=1, keepdims=True) + eps)
    gain = narrow[0:16, :].astype(f32)[1:2]
    second = (value * r * gain).astype(bf16)
    sent[:, 0:1536] = second
    logits = mm_nt(second, narrow[...])
    logits = pltpu.roll(jnp.concatenate([logits, jnp.zeros_like(logits)], axis=1), 126, 1)
    on = named[...] > 0.5
    logits = jnp.where(on, logits, -1e30)
    top = jnp.max(logits, axis=1, keepdims=True)
    e = jnp.where(on, jnp.exp(logits - top), 0.0)
    g = e / jnp.sum(e, axis=1, keepdims=True)
    gates[...] = g
    high = g.astype(bf16)
    low = pltpu.roll(g - high.astype(f32), 16, 1)
    lane = lax.broadcasted_iota(jnp.int32, g.shape, 1)
    sent[:, 1536:1664] = jnp.where(lane < 16, g, low).astype(bf16)


def project_out(mixed, w_out, tokens, narrow, named):
    vm = pl.BlockSpec(memory_space=pltpu.VMEM)
    shape = jax.ShapeDtypeStruct
    return pl.pallas_call(
        project_out_body,
        out_shape=(
            shape((128, 1664), bf16),
            shape((128, 1536), f32),
            shape((128, 128), f32),
            shape((128, 1536), bf16),
        ),
        in_specs=[vm] * 5,
        out_specs=(vm,) * 4,
        compiler_params=pltpu.CompilerParams(vmem_limit_bytes=56 * MIB),
        cost_estimate=pl.CostEstimate(flops=4_000_000_000, bytes_accessed=8_000_000, transcendentals=0),
        name="project_out",
    )(mixed, w_out, tokens, narrow, named)


def middle_body(
    w_out, sum_a, sum_b, sum_c, sum_d, grads, hidden, gates, narrow, _,
    grad_hidden, heads, grad_gain, grad_router, gx,
):
    gain = narrow[0:16, :].astype(f32)[1:2]
    total = sum_a[...].astype(f32)
    for term in (sum_b, sum_c, sum_d):
        total = total + term[...].astype(f32)
    value = hidden[...]
    r = lax.rsqrt(jnp.mean(value * value, axis=1, keepdims=True) + eps)
    second = (value * r * gain).astype(bf16)
    g = gates[...]
    table = total[:, 1536:1664]
    lane = lax.broadcasted_iota(jnp.int32, g.shape, 1)
    table = jnp.where(lane < 16, table + pltpu.roll(table, 112, 1), 0.0)
    logits = (g * (table - jnp.sum(g * table, axis=1, keepdims=True))).astype(bf16)
    grad_router[...] = mm(logits.astype(f32).T.astype(bf16), second)[0:16]
    router = pltpu.roll(logits.astype(f32), 2, 1)[:, 0:64].astype(bf16)
    grad_second = total[:, 0:1536] + mm(router, narrow[...])
    grad_gain[...] = jnp.sum(grad_second * value * r, axis=0, keepdims=True)
    scaled = grad_second * gain
    gh = (
        grads[...].astype(f32)
        + r * scaled
        - value * (r * r * r) * jnp.mean(value * scaled, axis=1, keepdims=True)
    )
    grad_hidden[...] = gh
    low = (residual_scale * gh).astype(bf16)
    gx[...] = mm_nt(low, w_out[...])
    low = low.astype(f32)
    for j in range(8):
        cols = slice(192 * j, 192 * (j + 1))
        heads[j] = jnp.concatenate([gx[:, cols], low[:, cols]], axis=1).astype(bf16)


def middle(w_out, sums, grads, hidden, gates, narrow, held):
    vm = pl.BlockSpec(memory_space=pltpu.VMEM)
    shape = jax.ShapeDtypeStruct
    return pl.pallas_call(
        middle_body,
        out_shape=(
            shape((128, 1536), f32),
            shape((8, 128, 384), bf16),
            shape((1, 1536), f32),
            shape((16, 1536), f32),
        ),
        in_specs=[vm] * 9 + [pl.BlockSpec(memory_space=pl.ANY)],
        out_specs=(vm,) * 4,
        scratch_shapes=[pltpu.VMEM((128, 1536), f32)],
        compiler_params=pltpu.CompilerParams(vmem_limit_bytes=56 * MIB),
        cost_estimate=pl.CostEstimate(flops=1_000_000, bytes_accessed=100_000, transcendentals=0),
        name="middle",
    )(w_out, *sums, grads, hidden, gates, narrow, held)


def shift(value, axis, amount):
    size = lax.axis_size(axis)
    return lax.ppermute(value, axis, [((i + amount) % size, i) for i in range(size)])


def swap(value):
    return lax.ppermute(value, "core", [(0, 1), (1, 0)])


def tied(*values):
    return lax.optimization_barrier(values)


def gather_x(block):
    return [block] + [shift(block, "x", m) for m in (1, 2, 3)]


def both_cores(blocks):
    return [each for block in blocks for each in (block, swap(block))]


def near_sum(own, other):
    return (own.astype(f32) + swap(other).astype(f32)).astype(bf16)


def exchange(near):
    return lax.all_to_all(near, "x", 0, 0, tiled=True)


def exchange_apart(near):
    x = lax.axis_index("x")
    pieces = [lax.dynamic_index_in_dim(near, (x + m) % 4, 0, False) for m in range(4)]
    return [pieces[0]] + [shift(pieces[m], "x", -m) for m in (2, 1, 3)]


def total_of(terms):
    total = terms[0].astype(f32)
    for term in terms[1:]:
        total = total + term.astype(f32)
    return total


def inverse_rms(values):
    return lax.rsqrt(jnp.mean(values * values, axis=-1, keepdims=True) + eps)


def per_device(
    tokens,
    segments,
    routes,
    gain_attn,
    w_query,
    w_key,
    w_value,
    w_out,
    gain_moe,
    w_router,
    expert_gate,
    expert_up,
    expert_down,
    out_grad,
):
    rows, width = tokens.shape
    parts = 8
    seq = rows * parts
    x, core = lax.axis_index("x"), lax.axis_index("core")
    me = x * 2 + core
    z = lax.axis_index("z")
    at = jnp.stack([x, core, z])

    share, sent = pack(
        at,
        w_query,
        w_key,
        w_value,
        gain_attn[None, :],
        gain_moe[None, :],
        w_router.T,
        tokens,
        segments[None, :],
    )
    out_all = lax.all_gather(w_out, ("z", "y"), axis=0, tiled=True)
    qkv_w = lax.all_to_all(share, ("z", "y"), 0, 0, tiled=True).reshape(width, 384)
    far = gather_x(sent)
    far[1], grads_sent = tied(far[1], out_grad)
    blocks = both_cores(far)
    grads_far = gather_x(grads_sent)
    lane = jnp.arange(128, dtype=jnp.int32)

    chips = (x + jnp.arange(4, dtype=jnp.int32)) % 4
    cores = jnp.bitwise_xor(core, jnp.arange(2, dtype=jnp.int32))
    ids = (chips[:, None] * 2 + cores[None, :]).reshape(parts)
    place = jnp.arange(seq, dtype=jnp.int32)
    freq = rope_base ** (
        -(jnp.arange(128, dtype=jnp.int32) % 32).astype(f32) * 2.0 / HEAD_DIM
    )[None, :]
    angles = place.astype(f32)[:, None] * freq

    named = jnp.any(routes[:, :, None] == lane[None, None, :], axis=1).astype(f32)

    normed, narrow, gain_one, q01, q2k, val, lse, cos, sin, starts, mixed_head = attend_forward(
        ids, blocks, qkv_w, jnp.cos(angles), jnp.sin(angles), freq, named
    )
    mixed_head, *grads_far = tied(mixed_head, *grads_far)
    grad_blocks = both_cores(grads_far)
    mixed = lax.all_to_all(mixed_head, ("x", "core"), 0, 0, tiled=True)
    sent_two, hidden, gates, mixed = project_out(
        mixed, out_all, tokens, narrow, named
    )
    far_two = gather_x(sent_two)
    grad_all, back = back_rows(ids, grad_blocks, expert_down)
    twins = [swap(block) for block in far_two]
    mixed, back, *far_two = tied(mixed, back, *far_two)
    second_blocks = [each for pair in zip(far_two, twins) for each in pair]
    mixed_all = lax.all_gather(mixed, ("x", "core"), axis=0, tiled=True)

    grad_w_gate, grad_w_up, grad_w_down, weighted, grad_gate_pre, grad_up_pre, routed = experts(
        ids, second_blocks, grad_all, back, expert_gate, expert_up
    )
    sums = lax.psum((grad_w_gate, grad_w_up, grad_w_down), ("z", "y"))
    own, other = experts_back(
        at, grad_gate_pre, grad_up_pre, routed, expert_gate, expert_up, ()
    )
    near = near_sum(own, other)
    near, weighted = tied(near, weighted)
    terms = exchange_apart(near)
    own_out, other_out = combine(at, weighted, expert_down)

    grad_hidden, heads, grad_gain_two, grad_router = middle(
        out_all, terms, out_grad, hidden, gates, narrow, own_out
    )
    grad_heads = lax.all_to_all(heads, ("x", "core"), 0, 0, tiled=True)
    own, other, table = attend_backward(
        at,
        grad_heads,
        q01,
        q2k,
        val,
        lse,
        cos,
        sin,
        starts,
        normed,
        qkv_w,
        gain_one,
        mixed_all,
        grad_gain_two,
        grad_router,
    )
    near_out, near_normed = near_sum(own_out, other_out), near_sum(own, other)
    near_out, near_normed, table = tied(near_out, near_normed, table)
    output = (hidden + residual_scale * total_of(exchange_apart(near_out))).astype(bf16)
    normed_mine = total_of(exchange_apart(near_normed))
    inputs = tokens.astype(f32)
    scale_one = inverse_rms(inputs)
    scaled_one = normed_mine * gain_one
    grad_inputs = (
        grad_hidden
        + scale_one * scaled_one
        - inputs * scale_one**3 * jnp.mean(inputs * scaled_one, axis=-1, keepdims=True)
    )

    pieces = lax.all_to_all(table, ("z", "y"), 0, 0, tiled=True)
    pieces, output, grad_inputs = tied(pieces, output, grad_inputs)
    lines = both_cores(gather_x(sum_pieces(pieces)))
    grad_gate, grad_up, grad_down = widen(*sums)
    grad_q, grad_k, grad_v, grad_o, gain_a, gain_b, router = assemble(ids, lines)
    return (
        output,
        grad_inputs,
        gain_a.reshape(-1),
        grad_q,
        grad_k,
        grad_v,
        grad_o,
        gain_b.reshape(-1),
        router.T,
        grad_gate,
        grad_up,
        grad_down,
    )


def solution(mesh):
    fine = Mesh(mesh.devices.reshape(4, 4, 4, 2), ("z", "y", "x", "core"))
    dp, expert, both = ("z", "y"), ("x", "core"), ("z", "y", "x", "core")
    placed = (
        P(both, None),
        P(both),
        P(both, None),
        P(dp),
        P(dp, None),
        P(dp, None),
        P(dp, None),
        P(dp, None),
        P(dp),
        P(dp, None),
        P(expert, None, None),
        P(expert, None, None),
        P(expert, None, None),
    )
    return jax.shard_map(
        per_device,
        mesh=fine,
        in_specs=placed + (P(both, None),),
        out_specs=(P(both, None),) * 2 + placed[3:],
        check_vma=False,
    )
```
